32 devices in a mesh: dp: 8 (over z, y), seq: 4 (over x, core).
Axes of the slice: x: 2, y: 2, z: 4, core: 2. Of those that a mesh axis runs over, the one named last changes fastest.
Arguments:
- text_in: bfloat16 [8, 256, 768], P('dp', 'seq'), may hold values from -6 to 6
- image_in: bfloat16 [32, 196, 768], P('dp', 'seq'), may hold values from -6 to 6
- tile_slide: int32 [32], replicated, may hold values from 0 to 7, as said below
- owner_map: int32 [8], replicated, may hold values from 0 to 7, each once
- text_cot: bfloat16 [8, 256, 768], P('dp', 'seq'), may hold values from -6 to 6
- w_query: bfloat16 [768, 768], P(('dp', 'seq')), may hold values from -0.21875 to 0.21875
- w_key: bfloat16 [768, 768], P(('dp', 'seq')), may hold values from -0.21875 to 0.21875
- w_value: bfloat16 [768, 768], P(('dp', 'seq')), may hold values from -0.21875 to 0.21875
- w_out: bfloat16 [768, 768], P(('dp', 'seq')), may hold values from -0.875 to 0.875
- c_query: bfloat16 [768, 768], P(('dp', 'seq')), may hold values from -0.21875 to 0.21875
- c_key: bfloat16 [768, 768], P(('dp', 'seq')), may hold values from -0.21875 to 0.21875
- c_value: bfloat16 [768, 768], P(('dp', 'seq')), may hold values from -0.21875 to 0.21875
- c_out: bfloat16 [768, 768], P(('dp', 'seq')), may hold values from -3.5 to 3.5
- w_up: bfloat16 [768, 3072], P(('dp', 'seq')), may hold values from -0.21875 to 0.21875
- w_down: bfloat16 [3072, 768], P(('dp', 'seq')), may hold values from -0.109375 to 0.109375
- b_up: bfloat16 [3072], P(('dp', 'seq')), may hold values from -3 to 3
- b_down: bfloat16 [768], P(('dp', 'seq')), may hold values from -3 to 3
- self_gain: bfloat16 [768], P(('dp', 'seq')), may hold values from 0.5 to 1.5
- self_shift: bfloat16 [768], P(('dp', 'seq')), may hold values from -2 to 2
- cross_gain: bfloat16 [768], P(('dp', 'seq')), may hold values from 0.5 to 1.5
- cross_shift: bfloat16 [768], P(('dp', 'seq')), may hold values from -2 to 2
- tile_gain: bfloat16 [768], P(('dp', 'seq')), may hold values from 0.5 to 1.5
- tile_shift: bfloat16 [768], P(('dp', 'seq')), may hold values from -2 to 2
- mlp_gain: bfloat16 [768], P(('dp', 'seq')), may hold values from 0.5 to 1.5
- mlp_shift: bfloat16 [768], P(('dp', 'seq')), may hold values from -2 to 2
Outputs:
- text_out: bfloat16 [8, 256, 768], P('dp', 'seq')
- text_grad: bfloat16 [8, 256, 768], P('dp', 'seq')
- image_grad: bfloat16 [32, 196, 768], P('dp', 'seq')
- query_grad: float32 [768, 768], P(('dp', 'seq'))
- key_grad: float32 [768, 768], P(('dp', 'seq'))
- value_grad: float32 [768, 768], P(('dp', 'seq'))
- proj_grad: float32 [768, 768], P(('dp', 'seq'))
- xquery_grad: float32 [768, 768], P(('dp', 'seq'))
- xkey_grad: float32 [768, 768], P(('dp', 'seq'))
- xvalue_grad: float32 [768, 768], P(('dp', 'seq'))
- xproj_grad: float32 [768, 768], P(('dp', 'seq'))
- up_grad: float32 [768, 3072], P(('dp', 'seq'))
- down_grad: float32 [3072, 768], P(('dp', 'seq'))
- upbias_grad: float32 [3072], P(('dp', 'seq'))
- downbias_grad: float32 [768], P(('dp', 'seq'))
- sgain_grad: float32 [768], P(('dp', 'seq'))
- sshift_grad: float32 [768], P(('dp', 'seq'))
- xgain_grad: float32 [768], P(('dp', 'seq'))
- xshift_grad: float32 [768], P(('dp', 'seq'))
- tgain_grad: float32 [768], P(('dp', 'seq'))
- tshift_grad: float32 [768], P(('dp', 'seq'))
- mgain_grad: float32 [768], P(('dp', 'seq'))
- mshift_grad: float32 [768], P(('dp', 'seq'))
The draws below stay inside these ranges and needn't reach their ends.
Inputs may be any that keep to these rules, and one draw needn't show every extreme that they name: `tile_slide`: no index of dp holds two tiles of the same slide; every slide has one tile or more; some slide has a tile on every index of dp. A permutation: row c of text_in, text_cot and text_out is the caption of the slide s with owner_map[s] = c.
All inputs are finite; a program needn't handle non-finite values.
Results may differ from the reference program's by a relative error of at most 0.024.
Values may be sent and summed in bfloat16 or wider, within the bound.
A program may use at most 256 MiB of HBM per device.

```python
import math
import jax
import jax.numpy as jnp
from jax import lax

D = 768
HEADS = 12
HEAD = 64
FF = 3072
PATCH = 196
TILE_DEV = 4
SLIDES = 8
TILES = 32
LEN = 256
N_DP = 8


def draw_tile_slide(key, part):
    key = jax.random.fold_in(key, 11)
    subkeys = jax.random.split(key, 5)
    half_count = N_DP // 2
    middle = jax.random.randint(subkeys[0], (1,), 1, half_count, dtype=jnp.int32)
    paired = jax.random.randint(subkeys[1], ((N_DP - 4) // 2,), 1, N_DP, dtype=jnp.int32)
    head_counts = jnp.concatenate([jnp.full((1,), N_DP, jnp.int32), middle, half_count - middle, jnp.full((1,), half_count, jnp.int32)])
    tail_counts = jnp.stack([paired, N_DP - paired], axis=1).reshape(-1)
    counts = jnp.concatenate([head_counts, tail_counts]).astype(jnp.int32)
    slide_order = jax.random.permutation(subkeys[2], N_DP).astype(jnp.int32)
    bounds = jnp.cumsum(counts).astype(jnp.int32)
    places = jnp.arange(TILES, dtype=jnp.int32)
    segment = jnp.sum((places[:, None] >= bounds[None, :]).astype(jnp.int32), axis=1).astype(jnp.int32)
    listed = slide_order[segment]
    source_order = jax.random.permutation(subkeys[3], N_DP).astype(jnp.int32)
    source = source_order[places % N_DP]
    local_orders = jax.vmap(lambda subkey: jax.random.permutation(subkey, TILE_DEV))(jax.random.split(subkeys[4], N_DP)).astype(jnp.int32)
    local_slot = local_orders[source, places // N_DP]
    return jnp.zeros((TILES,), jnp.int32).at[source * TILE_DEV + local_slot].set(listed)


def block_scale(rng, dims, cuts, low, largest):
    level, own = 1.0, jax.random.fold_in(rng, 6)
    for position, shards_of in cuts:
        steps = jnp.exp(jax.random.uniform(jax.random.fold_in(own, position), (shards_of,), jnp.float32, low / len(cuts), largest / len(cuts)))
        level = level * jnp.repeat(steps, dims[position] // shards_of).reshape([-1 if axis == position else 1 for axis in range(len(dims))])
    return level


def normal_values(key, shape, width, bound, cuts=(), held_as=jnp.bfloat16):
    entries = jax.random.normal(key, shape, jnp.float32) * width
    if len(cuts) > 0:
        entries = block_scale(key, shape, cuts, -0.22, 0.18) * entries
    return jnp.clip(entries, min=-bound, max=bound).astype(held_as)


def setup_inputs(seed: int = 0) -> dict:
    keys = jax.random.split(jax.random.key(seed), 26)
    return {
        "text_in": normal_values(keys[0], (SLIDES, LEN, D), 1.0, 6.0, ((0, 8), (1, 4))),
        "image_in": normal_values(keys[1], (TILES, PATCH, D), 1.0, 6.0, ((0, 8), (1, 4))),
        "tile_slide": draw_tile_slide(jax.random.fold_in(keys[25], 71), 0),
        "owner_map": jax.random.permutation(keys[3], SLIDES).astype(jnp.int32),
        "text_cot": normal_values(keys[4], (SLIDES, LEN, D), 1.0, 6.0, ((0, 8), (1, 4))),
        "w_query": normal_values(keys[5], (D, D), D ** -0.5, 0.21875, ((0, 32),)),
        "w_key": normal_values(keys[6], (D, D), D ** -0.5, 0.21875, ((0, 32),)),
        "w_value": normal_values(keys[7], (D, D), D ** -0.5, 0.21875, ((0, 32),)),
        "w_out": normal_values(keys[8], (D, D), (D // 16) ** -0.5, 0.875, ((0, 32),)),
        "c_query": normal_values(keys[9], (D, D), D ** -0.5, 0.21875, ((0, 32),)),
        "c_key": normal_values(keys[10], (D, D), D ** -0.5, 0.21875, ((0, 32),)),
        "c_value": normal_values(keys[11], (D, D), D ** -0.5, 0.21875, ((0, 32),)),
        "c_out": normal_values(keys[12], (D, D), (D // 256) ** -0.5, 3.5, ((0, 32),)),
        "w_up": normal_values(keys[13], (D, FF), D ** -0.5, 0.21875, ((0, 32),)),
        "w_down": normal_values(keys[14], (FF, D), FF ** -0.5, 0.109375, ((0, 32),)),
        "b_up": normal_values(keys[15], (FF,), 0.5, 3.0, ((0, 32),)),
        "b_down": normal_values(keys[16], (D,), 0.5, 3.0, ((0, 32),)),
        "self_gain": jnp.clip(1.0 + 0.1 * jax.random.normal(keys[17], (D,), jnp.float32), 0.5, 1.5).astype(jnp.bfloat16),
        "self_shift": normal_values(keys[18], (D,), 0.3, 2.0, ((0, 32),)),
        "cross_gain": jnp.clip(1.0 + 0.1 * jax.random.normal(keys[19], (D,), jnp.float32), 0.5, 1.5).astype(jnp.bfloat16),
        "cross_shift": normal_values(keys[20], (D,), 0.3, 2.0, ((0, 32),)),
        "tile_gain": jnp.clip(1.0 + 0.1 * jax.random.normal(keys[21], (D,), jnp.float32), 0.5, 1.5).astype(jnp.bfloat16),
        "tile_shift": normal_values(keys[22], (D,), 0.3, 2.0, ((0, 32),)),
        "mlp_gain": jnp.clip(1.0 + 0.1 * jax.random.normal(keys[23], (D,), jnp.float32), 0.5, 1.5).astype(jnp.bfloat16),
        "mlp_shift": normal_values(keys[24], (D,), 0.3, 2.0, ((0, 32),)),
    }


@jax.custom_vjp
def low(v):
    return lax.optimization_barrier(v.astype(jnp.bfloat16)).astype(jnp.float32)

@jax.custom_vjp
def low_back(v):
    return v

def low_keep(v):
    return (low(v), None)

def low_pass(kept, grad):
    return (grad,)

def back_keep(v):
    return (v, None)

def back_low(kept, grad):
    return (low(grad),)
low.defvjp(low_keep, low_pass)
low_back.defvjp(back_keep, back_low)
EPSILON = 1e-05
MASKED_SCORE = -1e+30

def norm_rows(values, gain_row, shift_row):
    average = lax.optimization_barrier(jnp.mean(values, axis=-1, keepdims=True))
    centered = values - average
    spread = lax.optimization_barrier(jnp.mean(centered * centered, axis=-1, keepdims=True))
    return centered * lax.rsqrt(spread + EPSILON) * gain_row + shift_row

def matmul(former, latter):
    return jnp.dot(former, latter, precision=lax.Precision.HIGHEST, preferred_element_type=jnp.float32)

def rounded(values):
    return low(low_back(values))

def attend(query_rows, key_rows, value_rows, allowed):
    factor = 1.0 / math.sqrt(HEAD)
    query_heads = query_rows.reshape(query_rows.shape[0], HEADS, HEAD)
    key_heads = key_rows.reshape(key_rows.shape[0], HEADS, HEAD)
    value_heads = value_rows.reshape(value_rows.shape[0], HEADS, HEAD)
    scores = low_back(jnp.einsum('qhd,khd->hqk', query_heads, key_heads, precision=lax.Precision.HIGHEST) * factor)
    scores = jnp.where(allowed[None], scores, MASKED_SCORE)
    highest = lax.optimization_barrier(jnp.max(scores, axis=2, keepdims=True))
    exponent = jnp.exp(scores - highest)
    weights = exponent / lax.optimization_barrier(jnp.sum(exponent, axis=2, keepdims=True))
    mixture = jnp.einsum('hqk,khd->qhd', low(weights), value_heads, precision=lax.Precision.HIGHEST)
    return mixture.reshape(query_rows.shape[0], HEADS * HEAD)

def slide_layer(params, text_rows, tile_block, tile_valid):
    query_mat, key_mat, value_mat, proj_mat, xquery_mat, xkey_mat, xvalue_mat, xproj_mat, up_mat, down_mat, up_bias, down_bias, gain_one, shift_one, gain_two, shift_two, gain_tile, shift_tile, gain_three, shift_three = params
    first_in = low(norm_rows(text_rows, gain_one, shift_one))
    query_one = rounded(matmul(first_in, query_mat))
    key_one = rounded(matmul(first_in, key_mat))
    value_one = rounded(matmul(first_in, value_mat))
    length = text_rows.shape[0]
    causal = jnp.arange(length)[:, None] >= jnp.arange(length)[None, :]
    mixed_one = rounded(attend(query_one, key_one, value_one, causal))
    second = text_rows + low_back(matmul(mixed_one, proj_mat))
    second_in = low(norm_rows(second, gain_two, shift_two))
    query_two = rounded(matmul(second_in, xquery_mat))
    flat_tiles = tile_block.reshape(tile_block.shape[0] * tile_block.shape[1], tile_block.shape[2])
    flat_in = rounded(norm_rows(flat_tiles, gain_tile, shift_tile))
    key_two = rounded(matmul(flat_in, xkey_mat))
    value_two = rounded(matmul(flat_in, xvalue_mat))
    allowed = jnp.repeat(tile_valid, tile_block.shape[1])[None, :]
    mixed_two = rounded(attend(query_two, key_two, value_two, allowed))
    third_sum = second + low_back(matmul(mixed_two, xproj_mat))
    third_in = low(norm_rows(third_sum, gain_three, shift_three))
    pre_gelu = low_back(matmul(third_in, up_mat) + up_bias)
    act_in = rounded(jax.nn.gelu(pre_gelu, approximate=False))
    return third_sum + matmul(act_in, down_mat) + down_bias

def reference(text_in, image_in, tile_slide, owner_map, text_cot, w_query, w_key, w_value, w_out, c_query, c_key, c_value, c_out, w_up, w_down, b_up, b_down, self_gain, self_shift, cross_gain, cross_shift, tile_gain, tile_shift, mlp_gain, mlp_shift):
    slide_ids = jnp.arange(SLIDES, dtype=jnp.int32)
    destination = owner_map[tile_slide].astype(jnp.int32)
    order = jnp.argsort(destination, stable=True).astype(jnp.int32)
    counts = lax.optimization_barrier(jnp.sum((destination[None, :] == slide_ids[:, None]).astype(jnp.int32), axis=1)).astype(jnp.int32)
    starts = (jnp.cumsum(counts) - counts).astype(jnp.int32)
    columns = jnp.arange(N_DP, dtype=jnp.int32)
    table = order[(starts[:, None] + jnp.minimum(columns[None, :], counts[:, None] - 1)).astype(jnp.int32)]
    valid = columns[None, :] < counts[:, None]
    params = tuple((member.astype(jnp.float32) for member in (w_query, w_key, w_value, w_out, c_query, c_key, c_value, c_out, w_up, w_down, b_up, b_down, self_gain, self_shift, cross_gain, cross_shift, tile_gain, tile_shift, mlp_gain, mlp_shift)))

    def forward(text_rows, image_rows, weights_all):
        padded = image_rows[table]

        def one_slide(inputs):
            return slide_layer(weights_all, inputs[0], inputs[1], inputs[2])
        return lax.map(jax.checkpoint(one_slide), (text_rows, padded, valid))
    outputs, pullback = jax.vjp(forward, text_in.astype(jnp.float32), image_in.astype(jnp.float32), params)
    grad_text, grad_image, grads = pullback(text_cot.astype(jnp.float32))
    return (outputs.astype(jnp.bfloat16), grad_text.astype(jnp.bfloat16), grad_image.astype(jnp.bfloat16), grads[0], grads[1], grads[2], grads[3], grads[4], grads[5], grads[6], grads[7], grads[8], grads[9], grads[10], grads[11], grads[12], grads[13], grads[14], grads[15], grads[16], grads[17], grads[18], grads[19])
```

```python
from functools import partial
import math
from types import SimpleNamespace

import jax
import jax.numpy as jnp
from jax import lax
from jax.experimental import pallas as pl
from jax.experimental.pallas import tpu as pltpu
from jax.sharding import PartitionSpec as P

HEAD = 64
LANES = 128
MESH = pl.DeviceIdType.MESH


EPSILON = 1e-05
MASKED_SCORE = -1e30


def combined_all(x, axis, combine):
    everything = jax.tree.map(lambda part: lax.all_gather(part, axis), x)
    initial = jax.tree.map(lambda part: part[0], everything)

    def step(k, so_far):
        return combine(so_far, jax.tree.map(lambda part: part[k], everything))

    return lax.fori_loop(1, lax.axis_size(axis), step, initial)


def norm_rows(values, gain_row, shift_row):
    average = jnp.mean(values, axis=-1, keepdims=True)
    centered = values - average
    spread = jnp.mean(centered * centered, axis=-1, keepdims=True)
    return centered * lax.rsqrt(spread + EPSILON) * gain_row + shift_row


def matmul(former, latter):
    return jnp.dot(former, latter, preferred_element_type=jnp.float32)


def matmul_trans(former, latter):
    return lax.dot_general(
        former, latter, (((1,), (1,)), ((), ())), preferred_element_type=jnp.float32
    )


def outer_sum(former, latter):
    return lax.dot_general(
        former, latter, (((0,), (0,)), ((), ())), preferred_element_type=jnp.float32
    )


def head_pair(matrix, pair_index):
    columns = lax.dynamic_slice_in_dim(matrix, pair_index * 2 * HEAD, 2 * HEAD, 1)
    return columns.reshape(columns.shape[0], 2, HEAD)


def put_pair(matrix, update, pair_index):
    return lax.dynamic_update_slice_in_dim(
        matrix, update.reshape(update.shape[0], 2 * HEAD), pair_index * 2 * HEAD, 1
    )


def pick_pair(stacked, pair_index):
    return lax.dynamic_index_in_dim(stacked, pair_index, 0, keepdims=False)


def pair_scores(query_rows, key_rows, allowed, pair_index):
    factor = 1.0 / math.sqrt(HEAD)
    scores = (
        jnp.einsum(
            "qhd,khd->hqk",
            head_pair(query_rows, pair_index),
            head_pair(key_rows, pair_index),
            preferred_element_type=jnp.float32,
        )
        * factor
    )
    return jnp.where(allowed[None], scores, MASKED_SCORE)


def attend_stats(query_rows, key_rows, allowed):
    pair_count = query_rows.shape[1] // (2 * HEAD)

    def one_pair(pair_index, state_now):
        row_max, row_sum = state_now
        scores = pair_scores(query_rows, key_rows, allowed, pair_index)
        highest = jnp.max(scores, axis=2)
        summed = jnp.sum(jnp.exp(scores - highest[..., None]), axis=2)
        return (
            lax.dynamic_update_index_in_dim(row_max, highest, pair_index, 0),
            lax.dynamic_update_index_in_dim(row_sum, summed, pair_index, 0),
        )

    empty_stats = jnp.zeros((pair_count, 2, query_rows.shape[0]), jnp.float32)
    return lax.fori_loop(0, pair_count, one_pair, (empty_stats, empty_stats))


def attend_forward(query_rows, key_rows, value_rows, allowed, maxima, totals):
    pair_count = query_rows.shape[1] // (2 * HEAD)
    stats_given = maxima is not None
    if not stats_given:
        maxima = jnp.zeros((pair_count, 2, query_rows.shape[0]), jnp.float32)
        totals = jnp.zeros_like(maxima)

    def one_pair(pair_index, state_now):
        output, row_max, row_sum = state_now
        scores = pair_scores(query_rows, key_rows, allowed, pair_index)
        if stats_given:
            highest = pick_pair(row_max, pair_index)
            exponent = jnp.exp(scores - highest[..., None])
            summed = pick_pair(row_sum, pair_index)
        else:
            highest = jnp.max(scores, axis=2)
            exponent = jnp.exp(scores - highest[..., None])
            summed = jnp.sum(exponent, axis=2)
            row_max = lax.dynamic_update_index_in_dim(row_max, highest, pair_index, 0)
            row_sum = lax.dynamic_update_index_in_dim(row_sum, summed, pair_index, 0)
        weights = (exponent / summed[..., None]).astype(jnp.bfloat16)
        mixture = jnp.einsum(
            "hqk,khd->qhd",
            weights,
            head_pair(value_rows, pair_index),
            preferred_element_type=jnp.float32,
        )
        return (put_pair(output, mixture, pair_index), row_max, row_sum)

    start_state = (jnp.zeros(query_rows.shape, jnp.float32), maxima, totals)
    return lax.fori_loop(0, pair_count, one_pair, start_state)


def attend_rowsums(query_rows, key_rows, value_rows, allowed, maxima, totals, grad_rows):
    pair_count = query_rows.shape[1] // (2 * HEAD)

    def one_pair(pair_index, row_terms):
        scores = pair_scores(query_rows, key_rows, allowed, pair_index)
        chances = (
            jnp.exp(scores - pick_pair(maxima, pair_index)[..., None])
            / pick_pair(totals, pair_index)[..., None]
        )
        grad_chances = jnp.einsum(
            "qhd,khd->hqk",
            head_pair(grad_rows, pair_index),
            head_pair(value_rows, pair_index),
            preferred_element_type=jnp.float32,
        )
        return lax.dynamic_update_index_in_dim(
            row_terms, jnp.sum(chances * grad_chances, axis=2), pair_index, 0
        )

    return lax.fori_loop(0, pair_count, one_pair, jnp.zeros_like(maxima))


def attend_backward(
    query_rows, key_rows, value_rows, allowed, maxima, totals, grad_rows, row_terms
):
    pair_count = query_rows.shape[1] // (2 * HEAD)
    factor = 1.0 / math.sqrt(HEAD)

    def one_pair(pair_index, state_now):
        grad_query, grad_key, grad_value = state_now
        scores = pair_scores(query_rows, key_rows, allowed, pair_index)
        chances = (
            jnp.exp(scores - pick_pair(maxima, pair_index)[..., None])
            / pick_pair(totals, pair_index)[..., None]
        )
        grad_heads = head_pair(grad_rows, pair_index)
        grad_chances = jnp.einsum(
            "qhd,khd->hqk",
            grad_heads,
            head_pair(value_rows, pair_index),
            preferred_element_type=jnp.float32,
        )
        if row_terms is None:
            weighted = jnp.sum(chances * grad_chances, axis=2)
        else:
            weighted = pick_pair(row_terms, pair_index)
        grad_scores = (chances * (grad_chances - weighted[..., None])).astype(jnp.bfloat16)
        query_part = (
            jnp.einsum(
                "hqk,khd->qhd",
                grad_scores,
                head_pair(key_rows, pair_index),
                preferred_element_type=jnp.float32,
            )
            * factor
        )
        key_part = (
            jnp.einsum(
                "hqk,qhd->khd",
                grad_scores,
                head_pair(query_rows, pair_index),
                preferred_element_type=jnp.float32,
            )
            * factor
        )
        value_part = jnp.einsum(
            "hqk,qhd->khd",
            chances.astype(jnp.bfloat16),
            grad_heads,
            preferred_element_type=jnp.float32,
        )
        return (
            put_pair(grad_query, query_part, pair_index),
            put_pair(grad_key, key_part, pair_index),
            put_pair(grad_value, value_part, pair_index),
        )

    start_state = (
        jnp.zeros(query_rows.shape, jnp.float32),
        jnp.zeros(key_rows.shape, jnp.float32),
        jnp.zeros(value_rows.shape, jnp.float32),
    )
    return lax.fori_loop(0, pair_count, one_pair, start_state)


def join_stats(former, latter):
    highest = jnp.maximum(former[0], latter[0])
    return (
        highest,
        former[1] * jnp.exp(former[0] - highest) + latter[1] * jnp.exp(latter[0] - highest),
    )


def split_rows(matrix, data_count, seq_count):
    return matrix.reshape(
        data_count, seq_count, matrix.shape[0] // (data_count * seq_count), matrix.shape[1]
    )


def fold_rows(pieces):
    return jnp.sum(pieces, axis=1).reshape(pieces.shape[0] * pieces.shape[2], pieces.shape[3])


def per_device(
    text_in,
    image_in,
    tile_slide,
    owner_map,
    text_cot,
    w_query,
    w_key,
    w_value,
    w_out,
    c_query,
    c_key,
    c_value,
    c_out,
    w_up,
    w_down,
    b_up,
    b_down,
    self_gain,
    self_shift,
    cross_gain,
    cross_shift,
    tile_gain,
    tile_shift,
    mlp_gain,
    mlp_shift,
):
    gathered = (
        lax.all_gather(w_query, ("dp", "seq"), axis=0, tiled=True),
        lax.all_gather(w_key, ("dp", "seq"), axis=0, tiled=True),
        lax.all_gather(w_value, ("dp", "seq"), axis=0, tiled=True),
        lax.all_gather(w_out, ("dp", "seq"), axis=0, tiled=True),
        lax.all_gather(c_query, ("dp", "seq"), axis=0, tiled=True),
        lax.all_gather(c_key, ("dp", "seq"), axis=0, tiled=True),
        lax.all_gather(c_value, ("dp", "seq"), axis=0, tiled=True),
        lax.all_gather(c_out, ("dp", "seq"), axis=0, tiled=True),
        lax.all_gather(w_up, ("dp", "seq"), axis=0, tiled=True),
        lax.all_gather(w_down, ("dp", "seq"), axis=0, tiled=True),
        lax.all_gather(b_up, ("dp", "seq"), axis=0, tiled=True),
        lax.all_gather(b_down, ("dp", "seq"), axis=0, tiled=True),
        lax.all_gather(self_gain, ("dp", "seq"), axis=0, tiled=True),
        lax.all_gather(self_shift, ("dp", "seq"), axis=0, tiled=True),
        lax.all_gather(cross_gain, ("dp", "seq"), axis=0, tiled=True),
        lax.all_gather(cross_shift, ("dp", "seq"), axis=0, tiled=True),
        lax.all_gather(tile_gain, ("dp", "seq"), axis=0, tiled=True),
        lax.all_gather(tile_shift, ("dp", "seq"), axis=0, tiled=True),
        lax.all_gather(mlp_gain, ("dp", "seq"), axis=0, tiled=True),
        lax.all_gather(mlp_shift, ("dp", "seq"), axis=0, tiled=True),
    )
    query_mat, key_mat, value_mat, proj_mat = (gathered[0], gathered[1], gathered[2], gathered[3])
    xquery_mat, xkey_mat, xvalue_mat, xproj_mat = (
        gathered[4],
        gathered[5],
        gathered[6],
        gathered[7],
    )
    up_mat, down_mat = (gathered[8], gathered[9])
    vectors = [member.astype(jnp.float32) for member in gathered[10:]]
    (
        up_bias,
        down_bias,
        gain_one,
        shift_one,
        gain_two,
        shift_two,
        gain_tile,
        shift_tile,
        gain_three,
        shift_three,
    ) = vectors
    text_rows = text_in[0].astype(jnp.float32)
    rows_here = text_rows.shape[0]
    hidden_dim = text_rows.shape[1]
    normed_one, norm_one_back = jax.vjp(norm_rows, text_rows, gain_one, shift_one)
    first_in = normed_one.astype(jnp.bfloat16)
    query_one = matmul(first_in, query_mat).astype(jnp.bfloat16)
    key_one = matmul(first_in, key_mat).astype(jnp.bfloat16)
    value_one = matmul(first_in, value_mat).astype(jnp.bfloat16)
    key_all, value_all = (
        lax.all_gather(key_one, "seq", axis=0, tiled=True),
        lax.all_gather(value_one, "seq", axis=0, tiled=True),
    )
    positions = lax.axis_index("seq") * rows_here + jnp.arange(rows_here)
    causal = positions[:, None] >= jnp.arange(key_all.shape[0])[None, :]
    attend_one, max_one, sum_one = attend_forward(query_one, key_all, value_all, causal, None, None)
    mixed_one = attend_one.astype(jnp.bfloat16)
    second = text_rows + matmul(mixed_one, proj_mat)
    normed_two, norm_two_back = jax.vjp(norm_rows, second, gain_two, shift_two)
    second_in = normed_two.astype(jnp.bfloat16)
    query_two = matmul(second_in, xquery_mat).astype(jnp.bfloat16)
    tile_rows = image_in.astype(jnp.float32)
    normed_tiles, norm_tile_back = jax.vjp(norm_rows, tile_rows, gain_tile, shift_tile)
    tiles_in = normed_tiles.astype(jnp.bfloat16)
    data_index = lax.axis_index("dp")
    data_count = lax.axis_size("dp")
    seq_count = lax.axis_size("seq")
    tile_count = image_in.shape[0]
    slot_rows = image_in.shape[1]
    slide_ids = jnp.arange(owner_map.shape[0])
    destination = jnp.sum(
        jnp.where(tile_slide[:, None] == slide_ids[None, :], owner_map[None, :], 0), axis=1
    )
    own_destination = lax.dynamic_slice_in_dim(destination, data_index * tile_count, tile_count)
    routing = (own_destination[None, :] == jnp.arange(data_count)[:, None]).astype(jnp.bfloat16)
    outgoing = jnp.einsum(
        "pt,trd->prd", routing, tiles_in, preferred_element_type=jnp.float32
    ).astype(jnp.bfloat16)
    incoming = lax.all_to_all(outgoing, "dp", split_axis=0, concat_axis=0, tiled=True)
    arrived = jnp.any(destination.reshape(data_count, tile_count) == data_index, axis=1)
    flat_in = incoming.reshape(data_count * slot_rows, hidden_dim)
    allowed_rows = jnp.broadcast_to(arrived[:, None], (data_count, slot_rows)).reshape(-1)
    key_two = matmul(flat_in, xkey_mat).astype(jnp.bfloat16)
    value_two = matmul(flat_in, xvalue_mat).astype(jnp.bfloat16)
    query_far = lax.all_gather(query_two, "seq", axis=0, tiled=True)
    allowed_near = allowed_rows[None, :]
    local_max, local_sum = attend_stats(query_far, key_two, allowed_near)
    max_two, sum_two = combined_all((local_max, local_sum), "seq", join_stats)
    partial_rows = attend_forward(query_far, key_two, value_two, allowed_near, max_two, sum_two)[0]
    attend_two = lax.psum_scatter(
        partial_rows.astype(jnp.bfloat16), "seq", scatter_dimension=0, tiled=True
    )
    third_sum = second + matmul(attend_two, xproj_mat)
    normed_three, norm_three_back = jax.vjp(norm_rows, third_sum, gain_three, shift_three)
    third_in = normed_three.astype(jnp.bfloat16)
    pre_gelu = matmul(third_in, up_mat) + up_bias
    activated, gelu_back = jax.vjp(partial(jax.nn.gelu, approximate=False), pre_gelu)
    act_in = activated.astype(jnp.bfloat16)
    result = third_sum + matmul(act_in, down_mat) + down_bias
    text_out = result.astype(jnp.bfloat16)[None]
    cot_rows = text_cot[0]
    grad_res = cot_rows.astype(jnp.float32)
    down_grad = outer_sum(act_in, cot_rows)
    downbias_grad = jnp.sum(grad_res, axis=0)
    grad_act = matmul_trans(cot_rows, down_mat).astype(jnp.bfloat16)
    grad_pre = gelu_back(grad_act.astype(jnp.float32))[0].astype(jnp.bfloat16)
    up_grad = outer_sum(third_in, grad_pre)
    upbias_grad = jnp.sum(grad_pre.astype(jnp.float32), axis=0)
    grad_mid, mgain_grad, mshift_grad = norm_three_back(matmul_trans(grad_pre, up_mat))
    grad_third = grad_res + grad_mid
    branch_two = grad_third.astype(jnp.bfloat16)
    xproj_grad = outer_sum(attend_two, branch_two)
    grad_attend_two = matmul_trans(branch_two, xproj_mat).astype(jnp.bfloat16)
    grad_far = lax.all_gather(grad_attend_two, "seq", axis=0, tiled=True)
    row_part = attend_rowsums(
        query_far, key_two, value_two, allowed_near, max_two, sum_two, grad_far
    )
    row_terms = lax.psum(row_part, "seq")
    query_grad_far, key_grad_two, value_grad_two = attend_backward(
        query_far, key_two, value_two, allowed_near, max_two, sum_two, grad_far, row_terms
    )
    query_grad_two = lax.psum_scatter(
        query_grad_far.astype(jnp.bfloat16), "seq", scatter_dimension=0, tiled=True
    )
    gkey_two = key_grad_two.astype(jnp.bfloat16)
    gvalue_two = value_grad_two.astype(jnp.bfloat16)
    xquery_grad = outer_sum(second_in, query_grad_two)
    xkey_grad = outer_sum(flat_in, gkey_two)
    xvalue_grad = outer_sum(flat_in, gvalue_two)
    grad_flat = (matmul_trans(gkey_two, xkey_mat) + matmul_trans(gvalue_two, xvalue_mat)).astype(
        jnp.bfloat16
    )
    grad_home = lax.all_to_all(
        grad_flat.reshape(data_count, slot_rows, hidden_dim),
        "dp",
        split_axis=0,
        concat_axis=0,
        tiled=True,
    )
    grad_tiles = jnp.einsum("pt,prd->trd", routing, grad_home, preferred_element_type=jnp.float32)
    image_back, tgain_grad, tshift_grad = norm_tile_back(grad_tiles)
    image_grad = image_back.astype(jnp.bfloat16)
    grad_mid_two, xgain_grad, xshift_grad = norm_two_back(matmul_trans(query_grad_two, xquery_mat))
    grad_second = grad_third + grad_mid_two
    branch_one = grad_second.astype(jnp.bfloat16)
    proj_grad = outer_sum(mixed_one, branch_one)
    grad_attend_one = matmul_trans(branch_one, proj_mat).astype(jnp.bfloat16)
    query_grad_one, key_grad_all, value_grad_all = attend_backward(
        query_one, key_all, value_all, causal, max_one, sum_one, grad_attend_one, None
    )
    key_grad_one, value_grad_one = (
        lax.psum_scatter(
            key_grad_all.astype(jnp.bfloat16), "seq", scatter_dimension=0, tiled=True
        ).astype(jnp.float32),
        lax.psum_scatter(
            value_grad_all.astype(jnp.bfloat16), "seq", scatter_dimension=0, tiled=True
        ).astype(jnp.float32),
    )
    gquery_one = query_grad_one.astype(jnp.bfloat16)
    gkey_one = key_grad_one.astype(jnp.bfloat16)
    gvalue_one = value_grad_one.astype(jnp.bfloat16)
    query_grad = outer_sum(first_in, gquery_one)
    key_grad = outer_sum(first_in, gkey_one)
    value_grad = outer_sum(first_in, gvalue_one)
    grad_norm_one = (
        matmul_trans(gquery_one, query_mat)
        + matmul_trans(gkey_one, key_mat)
        + matmul_trans(gvalue_one, value_mat)
    )
    grad_mid_one, sgain_grad, sshift_grad = norm_one_back(grad_norm_one)
    text_grad = (grad_second + grad_mid_one).astype(jnp.bfloat16)[None]
    pieces = (
        lax.all_to_all(
            split_rows(query_grad, data_count, seq_count).astype(jnp.bfloat16),
            "seq",
            split_axis=1,
            concat_axis=1,
            tiled=True,
        ).astype(jnp.float32),
        lax.all_to_all(
            split_rows(key_grad, data_count, seq_count).astype(jnp.bfloat16),
            "seq",
            split_axis=1,
            concat_axis=1,
            tiled=True,
        ).astype(jnp.float32),
        lax.all_to_all(
            split_rows(value_grad, data_count, seq_count).astype(jnp.bfloat16),
            "seq",
            split_axis=1,
            concat_axis=1,
            tiled=True,
        ).astype(jnp.float32),
        lax.all_to_all(
            split_rows(proj_grad, data_count, seq_count).astype(jnp.bfloat16),
            "seq",
            split_axis=1,
            concat_axis=1,
            tiled=True,
        ).astype(jnp.float32),
        lax.all_to_all(
            split_rows(xquery_grad, data_count, seq_count).astype(jnp.bfloat16),
            "seq",
            split_axis=1,
            concat_axis=1,
            tiled=True,
        ).astype(jnp.float32),
        lax.all_to_all(
            split_rows(xkey_grad, data_count, seq_count).astype(jnp.bfloat16),
            "seq",
            split_axis=1,
            concat_axis=1,
            tiled=True,
        ).astype(jnp.float32),
        lax.all_to_all(
            split_rows(xvalue_grad, data_count, seq_count).astype(jnp.bfloat16),
            "seq",
            split_axis=1,
            concat_axis=1,
            tiled=True,
        ).astype(jnp.float32),
        lax.all_to_all(
            split_rows(xproj_grad, data_count, seq_count).astype(jnp.bfloat16),
            "seq",
            split_axis=1,
            concat_axis=1,
            tiled=True,
        ).astype(jnp.float32),
        lax.all_to_all(
            split_rows(up_grad, data_count, seq_count).astype(jnp.bfloat16),
            "seq",
            split_axis=1,
            concat_axis=1,
            tiled=True,
        ).astype(jnp.float32),
        lax.all_to_all(
            split_rows(down_grad, data_count, seq_count).astype(jnp.bfloat16),
            "seq",
            split_axis=1,
            concat_axis=1,
            tiled=True,
        ).astype(jnp.float32),
    )
    folded = [fold_rows(member) for member in pieces]
    summed_mats = (
        lax.psum_scatter(folded[0], "dp", scatter_dimension=0, tiled=True),
        lax.psum_scatter(folded[1], "dp", scatter_dimension=0, tiled=True),
        lax.psum_scatter(folded[2], "dp", scatter_dimension=0, tiled=True),
        lax.psum_scatter(folded[3], "dp", scatter_dimension=0, tiled=True),
        lax.psum_scatter(folded[4], "dp", scatter_dimension=0, tiled=True),
        lax.psum_scatter(folded[5], "dp", scatter_dimension=0, tiled=True),
        lax.psum_scatter(folded[6], "dp", scatter_dimension=0, tiled=True),
        lax.psum_scatter(folded[7], "dp", scatter_dimension=0, tiled=True),
        lax.psum_scatter(folded[8], "dp", scatter_dimension=0, tiled=True),
        lax.psum_scatter(folded[9], "dp", scatter_dimension=0, tiled=True),
    )
    summed_vecs = (
        lax.psum_scatter(upbias_grad, ("dp", "seq"), scatter_dimension=0, tiled=True),
        lax.psum_scatter(downbias_grad, ("dp", "seq"), scatter_dimension=0, tiled=True),
        lax.psum_scatter(sgain_grad, ("dp", "seq"), scatter_dimension=0, tiled=True),
        lax.psum_scatter(sshift_grad, ("dp", "seq"), scatter_dimension=0, tiled=True),
        lax.psum_scatter(xgain_grad, ("dp", "seq"), scatter_dimension=0, tiled=True),
        lax.psum_scatter(xshift_grad, ("dp", "seq"), scatter_dimension=0, tiled=True),
        lax.psum_scatter(tgain_grad, ("dp", "seq"), scatter_dimension=0, tiled=True),
        lax.psum_scatter(tshift_grad, ("dp", "seq"), scatter_dimension=0, tiled=True),
        lax.psum_scatter(mgain_grad, ("dp", "seq"), scatter_dimension=0, tiled=True),
        lax.psum_scatter(mshift_grad, ("dp", "seq"), scatter_dimension=0, tiled=True),
    )
    return (text_out, text_grad, image_grad) + tuple(summed_mats) + tuple(summed_vecs)


def dot_plain(former, latter):
    return jnp.dot(former, latter, preferred_element_type=jnp.float32)


def dot_right(former, latter):
    return lax.dot_general(
        former, latter, (((1,), (1,)), ((), ())), preferred_element_type=jnp.float32
    )


def dot_left(former, latter):
    return lax.dot_general(
        former, latter, (((0,), (0,)), ((), ())), preferred_element_type=jnp.float32
    )


def low(values):
    return values.astype(jnp.bfloat16)


def wide(values):
    return values.astype(jnp.float32)


def block(index, size):
    if isinstance(index, int):
        return pl.ds(index * size, size)
    return pl.ds(pl.multiple_of(index * size, size), size)


def lanes(start, size):
    return pl.ds(start, size)


def norm_parts(values):
    average = jnp.mean(values, axis=-1, keepdims=True)
    centered = values - average
    spread = jnp.mean(centered * centered, axis=-1, keepdims=True)
    inverse = lax.rsqrt(spread + EPSILON)
    return centered * inverse, inverse


def norm_back(unit, inverse, gain_row, grad):
    scaled = grad * gain_row
    first = jnp.mean(scaled, axis=-1, keepdims=True)
    second = jnp.mean(scaled * unit, axis=-1, keepdims=True)
    return (scaled - first - unit * second) * inverse


def column_sum(values):
    return jnp.sum(values, axis=0, keepdims=True)


class Copies:
    def __init__(self, send_sems, recv_sems):
        self.send_sems, self.recv_sems = send_sems, recv_sems
        self.count = 0
        self.started = []

    def make(self, source, target, device):
        index = self.count
        self.count += 1
        return pltpu.make_async_remote_copy(
            src_ref=source,
            dst_ref=target,
            send_sem=self.send_sems.at[index],
            recv_sem=self.recv_sems.at[index],
            device_id=device,
            device_id_type=MESH,
        )

    def begin(self, source, target, device):
        copy = self.make(source, target, device)
        copy.start()
        self.started.append(copy)
        return copy


COPY_SLOTS = 256


def scratch_of(width, tokens, seq_count, data_count, hidden, main, shard):
    length = tokens * seq_count
    band = shard * seq_count
    inbox = data_count * main
    rests = seq_count * data_count
    keys = inbox * seq_count + rests
    bf16, f32 = jnp.bfloat16, jnp.float32
    return dict(
        vec_own=((16, LANES), f32),
        vec_all=((data_count, seq_count, 16, LANES), bf16),
        vec=((16, width), f32),
        up_bias=((1, hidden), f32),
        key_bias=((1, keys), f32),
        slab_out=((seq_count, shard, 1152 + hidden), bf16),
        slab_in=((seq_count, shard, 1152 + hidden), bf16),
        cols=((width, 1152 + hidden), bf16),
        halves=((width, 768), bf16),
        cot_all=((length, width), bf16),
        h1=((length, width), bf16),
        h2=((length, width), bf16),
        h3=((length, width), bf16),
        e1=((length, width), bf16),
        e2=((length, width), bf16),
        out_all=((data_count, shard, 2 * width), bf16),
        out_in=((seq_count, data_count // seq_count, shard, 2 * width), bf16),
        out_rows=((256, 2 * width), bf16),
        down_all=((hidden, width), bf16),
        outbox=((inbox, width), bf16),
        rest_rows=((data_count, width), f32),
        rest_wide=((rests * 16, LANES), f32),
        rest_out=((data_count, 16, LANES), bf16),
        rest_in=((seq_count, data_count, 16, LANES), bf16),
        tiles=((keys, width), bf16),
        kv2=((keys, 512), bf16),
        dkv2=((keys, 512), bf16),
        qm1=((3 * length, LANES), bf16),
        qm2=((3 * length, LANES), bf16),
        dom=((3 * length, LANES), bf16),
        qkv1=((length, 768), bf16),
        p1=((3 * length, length), f32),
        o1=((length, 256), bf16),
        o2=((length, 256), bf16),
        o_acc=((length, 256), f32),
        ds=((3 * length, keys), bf16),
        pr=((3 * length, keys), bf16),
        sums_out=((6, 3, tokens, width), bf16),
        sums_in=((6, 3, tokens, width), bf16),
        x2=((tokens, width), f32),
        x3=((tokens, width), f32),
        dx=((tokens, width), f32),
        act=((length, hidden), bf16),
        slope=((length, hidden), f32),
        du=((length, hidden), bf16),
        dqkv=((length, 768), bf16),
        dq2=((length, 256), bf16),
        dn=((keys, width), bf16),
        dn_pair=((2, inbox, width), bf16),
        dn_far=((inbox, width), bf16),
        dn_home=((inbox, width), bf16),
        dr_out=((seq_count, data_count, 16, LANES), bf16),
        dr_pair=((2, data_count, 16, LANES), bf16),
        dr_far=((data_count, 16, LANES), bf16),
        dr_home=((data_count, 16, LANES), bf16),
        g_cols=((width, 1152 + hidden), bf16),
        g_half=((width, 384), bf16),
        g_half2=((width, 384), bf16),
        half_in=((width, 384), bf16),
        g_down=((hidden, width), bf16),
        g_out=((data_count, shard, 2 * width), bf16),
        g_out_send=((2, seq_count, data_count // seq_count, shard, width), bf16),
        y_up=((4, band, hidden), bf16),
        z_up=((3, band, hidden), bf16),
        y_down=((4, band, width), bf16),
        z_down=((3, band, width), bf16),
        y_cross=((4, band, 384), bf16),
        z_cross=((3, band, 384), bf16),
        y_self=((4, band, 768), bf16),
        z_self=((3, band, 768), bf16),
        y_xout=((4, shard, width), bf16),
        z_xout=((3, shard, width), bf16),
        y_sout=((4, shard, width), bf16),
        z_sout=((3, shard, width), bf16),
        cols_out=((seq_count, shard, 1152 + hidden), bf16),
        cols_in=((seq_count, shard, 1152 + hidden), bf16),
        vv=((16, width), f32),
        vv_out=((data_count, 16, LANES), f32),
        vv_in=((data_count, 16, LANES), f32),
        vq=((seq_count, 16, LANES), f32),
    )


def lane_pick(parts, lane):
    result = None
    for source, first, place, size in parts:
        start = first // LANES * LANES
        stop = start + LANES * (1 if first + size <= start + LANES else 2)
        window = source[:, start:stop]
        turn = (place - first + start) % (stop - start)
        if turn:
            window = pltpu.roll(window, turn, 1)
        window = window[:, 0:LANES]
        if result is None:
            result = window
        else:
            result = jnp.where((lane >= place) & (lane < place + size), window, result)
    return result


def spans(start, stop, size):
    while start < stop:
        end = min(stop, (start // size + 1) * size)
        yield start, end - start
        start = end


def fused_kernel(names, n_in, *refs):
    (
        slide, owner, text, img, cot, w_query, w_key, w_value, w_out, c_query, c_key, c_value,
        c_out, w_up, w_down, b_up, b_down, *gains,
    ) = refs[:n_in]
    r_text, r_tgrad, r_igrad, r_cols, r_outs, r_down, r_vec = refs[n_in : n_in + 7]
    m = SimpleNamespace(**dict(zip(names, refs[n_in + 7 :])))
    links = Copies(m.send, m.recv)
    begin = links.begin

    _, tokens, width = text.shape
    seq_count = m.slab_out.shape[0]
    length = tokens * seq_count
    shard = w_out.shape[0]
    data_count = m.vec_all.shape[0]
    hidden = m.down_all.shape[0]
    band = shard * seq_count
    tile_count, real_rows, _ = img.shape
    slides = owner.shape[0]
    main = real_rows // 16 * 16
    inbox = data_count * main
    keys_main = inbox * seq_count
    rests = seq_count * data_count
    keys = keys_main + rests
    columns = width // LANES
    factor = 1.0 / math.sqrt(HEAD)
    z_count = data_count // 2

    d = lax.axis_index("dp")
    s = lax.axis_index("seq")
    z, y = d // 2, d % 2
    core = s % 2
    sibling = s + 1 - 2 * core
    across = (s + 2) % 4
    corner = 3 - s
    seq_peers = [sibling, across, corner]
    z_peers = [(z + k) % z_count for k in range(1, z_count)]
    z_from = [(z + z_count - k) % z_count for k in range(1, z_count)]
    near = (z * 2 + 1 - y, s)

    barrier = pltpu.get_barrier_semaphore()
    for peer in seq_peers:
        pl.semaphore_signal(barrier, inc=1, device_id=(d, peer), device_id_type=MESH)
    for k in range(1, data_count):
        pl.semaphore_signal(
            barrier, inc=1, device_id=((d + k) % data_count, s), device_id_type=MESH
        )

    lane = lax.broadcasted_iota(jnp.int32, (1, LANES), 1)
    head_masks = [
        jnp.where(lane < HEAD, 1.0, 0.0),
        jnp.where(lane >= HEAD, 1.0, 0.0),
        jnp.where(lane // HEAD == core, 1.0, 0.0),
    ]

    def arrive(copies):
        for copy in copies:
            copy.wait_recv()

    def seq_gather(views):
        own = [view(s) for view in views]
        pair = [begin(part, part, (d, sibling)) for part in own]
        far = [begin(part, part, (d, across)) for part in own]
        return views, pair, far

    def seq_pass(state):
        arrive(state[2])
        for part in [view(across) for view in state[0]]:
            state[1].append(begin(part, part, (d, sibling)))

    def seq_end(state):
        arrive(state[1])

    def rows_of(ref):
        return [lambda index: ref.at[block(index, tokens)]]

    def gather_far(view):
        own = view(d)
        return view, [begin(own, own, (peer * 2 + y, s)) for peer in z_peers], []

    def gather_near(state):
        own = state[0](d)
        state[2].append(begin(own, own, near))

    def gather_step(state, k):
        view, far, close = state
        far[k].wait_recv()
        part = view(z_from[k] * 2 + y)
        close.append(begin(part, part, near))

    def gather_forward(state):
        for k in range(z_count - 1):
            gather_step(state, k)

    def gather_end(state):
        arrive(state[2])

    def seq_sum_begin(slot, produce):
        both = low(produce(sibling, corner))
        m.sums_out[slot, 0] = both[0:tokens]
        m.sums_out[slot, 1] = both[tokens : 2 * tokens]
        pair = pl.ds(0, 2)
        copy = begin(m.sums_out.at[slot, pair], m.sums_in.at[slot, pair], (d, sibling))
        both = produce(across, s)
        return slot, copy, both[0:tokens], both[tokens : 2 * tokens]

    def seq_sum_pass(state):
        slot, copy, far, own = state
        copy.wait_recv()
        m.sums_out[slot, 2] = low(far + wide(m.sums_in[slot, 1]))
        return slot, begin(m.sums_out.at[slot, 2], m.sums_in.at[slot, 2], (d, across)), own

    def seq_sum_end(state):
        slot, copy, own = state
        own = own + wide(m.sums_in[slot, 0])
        copy.wait_recv()
        return own + wide(m.sums_in[slot, 2])

    def pick(ref, first, second, place=slice(None)):
        return jnp.concatenate(
            [ref[block(first, tokens), place], ref[block(second, tokens), place]], axis=0
        )

    def sum_begin(view, y_in, z_in):
        close = []
        for k in [*range(1, z_count), 0]:
            target = (z + k) % z_count
            close.append(begin(view(target * 2 + 1 - y), y_in.at[k], near))
        return SimpleNamespace(view=view, y_in=y_in, z_in=z_in, close=close, far=[], own=None)

    def sum_step(state, index):
        k = (index + 1) % z_count
        state.close[index].wait_recv()
        target = (z + k) % z_count
        part = state.view(target * 2 + y)
        total = wide(part[...]) + wide(state.y_in[k])
        if k == 0:
            state.own = total
        else:
            part[...] = low(total)
            state.far.append(begin(part, state.z_in.at[k - 1], (target * 2 + y, s)))

    def sum_middle(state):
        for index in range(z_count):
            sum_step(state, index)

    def sum_end(state):
        total = state.own
        for k, copy in enumerate(state.far):
            copy.wait_recv()
            total = total + wide(state.z_in[k])
        return total

    cross, own = (c_query, c_key, c_value), (w_query, w_key, w_value)
    up_wide = wide(w_up[...])
    slab_out, slab_in = m.slab_out, m.slab_in
    for j in range(seq_count):
        full, half = 3 * (j // 2) + 2 * (j % 2), 3 * (j // 2) + 1
        sources = [(matrix, full) for matrix in cross + own]
        sources += [(matrix, half) for matrix in (cross if j % 2 == 0 else own)]
        for k, (matrix, index) in enumerate(sources):
            place = slice(LANES * k, LANES * k + LANES)
            slab_out[j, :, place] = matrix[:, LANES * index : LANES * index + LANES]
        for tile in range(hidden // LANES):
            pieces = [
                (up_wide, band * (seq_count * (at // band) + j) + at % band, at % LANES, size)
                for at, size in spans(LANES * tile, LANES * tile + LANES, band)
            ]
            slab_out[j, :, 1152 + LANES * tile : 1152 + LANES * (tile + 1)] = low(
                lane_pick(pieces, lane)
            )
    vec_own = m.vec_own
    vec_own[...] = jnp.zeros(vec_own.shape, jnp.float32)
    for k, ref in enumerate((b_down, *gains)):
        vec_own[k : k + 1, 0:shard] = wide(ref[...])
    vec_own[9:10, 0:band] = wide(b_up[...])
    vec_all = m.vec_all
    vec_all[d, s] = low(vec_own[...])
    slab_in[s] = slab_out[s]
    out_all, down_all, cot_all = m.out_all, m.down_all, m.cot_all
    out_all[d, :, 0:width] = w_out[...]
    out_all[d, :, width : 2 * width] = c_out[...]
    down_all[block(d, band)] = w_down[...]
    cot_all[block(s, tokens)] = cot[0]
    m.rest_wide[...] = jnp.zeros(m.rest_wide.shape, jnp.float32)

    def destination(index):
        total = jnp.int32(0)
        for k in range(slides):
            total = total + jnp.where(slide[index] == k, owner[k], 0)
        return total

    own_places = [destination(d * tile_count + t) for t in range(tile_count)]
    route = [
        [jnp.where(place == p, 1.0, 0.0) for place in own_places] for p in range(data_count)
    ]
    spot = lax.broadcasted_iota(jnp.int32, (1, keys), 1)
    slot_of = jnp.where(spot < keys_main, spot % inbox // main, (spot - keys_main) % data_count)
    bias = jnp.zeros((1, keys), jnp.float32)
    for p in range(data_count):
        hits = jnp.int32(0)
        for t in range(tile_count):
            hits = hits + jnp.where(destination(p * tile_count + t) == d, 1, 0)
        bias = jnp.where(slot_of == p, jnp.where(hits > 0, 0.0, MASKED_SCORE), bias)
    m.key_bias[...] = bias
    text_unit, _ = norm_parts(wide(text[0]))

    pl.semaphore_wait(barrier, seq_count - 1 + data_count - 1)

    own_vec = vec_all.at[d, s]
    vec_seq = [begin(own_vec, own_vec, (d, peer)) for peer in seq_peers]
    slab_seq = [begin(slab_out.at[peer], slab_in.at[s], (d, peer)) for peer in seq_peers]
    tile_units = [norm_parts(wide(img[t]))[0] for t in range(tile_count)]
    arrive(vec_seq)
    vec_dp = [
        begin(vec_all.at[d], vec_all.at[d], ((d + k) % data_count, s))
        for k in range(1, data_count)
    ]
    arrive(slab_seq)
    cols = m.cols
    cols[block(d, band)] = low(
        jnp.concatenate([wide(slab_in[j]) for j in range(seq_count)], axis=0)
    )
    self_view = lambda index: cols.at[block(index, band), lanes(384, 768)]
    cross_view = lambda index: cols.at[block(index, band), lanes(0, 384)]
    up_view = lambda index: cols.at[block(index, band), lanes(1152, hidden)]
    down_view = lambda index: down_all.at[block(index, band)]
    out_view = lambda index: out_all.at[index]
    self_ag = gather_far(self_view)
    gather_near(self_ag)
    out_ag = gather_far(out_view)
    gather_near(out_ag)

    arrive(vec_dp)
    stacked = vec_all[...].reshape(data_count * seq_count * 16, LANES)
    row_of = lax.broadcasted_iota(jnp.int32, (LANES, width), 0)
    col_of = lax.broadcasted_iota(jnp.int32, (LANES, width), 1)
    spread = dot_plain(stacked, jnp.where(row_of == col_of % shard, 1.0, 0.0).astype(jnp.bfloat16))
    spread = spread.reshape(data_count * seq_count, 16, width)
    which = lax.broadcasted_iota(jnp.int32, spread.shape, 0)
    column = lax.broadcasted_iota(jnp.int32, spread.shape, 2)
    vec = m.vec
    vec[...] = jnp.sum(jnp.where(which == column // shard, spread, 0.0), axis=0)

    def vector(index):
        return vec[index : index + 1, :]

    h1, h2, h3, e1, e2 = m.h1, m.h2, m.h3, m.e1, m.e2
    h1[block(s, tokens)] = low(text_unit * vector(1) + vector(2))
    h1_ag = seq_gather(rows_of(h1))
    cot_ag = seq_gather(rows_of(cot_all))

    outbox, tiles = m.outbox, m.tiles
    rest_rows, rest_wide, rest_out, rest_in = m.rest_rows, m.rest_wide, m.rest_out, m.rest_in
    normed = [wide(low(unit * vector(5) + vector(6))) for unit in tile_units]
    for p in range(data_count):
        total = normed[0] * route[p][0]
        for t in range(1, tile_count):
            total = total + normed[t] * route[p][t]
        outbox[block(p, main)] = low(total[0:main])
        rest_rows[p : p + 1] = total[main:real_rows]
    for k in range(columns):
        rest_wide[pl.ds(k, data_count, stride=16), :] = rest_rows[:, LANES * k : LANES * (k + 1)]
    rest_out[...] = low(rest_wide[0 : 16 * data_count]).reshape(rest_out.shape)
    own_slot = block(s * data_count + d, main)
    tiles[own_slot] = outbox[block(d, main)]
    rest_in[s, d] = rest_out[d]

    tile_dp = []

    def tile_out(k):
        peer = (d + k) % data_count
        tile_dp.append(begin(outbox.at[block(peer, main)], tiles.at[own_slot], (peer, s)))
        tile_dp.append(begin(rest_out.at[peer], rest_in.at[s, d], (peer, s)))

    for k in range(2, data_count, 2):
        tile_out(k)
    seq_pass(h1_ag)
    gather_forward(self_ag)
    seq_pass(cot_ag)
    gather_forward(out_ag)
    for k in range(1, data_count, 2):
        tile_out(k)
    cross_ag = gather_far(cross_view)
    up_ag = gather_far(up_view)
    down_ag = gather_far(down_view)
    gather_near(cross_ag)
    gather_near(up_ag)
    gather_near(down_ag)
    gather_end(self_ag)
    halves = m.halves
    half_place = pl.ds(pl.multiple_of(core * 384, 384), 384)
    half_copy = begin(cols.at[:, lanes(768, 384)], halves.at[:, half_place], (d, sibling))
    halves[:, half_place] = cols[:, 768:1152]
    seq_end(h1_ag)
    qkv1, qm1, p1, o1 = m.qkv1, m.qm1, m.p1, m.o1
    qkv1[:, 0:384] = low(dot_plain(h1[...], cols[:, 384:768]))
    arrive([half_copy])
    qkv1[:, 384:768] = low(dot_plain(h1[...], halves[:, 384:768]))

    spot_q = lax.broadcasted_iota(jnp.int32, (length, length), 0)
    spot_k = lax.broadcasted_iota(jnp.int32, (length, length), 1)
    causal = spot_q >= spot_k
    mixed = []
    for head in range(3):
        base = 384 * (head // 2)
        qm = low(wide(qkv1[:, base : base + 128]) * head_masks[head])
        qm1[block(head, length)] = qm
        scores = dot_right(qm, qkv1[:, base + 128 : base + 256]) * factor
        scores = jnp.where(causal, scores, MASKED_SCORE)
        exponent = jnp.exp(scores - jnp.max(scores, axis=1, keepdims=True))
        chances = exponent / jnp.sum(exponent, axis=1, keepdims=True)
        p1[block(head, length)] = chances
        mixed.append(
            dot_plain(low(chances), qkv1[:, base + 256 : base + 384]) * head_masks[head]
        )
    o1[:, 0:128] = low(mixed[0] + mixed[1])
    o1[:, 128:256] = low(mixed[2])

    gather_end(out_ag)
    per_seq = data_count // seq_count
    out_in = m.out_in
    out_seq = []
    for peer in seq_peers:
        out_seq.append(
            begin(out_all.at[pl.ds(peer * per_seq, per_seq)], out_in.at[s], (d, peer))
        )
    out_in[s] = out_all[pl.ds(s * per_seq, per_seq)]
    row_up = lax.broadcasted_iota(jnp.int32, (LANES, hidden), 0)
    col_up = lax.broadcasted_iota(jnp.int32, (LANES, hidden), 1)
    spread = dot_plain(stacked, jnp.where(row_up == col_up % band, 1.0, 0.0).astype(jnp.bfloat16))
    spread = spread.reshape(data_count * seq_count, 16, hidden)
    which = lax.broadcasted_iota(jnp.int32, spread.shape, 0)
    column = lax.broadcasted_iota(jnp.int32, spread.shape, 2)
    picked = jnp.where(which == (column // band) * seq_count + s, spread, 0.0)
    m.up_bias[...] = jnp.sum(picked, axis=0)[9:10]

    arrive(tile_dp)
    whole_own = tiles.at[block(s, inbox)]
    tile_pair = [
        begin(whole_own, whole_own, (d, sibling)),
        begin(rest_in.at[s], rest_in.at[s], (d, sibling)),
    ]
    rest_far = begin(rest_in.at[s], rest_in.at[s], (d, across))
    quarter = inbox // 4

    def quarter_of(index, k):
        return tiles.at[pl.ds(pl.multiple_of(index * inbox + k * quarter, quarter), quarter)]

    def tile_send(k):
        part = quarter_of(s, k)
        return begin(part, part, (d, across))

    def tile_pass(k):
        tile_far[k].wait_recv()
        part = quarter_of(across, k)
        tile_pair.append(begin(part, part, (d, sibling)))

    tile_far = [tile_send(0)]
    arrive(out_seq)
    out_rows = m.out_rows
    natural = jnp.concatenate(
        [wide(out_in[j, i]) for i in range(per_seq) for j in range(seq_count)], axis=0
    )
    blank = jnp.zeros((64, 2 * width), jnp.float32)
    even = jnp.concatenate([natural, blank], axis=0)
    odd = jnp.concatenate([natural[64:192], blank, natural[0:64]], axis=0)
    out_rows[...] = low(jnp.where(core == 0, even, odd))

    state = seq_sum_begin(0, lambda i, j: dot_plain(pick(o1, i, j), out_rows[:, 0:width]))
    state = seq_sum_pass(state)
    tile_far.append(tile_send(1))
    x2, x3, dx = m.x2, m.x3, m.dx
    second = wide(text[0]) + seq_sum_end(state)
    x2[...] = second
    unit, _ = norm_parts(second)
    h2[block(s, tokens)] = low(unit * vector(3) + vector(4))
    h2_ag = seq_gather(rows_of(h2))
    tile_far += [tile_send(2), tile_send(3)]

    kv2, qm2, pr, o2, o_acc = m.kv2, m.qm2, m.pr, m.o2, m.o_acc

    def keys_values(here):
        rows = tiles[here]
        kv2[here, 0:256] = low(dot_plain(rows, cols[:, 128:384]))
        kv2[here, 256:512] = low(dot_plain(rows, halves[:, 128:384]))

    gather_forward(cross_ag)
    gather_end(cross_ag)
    keys_values(block(s, inbox))
    tile_pass(0)
    seq_pass(h2_ag)
    arrive(tile_pair[0:2])
    keys_values(block(sibling, inbox))
    tile_pass(1)
    rest_far.wait_recv()
    tile_pair.append(begin(rest_in.at[across], rest_in.at[across], (d, sibling)))
    gather_step(up_ag, 0)
    seq_end(h2_ag)
    query_full = dot_plain(h2[...], cols[:, 0:128])
    query_half = dot_plain(h2[...], halves[:, 0:128])
    for head in range(3):
        source = query_full if head < 2 else query_half
        qm2[block(head, length)] = low(wide(low(source)) * head_masks[head])
    tile_pass(2)
    tile_pass(3)
    keys_values(block(across, inbox))
    arrive(tile_pair[2:])
    keys_values(block(corner, inbox))
    rest_wide[...] = wide(rest_in[...]).reshape(rest_wide.shape)
    for k in range(columns):
        tiles[keys_main:keys, LANES * k : LANES * (k + 1)] = low(
            rest_wide[pl.ds(k, rests, stride=16), :]
        )
    keys_values(pl.ds(keys_main, rests))
    gather_step(up_ag, 1)
    gather_step(up_ag, 2)
    for head in range(3):
        base = 256 * (head // 2)
        place = 128 * (head // 2)

        @pl.loop(0, seq_count)
        def _(i):
            here = block(head * seq_count + i, tokens)
            scores = dot_right(qm2[here], kv2[:, base : base + 128]) * factor + m.key_bias[...]
            exponent = jnp.exp(scores - jnp.max(scores, axis=1, keepdims=True))
            chances = low(exponent / jnp.sum(exponent, axis=1, keepdims=True))
            pr[here] = chances
            result = dot_plain(chances, kv2[:, base + 128 : base + 256]) * head_masks[head]
            if head == 1:
                result = result + o_acc[block(i, tokens), place : place + 128]
            o_acc[block(i, tokens), place : place + 128] = result

        if head < 2:
            gather_step(down_ag, head)

    o2[...] = low(o_acc[...])
    state = seq_sum_begin(
        1, lambda i, j: dot_plain(pick(o2, i, j), out_rows[:, width : 2 * width])
    )
    state = seq_sum_pass(state)
    third = x2[...] + seq_sum_end(state)
    x3[...] = third
    unit, _ = norm_parts(third)
    h3[block(s, tokens)] = low(unit * vector(7) + vector(8))
    h3_ag = seq_gather(rows_of(h3))
    seq_end(cot_ag)
    seq_pass(h3_ag)
    gather_step(down_ag, 2)
    gather_end(down_ag)
    act, slope, du = m.act, m.slope, m.du
    slope[...] = dot_right(cot_all[...], down_all[...])
    gather_end(up_ag)
    seq_end(h3_ag)

    @pl.loop(0, seq_count)
    def _(i):
        here = block(i, tokens)
        pre = dot_plain(h3[here], cols[:, 1152 : 1152 + hidden]) + m.up_bias[...]
        cdf = 0.5 * (1.0 + lax.erf(pre * (1.0 / math.sqrt(2.0))))
        density = jnp.exp(-0.5 * pre * pre) * (1.0 / math.sqrt(2.0 * math.pi))
        act[here] = low(pre * cdf)
        grad = wide(low(slope[here]))
        du[here] = low(grad * (cdf + pre * density))

    state = seq_sum_begin(
        2, lambda i, j: dot_right(pick(du, i, j), cols[:, 1152 : 1152 + hidden])
    )
    state = seq_sum_pass(state)
    g_cols, g_down = m.g_cols, m.g_down
    g_down[...] = low(dot_left(act[...], cot_all[...]))
    g_down_view = lambda index: g_down.at[block(index, band)]
    down_rs = sum_begin(g_down_view, m.y_down, m.z_down)
    grad_mid = seq_sum_end(state)
    unit, inverse = norm_parts(x3[...])
    vv = m.vv
    vv[...] = jnp.zeros(vv.shape, jnp.float32)
    grad_out = wide(cot[0])
    dx3 = grad_out + norm_back(unit, inverse, vector(7), grad_mid)
    dx[...] = dx3
    e2[block(s, tokens)] = low(dx3)
    e2_ag = seq_gather(rows_of(e2))
    vv[0:1] = column_sum(grad_out)
    vv[7:8] = column_sum(grad_mid * unit)
    vv[8:9] = column_sum(grad_mid)
    vv[9:10, 0:hidden] = column_sum(wide(du[...]))

    g_cols[:, 1152 : 1152 + hidden] = low(dot_left(h3[...], du[...]))
    g_up_view = lambda index: g_cols.at[block(index, band), lanes(1152, hidden)]
    up_rs = sum_begin(g_up_view, m.y_up, m.z_up)
    sum_step(down_rs, 0)
    seq_pass(e2_ag)
    sum_step(down_rs, 1)
    seq_end(e2_ag)

    dom = m.dom
    grad_o = low(dot_right(e2[...], out_rows[:, width : 2 * width]))
    for head in range(3):
        place = 128 * (head // 2)
        dom[block(head, length)] = low(wide(grad_o[:, place : place + 128]) * head_masks[head])
    ds, dkv2, dq2 = m.ds, m.dkv2, m.dq2
    for head in range(3):
        base = 256 * (head // 2)
        place = 128 * (head // 2)

        @pl.loop(0, seq_count)
        def _(i):
            here = block(head * seq_count + i, tokens)
            chances = wide(pr[here])
            grad_p = dot_right(dom[here], kv2[:, base + 128 : base + 256])
            weighted = jnp.sum(chances * grad_p, axis=1, keepdims=True)
            grad_s = low(chances * (grad_p - weighted))
            ds[here] = grad_s
            result = dot_plain(grad_s, kv2[:, base : base + 128]) * (head_masks[head] * factor)
            if head == 1:
                result = result + o_acc[block(i, tokens), place : place + 128]
            o_acc[block(i, tokens), place : place + 128] = result

        if head < 2:
            sum_step(down_rs, 2 + head)

    dq2[...] = low(o_acc[...])
    state = seq_sum_begin(
        4,
        lambda i, j: dot_right(pick(dq2, i, j, slice(0, 128)), cols[:, 0:128])
        + dot_right(pick(dq2, i, j, slice(128, 256)), halves[:, 0:128]),
    )
    state = seq_sum_pass(state)

    g_out, g_out_send = m.g_out, m.g_out_send

    def out_grad(slot, value):
        odd = jnp.concatenate([value[192:256], value[0:128]], axis=0)
        natural = jnp.where(core == 0, value[0:192], odd)
        for i in range(per_seq):
            for j in range(seq_count):
                start = shard * (i * seq_count + j)
                g_out_send[slot, j, i] = low(natural[start : start + shard])
        target = g_out.at[pl.ds(s * per_seq, per_seq), :, lanes(slot * width, width)]
        copies = [begin(g_out_send.at[slot, peer], target, (d, peer)) for peer in seq_peers]
        g_out[pl.ds(s * per_seq, per_seq), :, slot * width : (slot + 1) * width] = g_out_send[
            slot, s
        ]
        return copies

    xout_seq = out_grad(1, dot_left(o2[...], e2[...]))
    sum_step(up_rs, 0)
    second_grad = seq_sum_end(state)
    unit, inverse = norm_parts(x2[...])
    dx2 = dx[...] + norm_back(unit, inverse, vector(3), second_grad)
    dx[...] = dx2
    e1[block(s, tokens)] = low(dx2)
    e1_ag = seq_gather(rows_of(e1))
    vv[3:4] = column_sum(second_grad * unit)
    vv[4:5] = column_sum(second_grad)
    sum_step(up_rs, 1)
    arrive(xout_seq)
    xout_view = lambda index: g_out.at[index, :, lanes(width, width)]
    xout_rs = sum_begin(xout_view, m.y_xout, m.z_xout)

    for tile in range(2):
        first, count = (0, 2 * length) if tile == 0 else (2 * length, length)
        base = 256 * tile
        for start, size in spans(0, keys, 512):
            cut = slice(start, start + size)
            dkv2[cut, base : base + 128] = low(
                dot_left(ds[first : first + count, cut], qm2[first : first + count]) * factor
            )
            dkv2[cut, base + 128 : base + 256] = low(
                dot_left(pr[first : first + count, cut], dom[first : first + count])
            )
    seq_pass(e1_ag)
    sum_step(up_rs, 2)
    dn = m.dn

    def tile_grads(here):
        dn[here] = low(
            dot_right(dkv2[here, 0:256], cols[:, 128:384])
            + dot_right(dkv2[here, 256:512], halves[:, 128:384])
        )

    dr_out, dr_pair, dr_far, dr_home = m.dr_out, m.dr_pair, m.dr_far, m.dr_home
    dn_pair, dn_far, dn_home = m.dn_pair, m.dn_far, m.dn_home
    tile_grads(block(corner, inbox))
    pair_far = begin(dn.at[block(corner, inbox)], dn_pair.at[1], (d, sibling))
    tile_grads(pl.ds(keys_main, rests))
    rest_wide[...] = jnp.zeros(rest_wide.shape, jnp.float32)
    for k in range(columns):
        rest_wide[pl.ds(k, rests, stride=16), :] = wide(
            dn[keys_main:keys, LANES * k : LANES * (k + 1)]
        )
    dr_out[...] = low(rest_wide[...]).reshape(dr_out.shape)
    rest_pair = [
        begin(dr_out.at[peer], dr_pair.at[k], (d, sibling))
        for k, peer in enumerate((sibling, corner))
    ]
    tile_grads(block(across, inbox))
    pair_far.wait_recv()
    fold = dn.at[block(across, inbox)]
    fold[...] = low(wide(fold[...]) + wide(dn_pair[1]))
    arrive(rest_pair)
    dr_out[across] = low(wide(dr_out[across]) + wide(dr_pair[1]))
    rest_far = begin(dr_out.at[across], dr_far, (d, across))

    def far_send(k):
        return begin(quarter_in(dn, across, k), dn_far.at[block(k, quarter)], (d, across))

    def quarter_in(ref, index, k):
        return ref.at[pl.ds(pl.multiple_of(index * inbox + k * quarter, quarter), quarter)]

    far_copies = [far_send(0)]
    g_half, g_half2, half_in = m.g_half, m.g_half2, m.half_in
    grad = dot_left(h2[...], dq2[...])
    g_cols[:, 0:128] = low(grad[:, 0:128])
    g_half[:, 0:128] = low(grad[:, 128:256])
    for cut in range(3):
        span = slice(256 * cut, 256 * cut + 256)
        grad = dot_left(tiles[:, span], dkv2[...])
        g_cols[span, 128:384] = low(grad[:, 0:256])
        g_half[span, 128:384] = low(grad[:, 256:512])
    half_cross = links.make(g_half, half_in, (d, sibling))

    @pl.when(core == 1)
    def _():
        half_cross.start()

    g_cross_view = lambda index: g_cols.at[block(index, band), lanes(0, 384)]
    cross_rs = sum_begin(g_cross_view, m.y_cross, m.z_cross)
    far_copies += [far_send(1)]
    tile_grads(block(sibling, inbox))
    pair_own = begin(dn.at[block(sibling, inbox)], dn_pair.at[0], (d, sibling))
    tile_grads(block(s, inbox))
    sum_step(up_rs, 3)
    sum_middle(xout_rs)

    seq_end(e1_ag)
    grad_o = low(dot_right(e1[...], out_rows[:, 0:width]))
    grads = []
    dqkv = m.dqkv
    for head in range(3):
        base = 384 * (head // 2)
        place = 128 * (head // 2)
        here = block(head, length)
        dm = low(wide(grad_o[:, place : place + 128]) * head_masks[head])
        chances = p1[here]
        grad_p = dot_right(dm, qkv1[:, base + 256 : base + 384])
        weighted = jnp.sum(chances * grad_p, axis=1, keepdims=True)
        grad_s = low(chances * (grad_p - weighted))
        grads.append(
            (
                dot_plain(grad_s, qkv1[:, base + 128 : base + 256]) * (head_masks[head] * factor),
                dot_left(grad_s, qm1[here]) * factor,
                dot_left(low(chances), dm),
            )
        )
    for k in range(3):
        dqkv[:, 128 * k : 128 * k + 128] = low(grads[0][k] + grads[1][k])
        dqkv[:, 384 + 128 * k : 512 + 128 * k] = low(grads[2][k])
    state = seq_sum_begin(
        5,
        lambda i, j: dot_right(pick(dqkv, i, j, slice(0, 384)), cols[:, 384:768])
        + dot_right(pick(dqkv, i, j, slice(384, 768)), halves[:, 384:768]),
    )

    grad = dot_left(h1[...], dqkv[...])
    g_cols[:, 384:768] = low(grad[:, 0:384])
    g_half2[...] = low(grad[:, 384:768])
    half_self = links.make(g_half2, half_in, (d, sibling))

    @pl.when(core == 0)
    def _():
        half_self.start()

    state = seq_sum_pass(state)
    sout_seq = out_grad(0, dot_left(o1[...], e1[...]))
    far_copies += [far_send(2), far_send(3)]
    g_self_view = lambda index: g_cols.at[block(index, band), lanes(384, 768)]

    @pl.when(core == 0)
    def _():
        half_cross.wait_recv()
        g_cols[:, 768:1152] = low(wide(g_half[...]) + wide(half_in[...]))

    @pl.when(core == 1)
    def _():
        half_self.wait_recv()
        g_cols[:, 768:1152] = low(wide(g_half2[...]) + wide(half_in[...]))

    self_rs = sum_begin(g_self_view, m.y_self, m.z_self)
    arrive(sout_seq)
    sout_view = lambda index: g_out.at[index, :, lanes(0, width)]
    sout_rs = sum_begin(sout_view, m.y_sout, m.z_sout)
    sum_middle(cross_rs)

    arrive([pair_own, rest_far])
    dr_out[s] = low(wide(dr_out[s]) + wide(dr_pair[0]) + wide(dr_far[...]))
    for k in range(4):
        far_copies[k].wait_recv()
        mine = quarter_in(dn, s, k)
        there = block(k, quarter)
        mine[...] = low(wide(mine[...]) + wide(dn_pair[0, there]) + wide(dn_far[there]))
    home_dp = []
    own_home = block(d, main)
    for k in range(1, data_count):
        peer = (d + k) % data_count
        source = dn.at[block(s * data_count + peer, main)]
        home_dp.append(begin(source, dn_home.at[own_home], (peer, s)))
        home_dp.append(begin(dr_out.at[s, peer], dr_home.at[d], (peer, s)))
    dn_home[own_home] = dn[block(s * data_count + d, main)]
    dr_home[d] = dr_out[s, d]

    first_grad = seq_sum_end(state)
    unit, inverse = norm_parts(wide(text[0]))
    vv[1:2] = column_sum(first_grad * unit)
    vv[2:3] = column_sum(first_grad)
    r_tgrad[...] = low(dx[...] + norm_back(unit, inverse, vector(1), first_grad))
    out_state = seq_sum_begin(3, lambda i, j: dot_plain(pick(act, i, j), down_all[...]))
    out_state = seq_sum_pass(out_state)

    sum_middle(self_rs)
    sum_middle(sout_rs)
    r_text[...] = low(x3[...] + seq_sum_end(out_state) + vector(0))

    cols_out, cols_in = m.cols_out, m.cols_in

    def finish_cols(first, size, state):
        total = low(sum_end(state))
        place = lanes(first, size)
        total = wide(total)
        for j in range(seq_count):
            cols_out[j, :, place] = low(total[shard * j : shard * (j + 1)])
        cols_in[s, :, place] = cols_out[s, :, place]
        return [
            begin(cols_out.at[peer, :, place], cols_in.at[s, :, place], (d, peer))
            for peer in seq_peers
        ]

    r_down[...] = sum_end(down_rs)
    ends = finish_cols(1152, hidden, up_rs)
    r_outs[1] = sum_end(xout_rs)
    ends += finish_cols(0, 384, cross_rs)

    arrive(home_dp)
    gain_sum = jnp.zeros((1, width), jnp.float32)
    shift_sum = jnp.zeros((1, width), jnp.float32)
    for t in range(tile_count):
        grad = wide(dn_home[block(0, main)]) * route[0][t]
        rest = wide(dr_home[0]) * route[0][t]
        for p in range(1, data_count):
            grad = grad + wide(dn_home[block(p, main)]) * route[p][t]
            rest = rest + wide(dr_home[p]) * route[p][t]
        rest = jnp.concatenate([rest[k : k + 1] for k in range(columns)], axis=1)
        unit, inverse = norm_parts(wide(img[t, 0:main]))
        gain_sum = gain_sum + column_sum(grad * unit)
        shift_sum = shift_sum + column_sum(grad)
        r_igrad[t, 0:main] = low(norm_back(unit, inverse, vector(5), grad))
        unit, inverse = norm_parts(wide(img[t, main:real_rows]))
        gain_sum = gain_sum + rest * unit
        shift_sum = shift_sum + rest
        r_igrad[t, main:real_rows] = low(norm_back(unit, inverse, vector(5), rest))
    vv[5:6] = gain_sum
    vv[6:7] = shift_sum

    vv_out, vv_in, vq = m.vv_out, m.vv_in, m.vq
    everything = vv[...]
    for p in range(data_count):
        turned = everything if p == 0 else pltpu.roll(everything, width - band * p, 1)
        vv_out[p] = turned[:, 0:LANES]
    vv_dp = []
    for k in range(1, data_count):
        peer = (d + k) % data_count
        vv_dp.append(begin(vv_out.at[peer], vv_in.at[d], (peer, s)))
    vv_in[d] = vv_out[d]

    ends += finish_cols(384, 768, self_rs)
    r_outs[0] = sum_end(sout_rs)

    arrive(vv_dp)
    total = vv_in[0]
    for p in range(1, data_count):
        total = total + vv_in[p]
    vq[s] = total
    vq_seq = [begin(vq.at[s], vq.at[s], (d, peer)) for peer in seq_peers]
    bias_grad = total[9:10]

    arrive(ends)
    r_cols[...] = cols_in[...]
    arrive(vq_seq)
    total = vq[0] + vq[1] + vq[2] + vq[3]
    r_vec[...] = pltpu.roll(total, (LANES - shard * s) % LANES, 1)
    r_vec[9:10] = bias_grad

    for copy in links.started:
        copy.wait_send()

    @pl.when(core == 0)
    def _():
        half_self.wait_send()

    @pl.when(core == 1)
    def _():
        half_cross.wait_send()


def unpack_kernel(t_out, t_grad, i_grad, cols, outs, down, vec, *results):
    o_text, o_tgrad, o_igrad, o_q, o_k, o_v, o_o, o_xq, o_xk, o_xv, o_xo, o_up, o_down, *vectors = (
        results
    )
    seq_count, shard, total = cols.shape
    hidden = total - 1152
    band = down.shape[0]
    o_text[0] = t_out[...]
    o_tgrad[0] = t_grad[...]
    o_igrad[...] = i_grad[...]
    for k, result in enumerate((o_xq, o_xk, o_xv, o_q, o_k, o_v)):
        here = slice(LANES * k, LANES * (k + 1))
        there = slice(768 + LANES * (k % 3), 768 + LANES * (k % 3 + 1))
        carrier = k // 3
        for j, tile in ((0, 0), (1, 2), (2, 3), (3, 5)):
            result[:, LANES * tile : LANES * (tile + 1)] = wide(cols[j, :, here])
        for j, tile in ((carrier, 1), (2 + carrier, 4)):
            result[:, LANES * tile : LANES * (tile + 1)] = wide(cols[j, :, there])
    o_o[...] = outs[0]
    o_xo[...] = outs[1]
    o_down[...] = down[...]
    lane = lax.broadcasted_iota(jnp.int32, (1, LANES), 1)
    parts = [wide(cols[j, :, 1152:total]) for j in range(seq_count)]
    for tile in range(hidden * seq_count // LANES):
        pieces = []
        for at, size in spans(LANES * tile, LANES * tile + LANES, band):
            group = at // band
            first = band * (group // seq_count) + at % band
            pieces.append((parts[group % seq_count], first, at % LANES, size))
        o_up[:, LANES * tile : LANES * (tile + 1)] = lane_pick(pieces, lane)
    vectors[0][...] = vec[9, 0:band]
    for k, result in enumerate(vectors[1:]):
        result[...] = vec[k, 0:shard]


def fused_device(
    text_in, image_in, tile_slide, owner_map, text_cot,
    w_query, w_key, w_value, w_out, c_query, c_key, c_value, c_out, w_up, w_down, b_up, b_down,
    self_gain, self_shift, cross_gain, cross_shift, tile_gain, tile_shift, mlp_gain, mlp_shift,
):
    data_count, seq_count = lax.axis_size("dp"), lax.axis_size("seq")
    tile_count, real_rows, width = image_in.shape
    tokens = text_in.shape[1]
    shard = w_query.shape[0]
    band = shard * seq_count
    hidden = w_up.shape[1] // seq_count
    main = real_rows // 16 * 16

    gains = (
        self_gain, self_shift, cross_gain, cross_shift, tile_gain, tile_shift, mlp_gain, mlp_shift,
    )
    inputs = (
        tile_slide, owner_map, text_in, image_in, text_cot, w_query, w_key, w_value, w_out,
        c_query, c_key, c_value, c_out, w_up, w_down,
        *[member.reshape(1, -1) for member in (b_up, b_down, *gains)],
    )
    in_specs = [pl.BlockSpec(memory_space=pltpu.SMEM)] * 2
    in_specs += [pl.BlockSpec(memory_space=pltpu.VMEM)] * (len(inputs) - 2)
    row_out = jax.ShapeDtypeStruct((tokens, width), jnp.bfloat16)
    packed_shape = [
        row_out,
        row_out,
        jax.ShapeDtypeStruct(image_in.shape, jnp.bfloat16),
        jax.ShapeDtypeStruct((seq_count, shard, 1152 + hidden), jnp.bfloat16),
        jax.ShapeDtypeStruct((2, shard, width), jnp.float32),
        jax.ShapeDtypeStruct((band, width), jnp.float32),
        jax.ShapeDtypeStruct((16, LANES), jnp.float32),
    ]
    shapes = scratch_of(width, tokens, seq_count, data_count, hidden, main, shard)
    scratch = [pltpu.VMEM(shape, kind) for shape, kind in shapes.values()]
    scratch += [pltpu.SemaphoreType.DMA((COPY_SLOTS,))] * 2
    names = [*shapes, "send", "recv"]
    packed = pl.pallas_call(
        partial(fused_kernel, names, len(inputs)),
        out_shape=packed_shape,
        in_specs=in_specs,
        out_specs=[pl.BlockSpec(memory_space=pltpu.VMEM)] * len(packed_shape),
        scratch_shapes=scratch,
        compiler_params=pltpu.CompilerParams(
            collective_id=0, has_side_effects=True, vmem_limit_bytes=60 * 1024 * 1024
        ),
        name="decoder_layer",
    )(*inputs)
    square = jax.ShapeDtypeStruct((shard, width), jnp.float32)
    out_shape = [
        jax.ShapeDtypeStruct(text_in.shape, jnp.bfloat16),
        jax.ShapeDtypeStruct(text_in.shape, jnp.bfloat16),
        jax.ShapeDtypeStruct(image_in.shape, jnp.bfloat16),
        *[square] * 8,
        jax.ShapeDtypeStruct((shard, hidden * seq_count), jnp.float32),
        jax.ShapeDtypeStruct((band, width), jnp.float32),
        jax.ShapeDtypeStruct((band,), jnp.float32),
        *[jax.ShapeDtypeStruct((shard,), jnp.float32)] * 9,
    ]
    return tuple(
        pl.pallas_call(
            unpack_kernel,
            out_shape=out_shape,
            in_specs=[pl.BlockSpec(memory_space=pltpu.VMEM)] * len(packed),
            out_specs=[pl.BlockSpec(memory_space=pltpu.VMEM)] * len(out_shape),
            name="unpack",
        )(*packed)
    )


def fused_fits(mesh):
    return mesh.shape["seq"] == 4 and 768 % (8 * mesh.shape["dp"] * mesh.shape["seq"]) == 0


def solution(mesh):
    placed = (
        P("dp", "seq", None),
        P("dp", "seq", None),
        P(),
        P(),
        P("dp", "seq", None),
        P(("dp", "seq"), None),
        P(("dp", "seq"), None),
        P(("dp", "seq"), None),
        P(("dp", "seq"), None),
        P(("dp", "seq"), None),
        P(("dp", "seq"), None),
        P(("dp", "seq"), None),
        P(("dp", "seq"), None),
        P(("dp", "seq"), None),
        P(("dp", "seq"), None),
        P(("dp", "seq")),
        P(("dp", "seq")),
        P(("dp", "seq")),
        P(("dp", "seq")),
        P(("dp", "seq")),
        P(("dp", "seq")),
        P(("dp", "seq")),
        P(("dp", "seq")),
        P(("dp", "seq")),
        P(("dp", "seq")),
    )
    return jax.shard_map(
        fused_device if fused_fits(mesh) else per_device,
        mesh=mesh,
        in_specs=placed,
        out_specs=(
            P("dp", "seq", None),
            P("dp", "seq", None),
            P("dp", "seq", None),
            P(("dp", "seq"), None),
            P(("dp", "seq"), None),
            P(("dp", "seq"), None),
            P(("dp", "seq"), None),
            P(("dp", "seq"), None),
            P(("dp", "seq"), None),
            P(("dp", "seq"), None),
            P(("dp", "seq"), None),
            P(("dp", "seq"), None),
            P(("dp", "seq"), None),
            P(("dp", "seq")),
            P(("dp", "seq")),
            P(("dp", "seq")),
            P(("dp", "seq")),
            P(("dp", "seq")),
            P(("dp", "seq")),
            P(("dp", "seq")),
            P(("dp", "seq")),
            P(("dp", "seq")),
            P(("dp", "seq")),
        ),
        check_vma=False,
    )
```

```python
from functools import partial
import math
from types import SimpleNamespace

import jax
import jax.numpy as jnp
from jax import lax
from jax.experimental import pallas as pl
from jax.experimental.pallas import tpu as pltpu
from jax.sharding import PartitionSpec as P

HEAD = 64
LANES = 128
MESH = pl.DeviceIdType.MESH


EPSILON = 1e-05
MASKED_SCORE = -1e30


def combined_all(x, axis, combine):
    everything = jax.tree.map(lambda part: lax.all_gather(part, axis), x)
    initial = jax.tree.map(lambda part: part[0], everything)

    def step(k, so_far):
        return combine(so_far, jax.tree.map(lambda part: part[k], everything))

    return lax.fori_loop(1, lax.axis_size(axis), step, initial)


def norm_rows(values, gain_row, shift_row):
    average = jnp.mean(values, axis=-1, keepdims=True)
    centered = values - average
    spread = jnp.mean(centered * centered, axis=-1, keepdims=True)
    return centered * lax.rsqrt(spread + EPSILON) * gain_row + shift_row


def matmul(former, latter):
    return jnp.dot(former, latter, preferred_element_type=jnp.float32)


def matmul_trans(former, latter):
    return lax.dot_general(
        former, latter, (((1,), (1,)), ((), ())), preferred_element_type=jnp.float32
    )


def outer_sum(former, latter):
    return lax.dot_general(
        former, latter, (((0,), (0,)), ((), ())), preferred_element_type=jnp.float32
    )


def head_pair(matrix, pair_index):
    columns = lax.dynamic_slice_in_dim(matrix, pair_index * 2 * HEAD, 2 * HEAD, 1)
    return columns.reshape(columns.shape[0], 2, HEAD)


def put_pair(matrix, update, pair_index):
    return lax.dynamic_update_slice_in_dim(
        matrix, update.reshape(update.shape[0], 2 * HEAD), pair_index * 2 * HEAD, 1
    )


def pick_pair(stacked, pair_index):
    return lax.dynamic_index_in_dim(stacked, pair_index, 0, keepdims=False)


def pair_scores(query_rows, key_rows, allowed, pair_index):
    factor = 1.0 / math.sqrt(HEAD)
    scores = (
        jnp.einsum(
            "qhd,khd->hqk",
            head_pair(query_rows, pair_index),
            head_pair(key_rows, pair_index),
            preferred_element_type=jnp.float32,
        )
        * factor
    )
    return jnp.where(allowed[None], scores, MASKED_SCORE)


def attend_stats(query_rows, key_rows, allowed):
    pair_count = query_rows.shape[1] // (2 * HEAD)

    def one_pair(pair_index, state_now):
        row_max, row_sum = state_now
        scores = pair_scores(query_rows, key_rows, allowed, pair_index)
        highest = jnp.max(scores, axis=2)
        summed = jnp.sum(jnp.exp(scores - highest[..., None]), axis=2)
        return (
            lax.dynamic_update_index_in_dim(row_max, highest, pair_index, 0),
            lax.dynamic_update_index_in_dim(row_sum, summed, pair_index, 0),
        )

    empty_stats = jnp.zeros((pair_count, 2, query_rows.shape[0]), jnp.float32)
    return lax.fori_loop(0, pair_count, one_pair, (empty_stats, empty_stats))


def attend_forward(query_rows, key_rows, value_rows, allowed, maxima, totals):
    pair_count = query_rows.shape[1] // (2 * HEAD)
    stats_given = maxima is not None
    if not stats_given:
        maxima = jnp.zeros((pair_count, 2, query_rows.shape[0]), jnp.float32)
        totals = jnp.zeros_like(maxima)

    def one_pair(pair_index, state_now):
        output, row_max, row_sum = state_now
        scores = pair_scores(query_rows, key_rows, allowed, pair_index)
        if stats_given:
            highest = pick_pair(row_max, pair_index)
            exponent = jnp.exp(scores - highest[..., None])
            summed = pick_pair(row_sum, pair_index)
        else:
            highest = jnp.max(scores, axis=2)
            exponent = jnp.exp(scores - highest[..., None])
            summed = jnp.sum(exponent, axis=2)
            row_max = lax.dynamic_update_index_in_dim(row_max, highest, pair_index, 0)
            row_sum = lax.dynamic_update_index_in_dim(row_sum, summed, pair_index, 0)
        weights = (exponent / summed[..., None]).astype(jnp.bfloat16)
        mixture = jnp.einsum(
            "hqk,khd->qhd",
            weights,
            head_pair(value_rows, pair_index),
            preferred_element_type=jnp.float32,
        )
        return (put_pair(output, mixture, pair_index), row_max, row_sum)

    start_state = (jnp.zeros(query_rows.shape, jnp.float32), maxima, totals)
    return lax.fori_loop(0, pair_count, one_pair, start_state)


def attend_rowsums(query_rows, key_rows, value_rows, allowed, maxima, totals, grad_rows):
    pair_count = query_rows.shape[1] // (2 * HEAD)

    def one_pair(pair_index, row_terms):
        scores = pair_scores(query_rows, key_rows, allowed, pair_index)
        chances = (
            jnp.exp(scores - pick_pair(maxima, pair_index)[..., None])
            / pick_pair(totals, pair_index)[..., None]
        )
        grad_chances = jnp.einsum(
            "qhd,khd->hqk",
            head_pair(grad_rows, pair_index),
            head_pair(value_rows, pair_index),
            preferred_element_type=jnp.float32,
        )
        return lax.dynamic_update_index_in_dim(
            row_terms, jnp.sum(chances * grad_chances, axis=2), pair_index, 0
        )

    return lax.fori_loop(0, pair_count, one_pair, jnp.zeros_like(maxima))


def attend_backward(
    query_rows, key_rows, value_rows, allowed, maxima, totals, grad_rows, row_terms
):
    pair_count = query_rows.shape[1] // (2 * HEAD)
    factor = 1.0 / math.sqrt(HEAD)

    def one_pair(pair_index, state_now):
        grad_query, grad_key, grad_value = state_now
        scores = pair_scores(query_rows, key_rows, allowed, pair_index)
        chances = (
            jnp.exp(scores - pick_pair(maxima, pair_index)[..., None])
            / pick_pair(totals, pair_index)[..., None]
        )
        grad_heads = head_pair(grad_rows, pair_index)
        grad_chances = jnp.einsum(
            "qhd,khd->hqk",
            grad_heads,
            head_pair(value_rows, pair_index),
            preferred_element_type=jnp.float32,
        )
        if row_terms is None:
            weighted = jnp.sum(chances * grad_chances, axis=2)
        else:
            weighted = pick_pair(row_terms, pair_index)
        grad_scores = (chances * (grad_chances - weighted[..., None])).astype(jnp.bfloat16)
        query_part = (
            jnp.einsum(
                "hqk,khd->qhd",
                grad_scores,
                head_pair(key_rows, pair_index),
                preferred_element_type=jnp.float32,
            )
            * factor
        )
        key_part = (
            jnp.einsum(
                "hqk,qhd->khd",
                grad_scores,
                head_pair(query_rows, pair_index),
                preferred_element_type=jnp.float32,
            )
            * factor
        )
        value_part = jnp.einsum(
            "hqk,qhd->khd",
            chances.astype(jnp.bfloat16),
            grad_heads,
            preferred_element_type=jnp.float32,
        )
        return (
            put_pair(grad_query, query_part, pair_index),
            put_pair(grad_key, key_part, pair_index),
            put_pair(grad_value, value_part, pair_index),
        )

    start_state = (
        jnp.zeros(query_rows.shape, jnp.float32),
        jnp.zeros(key_rows.shape, jnp.float32),
        jnp.zeros(value_rows.shape, jnp.float32),
    )
    return lax.fori_loop(0, pair_count, one_pair, start_state)


def join_stats(former, latter):
    highest = jnp.maximum(former[0], latter[0])
    return (
        highest,
        former[1] * jnp.exp(former[0] - highest) + latter[1] * jnp.exp(latter[0] - highest),
    )


def split_rows(matrix, data_count, seq_count):
    return matrix.reshape(
        data_count, seq_count, matrix.shape[0] // (data_count * seq_count), matrix.shape[1]
    )


def fold_rows(pieces):
    return jnp.sum(pieces, axis=1).reshape(pieces.shape[0] * pieces.shape[2], pieces.shape[3])


def per_device(
    text_in,
    image_in,
    tile_slide,
    owner_map,
    text_cot,
    w_query,
    w_key,
    w_value,
    w_out,
    c_query,
    c_key,
    c_value,
    c_out,
    w_up,
    w_down,
    b_up,
    b_down,
    self_gain,
    self_shift,
    cross_gain,
    cross_shift,
    tile_gain,
    tile_shift,
    mlp_gain,
    mlp_shift,
):
    gathered = (
        lax.all_gather(w_query, ("dp", "seq"), axis=0, tiled=True),
        lax.all_gather(w_key, ("dp", "seq"), axis=0, tiled=True),
        lax.all_gather(w_value, ("dp", "seq"), axis=0, tiled=True),
        lax.all_gather(w_out, ("dp", "seq"), axis=0, tiled=True),
        lax.all_gather(c_query, ("dp", "seq"), axis=0, tiled=True),
        lax.all_gather(c_key, ("dp", "seq"), axis=0, tiled=True),
        lax.all_gather(c_value, ("dp", "seq"), axis=0, tiled=True),
        lax.all_gather(c_out, ("dp", "seq"), axis=0, tiled=True),
        lax.all_gather(w_up, ("dp", "seq"), axis=0, tiled=True),
        lax.all_gather(w_down, ("dp", "seq"), axis=0, tiled=True),
        lax.all_gather(b_up, ("dp", "seq"), axis=0, tiled=True),
        lax.all_gather(b_down, ("dp", "seq"), axis=0, tiled=True),
        lax.all_gather(self_gain, ("dp", "seq"), axis=0, tiled=True),
        lax.all_gather(self_shift, ("dp", "seq"), axis=0, tiled=True),
        lax.all_gather(cross_gain, ("dp", "seq"), axis=0, tiled=True),
        lax.all_gather(cross_shift, ("dp", "seq"), axis=0, tiled=True),
        lax.all_gather(tile_gain, ("dp", "seq"), axis=0, tiled=True),
        lax.all_gather(tile_shift, ("dp", "seq"), axis=0, tiled=True),
        lax.all_gather(mlp_gain, ("dp", "seq"), axis=0, tiled=True),
        lax.all_gather(mlp_shift, ("dp", "seq"), axis=0, tiled=True),
    )
    query_mat, key_mat, value_mat, proj_mat = (gathered[0], gathered[1], gathered[2], gathered[3])
    xquery_mat, xkey_mat, xvalue_mat, xproj_mat = (
        gathered[4],
        gathered[5],
        gathered[6],
        gathered[7],
    )
    up_mat, down_mat = (gathered[8], gathered[9])
    vectors = [member.astype(jnp.float32) for member in gathered[10:]]
    (
        up_bias,
        down_bias,
        gain_one,
        shift_one,
        gain_two,
        shift_two,
        gain_tile,
        shift_tile,
        gain_three,
        shift_three,
    ) = vectors
    text_rows = text_in[0].astype(jnp.float32)
    rows_here = text_rows.shape[0]
    hidden_dim = text_rows.shape[1]
    normed_one, norm_one_back = jax.vjp(norm_rows, text_rows, gain_one, shift_one)
    first_in = normed_one.astype(jnp.bfloat16)
    query_one = matmul(first_in, query_mat).astype(jnp.bfloat16)
    key_one = matmul(first_in, key_mat).astype(jnp.bfloat16)
    value_one = matmul(first_in, value_mat).astype(jnp.bfloat16)
    key_all, value_all = (
        lax.all_gather(key_one, "seq", axis=0, tiled=True),
        lax.all_gather(value_one, "seq", axis=0, tiled=True),
    )
    positions = lax.axis_index("seq") * rows_here + jnp.arange(rows_here)
    causal = positions[:, None] >= jnp.arange(key_all.shape[0])[None, :]
    attend_one, max_one, sum_one = attend_forward(query_one, key_all, value_all, causal, None, None)
    mixed_one = attend_one.astype(jnp.bfloat16)
    second = text_rows + matmul(mixed_one, proj_mat)
    normed_two, norm_two_back = jax.vjp(norm_rows, second, gain_two, shift_two)
    second_in = normed_two.astype(jnp.bfloat16)
    query_two = matmul(second_in, xquery_mat).astype(jnp.bfloat16)
    tile_rows = image_in.astype(jnp.float32)
    normed_tiles, norm_tile_back = jax.vjp(norm_rows, tile_rows, gain_tile, shift_tile)
    tiles_in = normed_tiles.astype(jnp.bfloat16)
    data_index = lax.axis_index("dp")
    data_count = lax.axis_size("dp")
    seq_count = lax.axis_size("seq")
    tile_count = image_in.shape[0]
    slot_rows = image_in.shape[1]
    slide_ids = jnp.arange(owner_map.shape[0])
    destination = jnp.sum(
        jnp.where(tile_slide[:, None] == slide_ids[None, :], owner_map[None, :], 0), axis=1
    )
    own_destination = lax.dynamic_slice_in_dim(destination, data_index * tile_count, tile_count)
    routing = (own_destination[None, :] == jnp.arange(data_count)[:, None]).astype(jnp.bfloat16)
    outgoing = jnp.einsum(
        "pt,trd->prd", routing, tiles_in, preferred_element_type=jnp.float32
    ).astype(jnp.bfloat16)
    incoming = lax.all_to_all(outgoing, "dp", split_axis=0, concat_axis=0, tiled=True)
    arrived = jnp.any(destination.reshape(data_count, tile_count) == data_index, axis=1)
    flat_in = incoming.reshape(data_count * slot_rows, hidden_dim)
    allowed_rows = jnp.broadcast_to(arrived[:, None], (data_count, slot_rows)).reshape(-1)
    key_two = matmul(flat_in, xkey_mat).astype(jnp.bfloat16)
    value_two = matmul(flat_in, xvalue_mat).astype(jnp.bfloat16)
    query_far = lax.all_gather(query_two, "seq", axis=0, tiled=True)
    allowed_near = allowed_rows[None, :]
    local_max, local_sum = attend_stats(query_far, key_two, allowed_near)
    max_two, sum_two = combined_all((local_max, local_sum), "seq", join_stats)
    partial_rows = attend_forward(query_far, key_two, value_two, allowed_near, max_two, sum_two)[0]
    attend_two = lax.psum_scatter(
        partial_rows.astype(jnp.bfloat16), "seq", scatter_dimension=0, tiled=True
    )
    third_sum = second + matmul(attend_two, xproj_mat)
    normed_three, norm_three_back = jax.vjp(norm_rows, third_sum, gain_three, shift_three)
    third_in = normed_three.astype(jnp.bfloat16)
    pre_gelu = matmul(third_in, up_mat) + up_bias
    activated, gelu_back = jax.vjp(partial(jax.nn.gelu, approximate=False), pre_gelu)
    act_in = activated.astype(jnp.bfloat16)
    result = third_sum + matmul(act_in, down_mat) + down_bias
    text_out = result.astype(jnp.bfloat16)[None]
    cot_rows = text_cot[0]
    grad_res = cot_rows.astype(jnp.float32)
    down_grad = outer_sum(act_in, cot_rows)
    downbias_grad = jnp.sum(grad_res, axis=0)
    grad_act = matmul_trans(cot_rows, down_mat).astype(jnp.bfloat16)
    grad_pre = gelu_back(grad_act.astype(jnp.float32))[0].astype(jnp.bfloat16)
    up_grad = outer_sum(third_in, grad_pre)
    upbias_grad = jnp.sum(grad_pre.astype(jnp.float32), axis=0)
    grad_mid, mgain_grad, mshift_grad = norm_three_back(matmul_trans(grad_pre, up_mat))
    grad_third = grad_res + grad_mid
    branch_two = grad_third.astype(jnp.bfloat16)
    xproj_grad = outer_sum(attend_two, branch_two)
    grad_attend_two = matmul_trans(branch_two, xproj_mat).astype(jnp.bfloat16)
    grad_far = lax.all_gather(grad_attend_two, "seq", axis=0, tiled=True)
    row_part = attend_rowsums(
        query_far, key_two, value_two, allowed_near, max_two, sum_two, grad_far
    )
    row_terms = lax.psum(row_part, "seq")
    query_grad_far, key_grad_two, value_grad_two = attend_backward(
        query_far, key_two, value_two, allowed_near, max_two, sum_two, grad_far, row_terms
    )
    query_grad_two = lax.psum_scatter(
        query_grad_far.astype(jnp.bfloat16), "seq", scatter_dimension=0, tiled=True
    )
    gkey_two = key_grad_two.astype(jnp.bfloat16)
    gvalue_two = value_grad_two.astype(jnp.bfloat16)
    xquery_grad = outer_sum(second_in, query_grad_two)
    xkey_grad = outer_sum(flat_in, gkey_two)
    xvalue_grad = outer_sum(flat_in, gvalue_two)
    grad_flat = (matmul_trans(gkey_two, xkey_mat) + matmul_trans(gvalue_two, xvalue_mat)).astype(
        jnp.bfloat16
    )
    grad_home = lax.all_to_all(
        grad_flat.reshape(data_count, slot_rows, hidden_dim),
        "dp",
        split_axis=0,
        concat_axis=0,
        tiled=True,
    )
    grad_tiles = jnp.einsum("pt,prd->trd", routing, grad_home, preferred_element_type=jnp.float32)
    image_back, tgain_grad, tshift_grad = norm_tile_back(grad_tiles)
    image_grad = image_back.astype(jnp.bfloat16)
    grad_mid_two, xgain_grad, xshift_grad = norm_two_back(matmul_trans(query_grad_two, xquery_mat))
    grad_second = grad_third + grad_mid_two
    branch_one = grad_second.astype(jnp.bfloat16)
    proj_grad = outer_sum(mixed_one, branch_one)
    grad_attend_one = matmul_trans(branch_one, proj_mat).astype(jnp.bfloat16)
    query_grad_one, key_grad_all, value_grad_all = attend_backward(
        query_one, key_all, value_all, causal, max_one, sum_one, grad_attend_one, None
    )
    key_grad_one, value_grad_one = (
        lax.psum_scatter(
            key_grad_all.astype(jnp.bfloat16), "seq", scatter_dimension=0, tiled=True
        ).astype(jnp.float32),
        lax.psum_scatter(
            value_grad_all.astype(jnp.bfloat16), "seq", scatter_dimension=0, tiled=True
        ).astype(jnp.float32),
    )
    gquery_one = query_grad_one.astype(jnp.bfloat16)
    gkey_one = key_grad_one.astype(jnp.bfloat16)
    gvalue_one = value_grad_one.astype(jnp.bfloat16)
    query_grad = outer_sum(first_in, gquery_one)
    key_grad = outer_sum(first_in, gkey_one)
    value_grad = outer_sum(first_in, gvalue_one)
    grad_norm_one = (
        matmul_trans(gquery_one, query_mat)
        + matmul_trans(gkey_one, key_mat)
        + matmul_trans(gvalue_one, value_mat)
    )
    grad_mid_one, sgain_grad, sshift_grad = norm_one_back(grad_norm_one)
    text_grad = (grad_second + grad_mid_one).astype(jnp.bfloat16)[None]
    pieces = (
        lax.all_to_all(
            split_rows(query_grad, data_count, seq_count).astype(jnp.bfloat16),
            "seq",
            split_axis=1,
            concat_axis=1,
            tiled=True,
        ).astype(jnp.float32),
        lax.all_to_all(
            split_rows(key_grad, data_count, seq_count).astype(jnp.bfloat16),
            "seq",
            split_axis=1,
            concat_axis=1,
            tiled=True,
        ).astype(jnp.float32),
        lax.all_to_all(
            split_rows(value_grad, data_count, seq_count).astype(jnp.bfloat16),
            "seq",
            split_axis=1,
            concat_axis=1,
            tiled=True,
        ).astype(jnp.float32),
        lax.all_to_all(
            split_rows(proj_grad, data_count, seq_count).astype(jnp.bfloat16),
            "seq",
            split_axis=1,
            concat_axis=1,
            tiled=True,
        ).astype(jnp.float32),
        lax.all_to_all(
            split_rows(xquery_grad, data_count, seq_count).astype(jnp.bfloat16),
            "seq",
            split_axis=1,
            concat_axis=1,
            tiled=True,
        ).astype(jnp.float32),
        lax.all_to_all(
            split_rows(xkey_grad, data_count, seq_count).astype(jnp.bfloat16),
            "seq",
            split_axis=1,
            concat_axis=1,
            tiled=True,
        ).astype(jnp.float32),
        lax.all_to_all(
            split_rows(xvalue_grad, data_count, seq_count).astype(jnp.bfloat16),
            "seq",
            split_axis=1,
            concat_axis=1,
            tiled=True,
        ).astype(jnp.float32),
        lax.all_to_all(
            split_rows(xproj_grad, data_count, seq_count).astype(jnp.bfloat16),
            "seq",
            split_axis=1,
            concat_axis=1,
            tiled=True,
        ).astype(jnp.float32),
        lax.all_to_all(
            split_rows(up_grad, data_count, seq_count).astype(jnp.bfloat16),
            "seq",
            split_axis=1,
            concat_axis=1,
            tiled=True,
        ).astype(jnp.float32),
        lax.all_to_all(
            split_rows(down_grad, data_count, seq_count).astype(jnp.bfloat16),
            "seq",
            split_axis=1,
            concat_axis=1,
            tiled=True,
        ).astype(jnp.float32),
    )
    folded = [fold_rows(member) for member in pieces]
    summed_mats = (
        lax.psum_scatter(folded[0], "dp", scatter_dimension=0, tiled=True),
        lax.psum_scatter(folded[1], "dp", scatter_dimension=0, tiled=True),
        lax.psum_scatter(folded[2], "dp", scatter_dimension=0, tiled=True),
        lax.psum_scatter(folded[3], "dp", scatter_dimension=0, tiled=True),
        lax.psum_scatter(folded[4], "dp", scatter_dimension=0, tiled=True),
        lax.psum_scatter(folded[5], "dp", scatter_dimension=0, tiled=True),
        lax.psum_scatter(folded[6], "dp", scatter_dimension=0, tiled=True),
        lax.psum_scatter(folded[7], "dp", scatter_dimension=0, tiled=True),
        lax.psum_scatter(folded[8], "dp", scatter_dimension=0, tiled=True),
        lax.psum_scatter(folded[9], "dp", scatter_dimension=0, tiled=True),
    )
    summed_vecs = (
        lax.psum_scatter(upbias_grad, ("dp", "seq"), scatter_dimension=0, tiled=True),
        lax.psum_scatter(downbias_grad, ("dp", "seq"), scatter_dimension=0, tiled=True),
        lax.psum_scatter(sgain_grad, ("dp", "seq"), scatter_dimension=0, tiled=True),
        lax.psum_scatter(sshift_grad, ("dp", "seq"), scatter_dimension=0, tiled=True),
        lax.psum_scatter(xgain_grad, ("dp", "seq"), scatter_dimension=0, tiled=True),
        lax.psum_scatter(xshift_grad, ("dp", "seq"), scatter_dimension=0, tiled=True),
        lax.psum_scatter(tgain_grad, ("dp", "seq"), scatter_dimension=0, tiled=True),
        lax.psum_scatter(tshift_grad, ("dp", "seq"), scatter_dimension=0, tiled=True),
        lax.psum_scatter(mgain_grad, ("dp", "seq"), scatter_dimension=0, tiled=True),
        lax.psum_scatter(mshift_grad, ("dp", "seq"), scatter_dimension=0, tiled=True),
    )
    return (text_out, text_grad, image_grad) + tuple(summed_mats) + tuple(summed_vecs)


def dot_plain(former, latter):
    return jnp.dot(former, latter, preferred_element_type=jnp.float32)


def dot_right(former, latter):
    return lax.dot_general(
        former, latter, (((1,), (1,)), ((), ())), preferred_element_type=jnp.float32
    )


def dot_left(former, latter):
    return lax.dot_general(
        former, latter, (((0,), (0,)), ((), ())), preferred_element_type=jnp.float32
    )


def low(values):
    return values.astype(jnp.bfloat16)


def wide(values):
    return values.astype(jnp.float32)


def block(index, size):
    if isinstance(index, int):
        return pl.ds(index * size, size)
    return pl.ds(pl.multiple_of(index * size, size), size)


def lanes(start, size):
    return pl.ds(start, size)


def norm_parts(values):
    average = jnp.mean(values, axis=-1, keepdims=True)
    centered = values - average
    spread = jnp.mean(centered * centered, axis=-1, keepdims=True)
    inverse = lax.rsqrt(spread + EPSILON)
    return centered * inverse, inverse


def norm_back(unit, inverse, gain_row, grad):
    scaled = grad * gain_row
    first = jnp.mean(scaled, axis=-1, keepdims=True)
    second = jnp.mean(scaled * unit, axis=-1, keepdims=True)
    return (scaled - first - unit * second) * inverse


def column_sum(values):
    return jnp.sum(values, axis=0, keepdims=True)


class Copies:
    def __init__(self, send_sems, recv_sems):
        self.send_sems, self.recv_sems = send_sems, recv_sems
        self.count = 0
        self.started = []

    def make(self, source, target, device):
        index = self.count
        self.count += 1
        return pltpu.make_async_remote_copy(
            src_ref=source,
            dst_ref=target,
            send_sem=self.send_sems.at[index],
            recv_sem=self.recv_sems.at[index],
            device_id=device,
            device_id_type=MESH,
        )

    def begin(self, source, target, device):
        copy = self.make(source, target, device)
        copy.start()
        self.started.append(copy)
        return copy


COPY_SLOTS = 256


def scratch_of(width, tokens, seq_count, data_count, hidden, main, shard):
    length = tokens * seq_count
    band = shard * seq_count
    inbox = data_count * main
    rests = seq_count * data_count
    keys = inbox * seq_count + rests
    bf16, f32 = jnp.bfloat16, jnp.float32
    return dict(
        vec_own=((16, LANES), f32),
        vec_all=((data_count, seq_count, 16, LANES), bf16),
        vec=((16, width), f32),
        up_bias=((1, hidden), f32),
        key_bias=((1, keys), f32),
        slab_out=((seq_count, shard, 1536 + hidden), bf16),
        slab_in=((seq_count, shard, 1536 + hidden), bf16),
        cols=((width, 768 + hidden), bf16),
        halves=((data_count, 2, band // 2, 768), bf16),
        cot_all=((length, width), bf16),
        h1=((length, width), bf16),
        h2=((length, width), bf16),
        h3=((length, width), bf16),
        e1=((length, width), bf16),
        e2=((length, width), bf16),
        out_all=((data_count, shard, 2 * width), bf16),
        out_in=((seq_count, data_count // seq_count, shard, 2 * width), bf16),
        out_rows=((256, 2 * width), bf16),
        down_all=((hidden, width), bf16),
        outbox=((inbox, width), bf16),
        rest_rows=((data_count, width), f32),
        rest_wide=((rests * 16, LANES), f32),
        rest_out=((data_count, 16, LANES), bf16),
        rest_in=((seq_count, data_count, 16, LANES), bf16),
        tiles=((keys, width), bf16),
        kv2=((keys, 512), bf16),
        dkv2=((keys, 512), bf16),
        qm1=((3 * length, LANES), bf16),
        qm2=((3 * length, LANES), bf16),
        dom=((3 * length, LANES), bf16),
        qkv1=((length, 768), bf16),
        p1=((3 * length, length), f32),
        o1=((length, 256), bf16),
        o2=((length, 256), bf16),
        o_acc=((length, 256), f32),
        ds=((3 * length, keys), bf16),
        pr=((3 * length, keys), bf16),
        sums_out=((6, 3, tokens, width), bf16),
        sums_in=((6, 3, tokens, width), bf16),
        x2=((tokens, width), f32),
        x3=((tokens, width), f32),
        dx=((tokens, width), f32),
        act=((length, hidden), bf16),
        slope=((length, hidden), f32),
        du=((length, hidden), bf16),
        dqkv=((length, 768), bf16),
        dq2=((length, 256), bf16),
        dn=((keys, width), bf16),
        dn_pair=((2, inbox, width), bf16),
        dn_far=((inbox, width), bf16),
        dn_home=((inbox, width), bf16),
        dr_out=((seq_count, data_count, 16, LANES), bf16),
        dr_pair=((2, data_count, 16, LANES), bf16),
        dr_far=((data_count, 16, LANES), bf16),
        dr_home=((data_count, 16, LANES), bf16),
        g_cols=((width, 768 + hidden), bf16),
        g_half=((data_count, 2, band // 2, 768), bf16),
        half_in=((data_count, band // 2, 768), bf16),
        g_cross=((width, 256), bf16),
        g_down=((hidden, width), bf16),
        g_out=((data_count, shard, 2 * width), bf16),
        g_out_send=((2, seq_count, data_count // seq_count, shard, width), bf16),
        y_up=((4, band, hidden), bf16),
        z_up=((3, band, hidden), bf16),
        y_down=((4, band, width), bf16),
        z_down=((3, band, width), bf16),
        y_full=((4, band, 768), bf16),
        z_full=((3, band, 768), bf16),
        y_half=((4, band // 2, 768), bf16),
        z_half=((3, band // 2, 768), bf16),
        y_xout=((4, shard, width), bf16),
        z_xout=((3, shard, width), bf16),
        y_sout=((4, shard, width), bf16),
        z_sout=((3, shard, width), bf16),
        cols_out=((seq_count, shard, 768 + hidden), bf16),
        cols_in=((seq_count, shard, 768 + hidden), bf16),
        ends_out=((2, shard, 768), bf16),
        ends_in=((seq_count, shard, 768), bf16),
        vv=((16, width), f32),
        vv_out=((data_count, 16, LANES), f32),
        vv_in=((data_count, 16, LANES), f32),
        vq=((seq_count, 16, LANES), f32),
    )


def lane_pick(parts, lane):
    result = None
    for source, first, place, size in parts:
        start = first // LANES * LANES
        stop = start + LANES * (1 if first + size <= start + LANES else 2)
        window = source[:, start:stop]
        turn = (place - first + start) % (stop - start)
        if turn:
            window = pltpu.roll(window, turn, 1)
        window = window[:, 0:LANES]
        if result is None:
            result = window
        else:
            result = jnp.where((lane >= place) & (lane < place + size), window, result)
    return result


def spans(start, stop, size):
    while start < stop:
        end = min(stop, (start // size + 1) * size)
        yield start, end - start
        start = end


def fused_kernel(names, n_in, *refs):
    (
        slide, owner, text, img, cot, w_query, w_key, w_value, w_out, c_query, c_key, c_value,
        c_out, w_up, w_down, b_up, b_down, *gains,
    ) = refs[:n_in]
    r_text, r_tgrad, r_igrad, r_cols, r_half, r_outs, r_down, r_vec = refs[n_in : n_in + 8]
    m = SimpleNamespace(**dict(zip(names, refs[n_in + 8 :])))
    links = Copies(m.send, m.recv)
    begin = links.begin

    _, tokens, width = text.shape
    seq_count = m.slab_out.shape[0]
    length = tokens * seq_count
    shard = w_out.shape[0]
    data_count = m.vec_all.shape[0]
    hidden = m.down_all.shape[0]
    band = shard * seq_count
    tile_count, real_rows, _ = img.shape
    slides = owner.shape[0]
    main = real_rows // 16 * 16
    inbox = data_count * main
    keys_main = inbox * seq_count
    rests = seq_count * data_count
    keys = keys_main + rests
    columns = width // LANES
    factor = 1.0 / math.sqrt(HEAD)
    z_count = data_count // 2

    d = lax.axis_index("dp")
    s = lax.axis_index("seq")
    z, y = d // 2, d % 2
    core = s % 2
    sibling = s + 1 - 2 * core
    across = (s + 2) % 4
    corner = 3 - s
    seq_peers = [sibling, across, corner]
    z_pair = z + 1 - 2 * (z % 2)
    z_across = (z + 2) % 4
    z_corner = 3 - z
    near = (z * 2 + 1 - y, s)
    beside = (z_pair * 2 + y, s)
    beyond = (z_across * 2 + y, s)

    barrier = pltpu.get_barrier_semaphore()
    for peer in seq_peers:
        pl.semaphore_signal(barrier, inc=1, device_id=(d, peer), device_id_type=MESH)
    for k in range(1, data_count):
        pl.semaphore_signal(
            barrier, inc=1, device_id=((d + k) % data_count, s), device_id_type=MESH
        )

    lane = lax.broadcasted_iota(jnp.int32, (1, LANES), 1)
    head_masks = [
        jnp.where(lane < HEAD, 1.0, 0.0),
        jnp.where(lane >= HEAD, 1.0, 0.0),
        jnp.where(lane // HEAD == core, 1.0, 0.0),
    ]

    def arrive(copies):
        for copy in copies:
            copy.wait_recv()

    def seq_gather(views):
        own = [view(s) for view in views]
        pair = [begin(part, part, (d, sibling)) for part in own]
        far = [begin(part, part, (d, across)) for part in own]
        return views, pair, far

    def seq_pass(state):
        arrive(state[2])
        for part in [view(across) for view in state[0]]:
            state[1].append(begin(part, part, (d, sibling)))

    def seq_end(state):
        arrive(state[1])

    def rows_of(ref):
        return [lambda index: ref.at[block(index, tokens)]]

    def send_all(refs, device):
        return [begin(ref, ref, device) for ref in refs]

    def gather_far(view):
        own = view(d)
        return view, [send_all(own, beyond), send_all(own, beside)], []

    def gather_near(state):
        state[2].extend(send_all(state[0](d), near))

    def gather_step(state, k):
        view, far, close = state
        arrive(far[k])
        part = view((z_across, z_pair, z_corner)[k] * 2 + y)
        if k == 0:
            far.append(send_all(part, beside))
        close.extend(send_all(part, near))

    def gather_end(state):
        arrive(state[2])

    def seq_sum_begin(slot, produce):
        both = low(produce(sibling, corner))
        m.sums_out[slot, 0] = both[0:tokens]
        m.sums_out[slot, 1] = both[tokens : 2 * tokens]
        pair = pl.ds(0, 2)
        copy = begin(m.sums_out.at[slot, pair], m.sums_in.at[slot, pair], (d, sibling))
        both = produce(across, s)
        return slot, copy, both[0:tokens], both[tokens : 2 * tokens]

    def seq_sum_pass(state):
        slot, copy, far, own = state
        copy.wait_recv()
        m.sums_out[slot, 2] = low(far + wide(m.sums_in[slot, 1]))
        return slot, begin(m.sums_out.at[slot, 2], m.sums_in.at[slot, 2], (d, across)), own

    def seq_sum_end(state):
        slot, copy, own = state
        own = own + wide(m.sums_in[slot, 0])
        copy.wait_recv()
        return own + wide(m.sums_in[slot, 2])

    def pick(ref, first, second, place=slice(None)):
        return jnp.concatenate(
            [ref[block(first, tokens), place], ref[block(second, tokens), place]], axis=0
        )

    sum_targets = (z_corner, z_pair, z_across, z)

    def sum_begin(view, y_in, z_in):
        close = [
            [
                begin(part, ref.at[k], near)
                for part, ref in zip(view(target * 2 + 1 - y), y_in, strict=True)
            ]
            for k, target in enumerate(sum_targets)
        ]
        return SimpleNamespace(view=view, y_in=y_in, z_in=z_in, close=close, far=[], own=[])

    def sum_step(state, k):
        arrive(state.close[k])
        if k == 2:
            arrive(state.far[0])
        copies = []
        for index, part in enumerate(state.view(sum_targets[k] * 2 + y)):
            total = wide(part[...]) + wide(state.y_in[index][k])
            if k == 3:
                state.own.append(total)
                continue
            if k == 2:
                total = total + wide(state.z_in[index][0])
            part[...] = low(total)
            target = state.z_in[index].at[k]
            copies.append(begin(part, target, beyond if k == 2 else beside))
        state.far.append(copies)

    def sum_middle(state):
        for k in range(4):
            sum_step(state, k)

    def sum_end(state):
        arrive(state.far[1] + state.far[2])
        return [
            own + wide(ref[1]) + wide(ref[2])
            for own, ref in zip(state.own, state.z_in, strict=True)
        ]

    cross, own = (c_query, c_key, c_value), (w_query, w_key, w_value)
    up_wide = wide(w_up[...])
    slab_out, slab_in = m.slab_out, m.slab_in
    for j in range(seq_count):
        full, half = 3 * (j // 2) + 2 * (j % 2), 3 * (j // 2) + 1
        sources = [(matrix, full) for matrix in cross + own]
        sources += [(matrix, half) for matrix in cross + own]
        for k, (matrix, index) in enumerate(sources):
            place = slice(LANES * k, LANES * k + LANES)
            slab_out[j, :, place] = matrix[:, LANES * index : LANES * index + LANES]
        for tile in range(hidden // LANES):
            pieces = [
                (up_wide, band * (seq_count * (at // band) + j) + at % band, at % LANES, size)
                for at, size in spans(LANES * tile, LANES * tile + LANES, band)
            ]
            slab_out[j, :, 1536 + LANES * tile : 1536 + LANES * (tile + 1)] = low(
                lane_pick(pieces, lane)
            )
    vec_own = m.vec_own
    vec_own[...] = jnp.zeros(vec_own.shape, jnp.float32)
    for k, ref in enumerate((b_down, *gains)):
        vec_own[k : k + 1, 0:shard] = wide(ref[...])
    vec_own[9:10, 0:band] = wide(b_up[...])
    vec_all = m.vec_all
    vec_all[d, s] = low(vec_own[...])
    slab_in[s] = slab_out[s]
    out_all, down_all, cot_all = m.out_all, m.down_all, m.cot_all
    out_all[d, :, 0:width] = w_out[...]
    out_all[d, :, width : 2 * width] = c_out[...]
    down_all[block(d, band)] = w_down[...]
    cot_all[block(s, tokens)] = cot[0]
    m.rest_wide[...] = jnp.zeros(m.rest_wide.shape, jnp.float32)

    def destination(index):
        total = jnp.int32(0)
        for k in range(slides):
            total = total + jnp.where(slide[index] == k, owner[k], 0)
        return total

    own_places = [destination(d * tile_count + t) for t in range(tile_count)]
    route = [
        [jnp.where(place == p, 1.0, 0.0) for place in own_places] for p in range(data_count)
    ]
    spot = lax.broadcasted_iota(jnp.int32, (1, keys), 1)
    slot_of = jnp.where(spot < keys_main, spot % inbox // main, (spot - keys_main) % data_count)
    bias = jnp.zeros((1, keys), jnp.float32)
    for p in range(data_count):
        hits = jnp.int32(0)
        for t in range(tile_count):
            hits = hits + jnp.where(destination(p * tile_count + t) == d, 1, 0)
        bias = jnp.where(slot_of == p, jnp.where(hits > 0, 0.0, MASKED_SCORE), bias)
    m.key_bias[...] = bias
    text_unit, _ = norm_parts(wide(text[0]))

    outbox, tiles = m.outbox, m.tiles
    rest_rows, rest_wide, rest_out, rest_in = m.rest_rows, m.rest_wide, m.rest_out, m.rest_in
    units = [wide(low(norm_parts(wide(img[t]))[0])) for t in range(tile_count)]
    for p in range(data_count):
        total = units[0] * route[p][0]
        for t in range(1, tile_count):
            total = total + units[t] * route[p][t]
        outbox[block(p, main)] = low(total[0:main])
        rest_rows[p : p + 1] = total[main:real_rows]
    for k in range(columns):
        rest_wide[pl.ds(k, data_count, stride=16), :] = rest_rows[:, LANES * k : LANES * (k + 1)]
    rest_out[...] = low(rest_wide[0 : 16 * data_count]).reshape(rest_out.shape)
    own_slot = block(s * data_count + d, main)
    tiles[own_slot] = outbox[block(d, main)]
    rest_in[s, d] = rest_out[d]
    tile_dp = []

    def tile_out(k):
        peer = (d + k) % data_count
        tile_dp.append(begin(outbox.at[block(peer, main)], tiles.at[own_slot], (peer, s)))
        tile_dp.append(begin(rest_out.at[peer], rest_in.at[s, d], (peer, s)))

    pl.semaphore_wait(barrier, seq_count - 1 + data_count - 1)

    own_vec = vec_all.at[d, s]
    vec_dp = [begin(own_vec, own_vec, ((d + k) % data_count, s)) for k in range(1, data_count)]
    slab_seq = [begin(slab_out.at[peer], slab_in.at[s], (d, peer)) for peer in seq_peers]
    for k in (2, 1, 4, 3, 6, 5, 7):
        tile_out(k)
    out_view = lambda index: [out_all.at[index]]
    out_ag = gather_far(out_view)
    gather_near(out_ag)
    arrive(vec_dp)
    vec_column = vec_all.at[:, s]
    vec_seq = [begin(vec_column, vec_column, (d, peer)) for peer in seq_peers]
    arrive(slab_seq)
    cols, halves = m.cols, m.halves
    rows = jnp.concatenate([wide(slab_in[j]) for j in range(seq_count)], axis=0)
    cols[block(d, band), 0:768] = low(rows[:, 0:768])
    cols[block(d, band), 768 : 768 + hidden] = low(rows[:, 1536 : 1536 + hidden])
    rows = rows[:, 768:1536]
    rows = jnp.where(core == 0, rows[0 : band // 2], rows[band // 2 : band])
    halves[d, core] = low(rows)

    def group_view(full, half, first):
        place = lanes(first, 384)
        return lambda index: [
            full.at[block(index, band), place],
            half.at[index, core, :, place],
        ]

    def half_cols(first, size):
        return halves[:, :, :, first : first + size].reshape(width, size)

    def half_swap(first):
        part = halves.at[:, core, :, lanes(first, 384)]
        return begin(part, part, (d, sibling))

    self_view, cross_view = group_view(cols, halves, 384), group_view(cols, halves, 0)
    up_view = lambda index: [cols.at[block(index, band), lanes(768, hidden)]]
    down_view = lambda index: [down_all.at[block(index, band)]]
    self_ag = gather_far(self_view)
    gather_near(self_ag)
    gather_step(out_ag, 0)
    gather_step(out_ag, 1)

    arrive(vec_seq)
    stacked = vec_all[...].reshape(data_count * seq_count * 16, LANES)
    row_of = lax.broadcasted_iota(jnp.int32, (LANES, width), 0)
    col_of = lax.broadcasted_iota(jnp.int32, (LANES, width), 1)
    spread = dot_plain(stacked, jnp.where(row_of == col_of % shard, 1.0, 0.0).astype(jnp.bfloat16))
    spread = spread.reshape(data_count * seq_count, 16, width)
    which = lax.broadcasted_iota(jnp.int32, spread.shape, 0)
    column = lax.broadcasted_iota(jnp.int32, spread.shape, 2)
    vec = m.vec
    vec[...] = jnp.sum(jnp.where(which == column // shard, spread, 0.0), axis=0)

    def vector(index):
        return vec[index : index + 1, :]

    h1, h2, h3, e1, e2 = m.h1, m.h2, m.h3, m.e1, m.e2
    h1[block(s, tokens)] = low(text_unit * vector(1) + vector(2))
    h1_ag = seq_gather(rows_of(h1))

    arrive(tile_dp)
    whole_place = block(s, inbox)
    tiles[whole_place] = low(wide(tiles[whole_place]) * vector(5) + vector(6))
    whole_own = tiles.at[block(s, inbox)]
    tile_pair = [
        begin(whole_own, whole_own, (d, sibling)),
        begin(rest_in.at[s], rest_in.at[s], (d, sibling)),
    ]
    rest_far = begin(rest_in.at[s], rest_in.at[s], (d, across))
    quarter = inbox // 4

    def quarter_of(index, k):
        return tiles.at[pl.ds(pl.multiple_of(index * inbox + k * quarter, quarter), quarter)]

    def tile_send(k):
        part = quarter_of(s, k)
        return begin(part, part, (d, across))

    def tile_pass(k):
        tile_far[k].wait_recv()
        part = quarter_of(across, k)
        tile_pair.append(begin(part, part, (d, sibling)))

    tile_far = [tile_send(k) for k in range(4)]
    gather_step(out_ag, 2)
    gather_step(self_ag, 0)
    gather_step(self_ag, 1)
    seq_pass(h1_ag)
    gather_end(out_ag)
    per_seq = data_count // seq_count
    out_in = m.out_in
    out_seq = []
    for peer in (across, corner, sibling):
        out_seq.append(
            begin(out_all.at[pl.ds(peer * per_seq, per_seq)], out_in.at[s], (d, peer))
        )
    out_in[s] = out_all[pl.ds(s * per_seq, per_seq)]
    cross_ag = gather_far(cross_view)
    gather_near(cross_ag)
    gather_step(self_ag, 2)
    up_ag = gather_far(up_view)
    down_ag = gather_far(down_view)
    gather_end(self_ag)
    half_copy = half_swap(384)
    seq_end(h1_ag)
    qkv1, qm1, p1, o1 = m.qkv1, m.qm1, m.p1, m.o1
    qkv1[:, 0:384] = low(dot_plain(h1[...], cols[:, 384:768]))
    arrive([half_copy])
    qkv1[:, 384:768] = low(dot_plain(h1[...], half_cols(384, 384)))
    gather_step(cross_ag, 0)
    gather_step(cross_ag, 1)
    gather_near(up_ag)
    gather_near(down_ag)

    spot_q = lax.broadcasted_iota(jnp.int32, (length, length), 0)
    spot_k = lax.broadcasted_iota(jnp.int32, (length, length), 1)
    causal = spot_q >= spot_k
    mixed = []
    for head in range(3):
        base = 384 * (head // 2)
        qm = low(wide(qkv1[:, base : base + 128]) * head_masks[head])
        qm1[block(head, length)] = qm
        scores = dot_right(qm, qkv1[:, base + 128 : base + 256]) * factor
        scores = jnp.where(causal, scores, MASKED_SCORE)
        exponent = jnp.exp(scores - jnp.max(scores, axis=1, keepdims=True))
        chances = exponent / jnp.sum(exponent, axis=1, keepdims=True)
        p1[block(head, length)] = chances
        mixed.append(
            dot_plain(low(chances), qkv1[:, base + 256 : base + 384]) * head_masks[head]
        )
    o1[:, 0:128] = low(mixed[0] + mixed[1])
    o1[:, 128:256] = low(mixed[2])

    arrive(out_seq)
    out_rows = m.out_rows
    natural = jnp.concatenate(
        [wide(out_in[j, i]) for i in range(per_seq) for j in range(seq_count)], axis=0
    )
    blank = jnp.zeros((64, 2 * width), jnp.float32)
    even = jnp.concatenate([natural, blank], axis=0)
    odd = jnp.concatenate([natural[64:192], blank, natural[0:64]], axis=0)
    out_rows[...] = low(jnp.where(core == 0, even, odd))

    state = seq_sum_begin(0, lambda i, j: dot_plain(pick(o1, i, j), out_rows[:, 0:width]))
    state = seq_sum_pass(state)
    gather_step(cross_ag, 2)
    x2, x3, dx = m.x2, m.x3, m.dx
    second = wide(text[0]) + seq_sum_end(state)
    x2[...] = second
    unit, _ = norm_parts(second)
    h2[block(s, tokens)] = low(unit * vector(3) + vector(4))
    h2_ag = seq_gather(rows_of(h2))
    cot_ag = seq_gather(rows_of(cot_all))
    gather_step(up_ag, 0)
    gather_step(up_ag, 1)
    row_up = lax.broadcasted_iota(jnp.int32, (LANES, hidden), 0)
    col_up = lax.broadcasted_iota(jnp.int32, (LANES, hidden), 1)
    spread = dot_plain(stacked, jnp.where(row_up == col_up % band, 1.0, 0.0).astype(jnp.bfloat16))
    spread = spread.reshape(data_count * seq_count, 16, hidden)
    which = lax.broadcasted_iota(jnp.int32, spread.shape, 0)
    column = lax.broadcasted_iota(jnp.int32, spread.shape, 2)
    picked = jnp.where(which == (column // band) * seq_count + s, spread, 0.0)
    m.up_bias[...] = jnp.sum(picked, axis=0)[9:10]


    kv2, qm2, pr, o2, o_acc = m.kv2, m.qm2, m.pr, m.o2, m.o_acc

    def keys_values(here):
        rows = tiles[here]
        kv2[here, 0:256] = low(dot_plain(rows, cols[:, 128:384]))
        kv2[here, 256:512] = low(dot_plain(rows, half_cols(128, 256)))

    gather_end(cross_ag)
    half_copy = half_swap(0)
    arrive([half_copy])
    keys_values(block(s, inbox))
    tile_pass(0)
    seq_pass(h2_ag)
    arrive(tile_pair[0:2])
    keys_values(block(sibling, inbox))
    tile_pass(1)
    rest_far.wait_recv()
    tile_pair.append(begin(rest_in.at[across], rest_in.at[across], (d, sibling)))
    gather_step(up_ag, 2)
    gather_step(down_ag, 0)
    seq_end(h2_ag)
    query_full = dot_plain(h2[...], cols[:, 0:128])
    query_half = dot_plain(h2[...], half_cols(0, 128))
    for head in range(3):
        source = query_full if head < 2 else query_half
        qm2[block(head, length)] = low(wide(low(source)) * (head_masks[head] * factor))
    tile_pass(2)
    tile_pass(3)
    keys_values(block(across, inbox))
    arrive(tile_pair[2:])
    keys_values(block(corner, inbox))
    rest_wide[...] = wide(rest_in[...]).reshape(rest_wide.shape)
    for k in range(columns):
        place = slice(LANES * k, LANES * (k + 1))
        tiles[keys_main:keys, place] = low(
            rest_wide[pl.ds(k, rests, stride=16), :] * vec[5:6, place] + vec[6:7, place]
        )
    keys_values(pl.ds(keys_main, rests))
    gather_step(down_ag, 1)
    for head in range(3):
        base = 256 * (head // 2)
        place = 128 * (head // 2)

        here = block(head, length)
        scores = dot_right(qm2[here], kv2[:, base : base + 128]) + m.key_bias[...]
        exponent = jnp.exp(scores - jnp.max(scores, axis=1, keepdims=True))
        chances = low(exponent * (1.0 / jnp.sum(exponent, axis=1, keepdims=True)))
        pr[here] = chances
        result = dot_plain(chances, kv2[:, base + 128 : base + 256]) * head_masks[head]
        if head == 1:
            result = result + o_acc[:, place : place + 128]
        o_acc[:, place : place + 128] = result
        if head == 0:
            gather_step(down_ag, 2)

    o2[...] = low(o_acc[...])
    state = seq_sum_begin(
        1, lambda i, j: dot_plain(pick(o2, i, j), out_rows[:, width : 2 * width])
    )
    state = seq_sum_pass(state)
    third = x2[...] + seq_sum_end(state)
    x3[...] = third
    unit, _ = norm_parts(third)
    h3[block(s, tokens)] = low(unit * vector(7) + vector(8))
    h3_ag = seq_gather(rows_of(h3))
    seq_pass(cot_ag)
    seq_end(cot_ag)
    seq_pass(h3_ag)
    gather_end(down_ag)
    act, slope, du = m.act, m.slope, m.du
    slope[...] = dot_right(cot_all[...], down_all[...])
    gather_end(up_ag)
    seq_end(h3_ag)

    @pl.loop(0, seq_count)
    def _(i):
        here = block(i, tokens)
        pre = dot_plain(h3[here], cols[:, 768 : 768 + hidden]) + m.up_bias[...]
        cdf = 0.5 * (1.0 + lax.erf(pre * (1.0 / math.sqrt(2.0))))
        density = jnp.exp(-0.5 * pre * pre) * (1.0 / math.sqrt(2.0 * math.pi))
        act[here] = low(pre * cdf)
        grad = wide(low(slope[here]))
        du[here] = low(grad * (cdf + pre * density))

    state = seq_sum_begin(
        2, lambda i, j: dot_right(pick(du, i, j), cols[:, 768 : 768 + hidden])
    )
    state = seq_sum_pass(state)
    g_cols, g_down = m.g_cols, m.g_down
    g_down[...] = low(dot_left(act[...], cot_all[...]))
    g_down_view = lambda index: [g_down.at[block(index, band)]]
    down_rs = sum_begin(g_down_view, [m.y_down], [m.z_down])
    grad_mid = seq_sum_end(state)
    unit, inverse = norm_parts(x3[...])
    vv = m.vv
    vv[...] = jnp.zeros(vv.shape, jnp.float32)
    grad_out = wide(cot[0])
    dx3 = grad_out + norm_back(unit, inverse, vector(7), grad_mid)
    dx[...] = dx3
    e2[block(s, tokens)] = low(dx3)
    e2_ag = seq_gather(rows_of(e2))
    vv[0:1] = column_sum(grad_out)
    vv[7:8] = column_sum(grad_mid * unit)
    vv[8:9] = column_sum(grad_mid)
    vv[9:10, 0:hidden] = column_sum(wide(du[...]))

    g_cols[:, 768 : 768 + hidden] = low(dot_left(h3[...], du[...]))
    g_up_view = lambda index: [g_cols.at[block(index, band), lanes(768, hidden)]]
    up_rs = sum_begin(g_up_view, [m.y_up], [m.z_up])
    sum_step(down_rs, 0)
    seq_pass(e2_ag)
    sum_step(down_rs, 1)
    seq_end(e2_ag)

    dom = m.dom
    grad_o = low(dot_right(e2[...], out_rows[:, width : 2 * width]))
    for head in range(3):
        place = 128 * (head // 2)
        dom[block(head, length)] = low(wide(grad_o[:, place : place + 128]) * head_masks[head])
    ds, dkv2, dq2 = m.ds, m.dkv2, m.dq2
    for head in range(3):
        base = 256 * (head // 2)
        place = 128 * (head // 2)

        here = block(head, length)
        chances = wide(pr[here])
        grad_p = dot_right(dom[here], kv2[:, base + 128 : base + 256])
        weighted = jnp.sum(chances * grad_p, axis=1, keepdims=True)
        grad_s = low(chances * (grad_p - weighted))
        ds[here] = grad_s
        result = dot_plain(grad_s, kv2[:, base : base + 128]) * (head_masks[head] * factor)
        if head == 1:
            result = result + o_acc[:, place : place + 128]
        o_acc[:, place : place + 128] = result
        if head < 2:
            sum_step(down_rs, 2 + head)

    dq2[...] = low(o_acc[...])
    sum_step(up_rs, 0)
    state = seq_sum_begin(
        4,
        lambda i, j: dot_right(pick(dq2, i, j, slice(0, 128)), cols[:, 0:128])
        + dot_right(pick(dq2, i, j, slice(128, 256)), half_cols(0, 128)),
    )

    g_out, g_out_send = m.g_out, m.g_out_send

    def out_grad(slot, value):
        odd = jnp.concatenate([value[192:256], value[0:128]], axis=0)
        natural = jnp.where(core == 0, value[0:192], odd)
        for i in range(per_seq):
            for j in range(seq_count):
                start = shard * (i * seq_count + j)
                g_out_send[slot, j, i] = low(natural[start : start + shard])
        target = g_out.at[pl.ds(s * per_seq, per_seq), :, lanes(slot * width, width)]
        copies = [begin(g_out_send.at[slot, peer], target, (d, peer)) for peer in seq_peers]
        g_out[pl.ds(s * per_seq, per_seq), :, slot * width : (slot + 1) * width] = g_out_send[
            slot, s
        ]
        return copies

    xout_seq = out_grad(1, dot_left(o2[...], e2[...]))
    state = seq_sum_pass(state)
    for tile in range(2):
        first, count = (0, 2 * length) if tile == 0 else (2 * length, length)
        base = 256 * tile
        for start, size in spans(0, keys, 512):
            cut = slice(start, start + size)
            dkv2[cut, base : base + 128] = low(
                dot_left(ds[first : first + count, cut], qm2[first : first + count])
            )
            dkv2[cut, base + 128 : base + 256] = low(
                dot_left(pr[first : first + count, cut], dom[first : first + count])
            )
    sum_step(up_rs, 1)
    second_grad = seq_sum_end(state)
    unit, inverse = norm_parts(x2[...])
    dx2 = dx[...] + norm_back(unit, inverse, vector(3), second_grad)
    dx[...] = dx2
    e1[block(s, tokens)] = low(dx2)
    e1_ag = seq_gather(rows_of(e1))
    vv[3:4] = column_sum(second_grad * unit)
    vv[4:5] = column_sum(second_grad)
    sum_step(up_rs, 2)
    arrive(xout_seq)
    xout_view = lambda index: [g_out.at[index, :, lanes(width, width)]]
    xout_rs = sum_begin(xout_view, [m.y_xout], [m.z_xout])

    dn = m.dn

    def tile_grads(here):
        dn[here] = low(
            dot_right(dkv2[here, 0:256], cols[:, 128:384])
            + dot_right(dkv2[here, 256:512], half_cols(128, 256))
        )

    dr_out, dr_pair, dr_far, dr_home = m.dr_out, m.dr_pair, m.dr_far, m.dr_home
    dn_pair, dn_far, dn_home = m.dn_pair, m.dn_far, m.dn_home
    tile_grads(block(corner, inbox))
    pair_far = begin(dn.at[block(corner, inbox)], dn_pair.at[1], (d, sibling))
    tile_grads(pl.ds(keys_main, rests))
    rest_wide[...] = jnp.zeros(rest_wide.shape, jnp.float32)
    for k in range(columns):
        rest_wide[pl.ds(k, rests, stride=16), :] = wide(
            dn[keys_main:keys, LANES * k : LANES * (k + 1)]
        )
    dr_out[...] = low(rest_wide[...]).reshape(dr_out.shape)
    rest_pair = [
        begin(dr_out.at[peer], dr_pair.at[k], (d, sibling))
        for k, peer in enumerate((sibling, corner))
    ]
    tile_grads(block(across, inbox))
    seq_pass(e1_ag)
    pair_far.wait_recv()
    fold = dn.at[block(across, inbox)]
    fold[...] = low(wide(fold[...]) + wide(dn_pair[1]))
    arrive(rest_pair)
    dr_out[across] = low(wide(dr_out[across]) + wide(dr_pair[1]))
    rest_far = begin(dr_out.at[across], dr_far, (d, across))

    def far_send(k):
        return begin(quarter_in(dn, across, k), dn_far.at[block(k, quarter)], (d, across))

    def quarter_in(ref, index, k):
        return ref.at[pl.ds(pl.multiple_of(index * inbox + k * quarter, quarter), quarter)]

    far_copies = [far_send(k) for k in range(4)]
    sum_step(up_rs, 3)
    g_half, half_in, g_cross = m.g_half, m.half_in, m.g_cross
    half_shape = (data_count, 2, band // 2)

    def half_send(first):
        place = lanes(first, 384)
        return begin(g_half.at[:, 1 - core, :, place], half_in.at[:, :, place], (d, sibling))

    def half_add(first, copy):
        copy.wait_recv()
        place = lanes(first, 384)
        g_half[:, core, :, place] = low(
            wide(g_half[:, core, :, place]) + wide(half_in[:, :, place])
        )

    seq_end(e1_ag)
    grad_o = low(dot_right(e1[...], out_rows[:, 0:width]))
    grads = []
    dqkv = m.dqkv
    for head in range(3):
        base = 384 * (head // 2)
        place = 128 * (head // 2)
        here = block(head, length)
        dm = low(wide(grad_o[:, place : place + 128]) * head_masks[head])
        chances = p1[here]
        grad_p = dot_right(dm, qkv1[:, base + 256 : base + 384])
        weighted = jnp.sum(chances * grad_p, axis=1, keepdims=True)
        grad_s = low(chances * (grad_p - weighted))
        grads.append(
            (
                dot_plain(grad_s, qkv1[:, base + 128 : base + 256]) * (head_masks[head] * factor),
                dot_left(grad_s, qm1[here]) * factor,
                dot_left(low(chances), dm),
            )
        )
    for k in range(3):
        dqkv[:, 128 * k : 128 * k + 128] = low(grads[0][k] + grads[1][k])
        dqkv[:, 384 + 128 * k : 512 + 128 * k] = low(grads[2][k])
    state = seq_sum_begin(
        5,
        lambda i, j: dot_right(pick(dqkv, i, j, slice(0, 384)), cols[:, 384:768])
        + dot_right(pick(dqkv, i, j, slice(384, 768)), half_cols(384, 384)),
    )

    grad = dot_left(h1[...], dqkv[...])
    g_cols[:, 384:768] = low(grad[:, 0:384])
    g_half[:, :, :, 384:768] = low(grad[:, 384:768]).reshape(*half_shape, 384)
    half_copy = half_send(384)
    state = seq_sum_pass(state)
    sout_seq = out_grad(0, dot_left(o1[...], e1[...]))
    half_add(384, half_copy)
    self_rs = sum_begin(
        group_view(g_cols, g_half, 384),
        [m.y_full.at[:, :, lanes(384, 384)], m.y_half.at[:, :, lanes(384, 384)]],
        [m.z_full.at[:, :, lanes(384, 384)], m.z_half.at[:, :, lanes(384, 384)]],
    )
    out_state = seq_sum_begin(3, lambda i, j: dot_plain(pick(act, i, j), down_all[...]))
    tile_grads(block(sibling, inbox))
    pair_own = begin(dn.at[block(sibling, inbox)], dn_pair.at[0], (d, sibling))
    tile_grads(block(s, inbox))

    sum_middle(xout_rs)
    out_state = seq_sum_pass(out_state)
    grad = dot_left(h2[...], dq2[...])
    g_cols[:, 0:128] = low(grad[:, 0:128])
    g_half[:, :, :, 0:128] = low(grad[:, 128:256]).reshape(*half_shape, 128)
    for cut in range(3):
        span = slice(256 * cut, 256 * cut + 256)
        grad = dot_left(tiles[:, span], dkv2[...])
        g_cols[span, 128:384] = low(grad[:, 0:256])
        g_cross[span] = low(grad[:, 256:512])
    g_half[:, :, :, 128:384] = g_cross[...].reshape(*half_shape, 256)
    half_copy = half_send(0)
    sum_step(self_rs, 0)
    half_add(0, half_copy)
    cross_rs = sum_begin(
        group_view(g_cols, g_half, 0),
        [m.y_full.at[:, :, lanes(0, 384)], m.y_half.at[:, :, lanes(0, 384)]],
        [m.z_full.at[:, :, lanes(0, 384)], m.z_half.at[:, :, lanes(0, 384)]],
    )
    sum_step(self_rs, 1)
    arrive(sout_seq)
    sout_view = lambda index: [g_out.at[index, :, lanes(0, width)]]
    sout_rs = sum_begin(sout_view, [m.y_sout], [m.z_sout])
    sum_step(self_rs, 2)
    sum_step(self_rs, 3)
    sum_step(cross_rs, 0)
    sum_step(cross_rs, 1)
    first_grad = seq_sum_end(state)
    unit, inverse = norm_parts(wide(text[0]))
    vv[1:2] = column_sum(first_grad * unit)
    vv[2:3] = column_sum(first_grad)
    r_tgrad[...] = low(dx[...] + norm_back(unit, inverse, vector(1), first_grad))
    arrive([pair_own, rest_far])
    dr_out[s] = low(wide(dr_out[s]) + wide(dr_pair[0]) + wide(dr_far[...]))

    home_dp = []
    own_home = block(d, main)
    for k in range(4):
        far_copies[k].wait_recv()
        mine = quarter_in(dn, s, k)
        there = block(k, quarter)
        mine[...] = low(wide(mine[...]) + wide(dn_pair[0, there]) + wide(dn_far[there]))

    def home_send(k):
        peer = (d + k) % data_count
        source = dn.at[block(s * data_count + peer, main)]
        home_dp.append(begin(source, dn_home.at[own_home], (peer, s)))
        home_dp.append(begin(dr_out.at[s, peer], dr_home.at[d], (peer, s)))

    for k in (2, 1, 4, 3, 6, 5, 7):
        home_send(k)
    dn_home[own_home] = dn[block(s * data_count + d, main)]
    dr_home[d] = dr_out[s, d]
    sum_step(cross_rs, 2)
    sum_step(cross_rs, 3)
    sum_middle(sout_rs)
    r_text[...] = low(x3[...] + seq_sum_end(out_state) + vector(0))

    cols_out, cols_in, ends_out, ends_in = m.cols_out, m.cols_in, m.ends_out, m.ends_in

    def finish_cols(first, size, total):
        place = lanes(first, size)
        for j in range(seq_count):
            cols_out[j, :, place] = low(total[shard * j : shard * (j + 1)])
        cols_in[s, :, place] = cols_out[s, :, place]
        return [
            begin(cols_out.at[peer, :, place], cols_in.at[s, :, place], (d, peer))
            for peer in seq_peers
        ]

    def finish_half(first, total):
        place = lanes(first, 384)
        for j in range(2):
            ends_out[j, :, place] = low(total[shard * j : shard * (j + 1)])
        ends_in[s, :, place] = ends_out[core, :, place]
        return [
            begin(ends_out.at[peer % 2, :, place], ends_in.at[s, :, place], (d, peer))
            for peer in seq_peers
        ]

    (r_down[...],) = sum_end(down_rs)
    ends = finish_cols(768, hidden, sum_end(up_rs)[0])
    (r_outs[1],) = sum_end(xout_rs)
    full, half = sum_end(self_rs)
    ends += finish_cols(384, 384, full) + finish_half(384, half)

    arrive(home_dp)
    gain_sum = jnp.zeros((1, width), jnp.float32)
    shift_sum = jnp.zeros((1, width), jnp.float32)
    for t in range(tile_count):
        grad = wide(dn_home[block(0, main)]) * route[0][t]
        rest = wide(dr_home[0]) * route[0][t]
        for p in range(1, data_count):
            grad = grad + wide(dn_home[block(p, main)]) * route[p][t]
            rest = rest + wide(dr_home[p]) * route[p][t]
        rest = jnp.concatenate([rest[k : k + 1] for k in range(columns)], axis=1)
        unit, inverse = norm_parts(wide(img[t, 0:main]))
        gain_sum = gain_sum + column_sum(grad * unit)
        shift_sum = shift_sum + column_sum(grad)
        r_igrad[t, 0:main] = low(norm_back(unit, inverse, vector(5), grad))
        unit, inverse = norm_parts(wide(img[t, main:real_rows]))
        gain_sum = gain_sum + rest * unit
        shift_sum = shift_sum + rest
        r_igrad[t, main:real_rows] = low(norm_back(unit, inverse, vector(5), rest))
    vv[5:6] = gain_sum
    vv[6:7] = shift_sum

    vv_out, vv_in, vq = m.vv_out, m.vv_in, m.vq
    everything = vv[...]
    for p in range(data_count):
        turned = everything if p == 0 else pltpu.roll(everything, width - band * p, 1)
        vv_out[p] = turned[:, 0:LANES]
    vv_dp = []
    for k in range(1, data_count):
        peer = (d + k) % data_count
        vv_dp.append(begin(vv_out.at[peer], vv_in.at[d], (peer, s)))
    vv_in[d] = vv_out[d]

    full, half = sum_end(cross_rs)
    ends += finish_cols(0, 384, full) + finish_half(0, half)
    (r_outs[0],) = sum_end(sout_rs)

    arrive(vv_dp)
    total = vv_in[0]
    for p in range(1, data_count):
        total = total + vv_in[p]
    vq[s] = total
    vq_seq = [begin(vq.at[s], vq.at[s], (d, peer)) for peer in seq_peers]
    bias_grad = total[9:10]

    arrive(ends)
    r_cols[...] = cols_in[...]
    r_half[...] = ends_in[...]
    arrive(vq_seq)
    total = vq[0] + vq[1] + vq[2] + vq[3]
    r_vec[...] = pltpu.roll(total, (LANES - shard * s) % LANES, 1)
    r_vec[9:10] = bias_grad

    for copy in links.started:
        copy.wait_send()


def unpack_kernel(t_out, t_grad, i_grad, cols, ends, outs, down, vec, *results):
    o_text, o_tgrad, o_igrad, o_q, o_k, o_v, o_o, o_xq, o_xk, o_xv, o_xo, o_up, o_down, *vectors = (
        results
    )
    seq_count, shard, total = cols.shape
    hidden = total - 768
    core = lax.axis_index("seq") // 2
    band = down.shape[0]
    o_text[0] = t_out[...]
    o_tgrad[0] = t_grad[...]
    o_igrad[...] = i_grad[...]
    for k, result in enumerate((o_xq, o_xk, o_xv, o_q, o_k, o_v)):
        here = slice(LANES * k, LANES * (k + 1))
        for j, tile in ((0, 0), (1, 2), (2, 3), (3, 5)):
            result[:, LANES * tile : LANES * (tile + 1)] = wide(cols[j, :, here])
        for j, tile in ((0, 1), (2, 4)):
            result[:, LANES * tile : LANES * (tile + 1)] = wide(ends[j + core, :, here])
    o_o[...] = outs[0]
    o_xo[...] = outs[1]
    o_down[...] = down[...]
    lane = lax.broadcasted_iota(jnp.int32, (1, LANES), 1)
    parts = [wide(cols[j, :, 768:total]) for j in range(seq_count)]
    for tile in range(hidden * seq_count // LANES):
        pieces = []
        for at, size in spans(LANES * tile, LANES * tile + LANES, band):
            group = at // band
            first = band * (group // seq_count) + at % band
            pieces.append((parts[group % seq_count], first, at % LANES, size))
        o_up[:, LANES * tile : LANES * (tile + 1)] = lane_pick(pieces, lane)
    vectors[0][...] = vec[9, 0:band]
    for k, result in enumerate(vectors[1:]):
        result[...] = vec[k, 0:shard]


def fused_device(
    text_in, image_in, tile_slide, owner_map, text_cot,
    w_query, w_key, w_value, w_out, c_query, c_key, c_value, c_out, w_up, w_down, b_up, b_down,
    self_gain, self_shift, cross_gain, cross_shift, tile_gain, tile_shift, mlp_gain, mlp_shift,
):
    data_count, seq_count = lax.axis_size("dp"), lax.axis_size("seq")
    tile_count, real_rows, width = image_in.shape
    tokens = text_in.shape[1]
    shard = w_query.shape[0]
    band = shard * seq_count
    hidden = w_up.shape[1] // seq_count
    main = real_rows // 16 * 16

    gains = (
        self_gain, self_shift, cross_gain, cross_shift, tile_gain, tile_shift, mlp_gain, mlp_shift,
    )
    inputs = (
        tile_slide, owner_map, text_in, image_in, text_cot, w_query, w_key, w_value, w_out,
        c_query, c_key, c_value, c_out, w_up, w_down,
        *[member.reshape(1, -1) for member in (b_up, b_down, *gains)],
    )
    in_specs = [pl.BlockSpec(memory_space=pltpu.SMEM)] * 2
    in_specs += [pl.BlockSpec(memory_space=pltpu.VMEM)] * (len(inputs) - 2)
    row_out = jax.ShapeDtypeStruct((tokens, width), jnp.bfloat16)
    packed_shape = [
        row_out,
        row_out,
        jax.ShapeDtypeStruct(image_in.shape, jnp.bfloat16),
        jax.ShapeDtypeStruct((seq_count, shard, 768 + hidden), jnp.bfloat16),
        jax.ShapeDtypeStruct((seq_count, shard, 768), jnp.bfloat16),
        jax.ShapeDtypeStruct((2, shard, width), jnp.float32),
        jax.ShapeDtypeStruct((band, width), jnp.float32),
        jax.ShapeDtypeStruct((16, LANES), jnp.float32),
    ]
    shapes = scratch_of(width, tokens, seq_count, data_count, hidden, main, shard)
    scratch = [pltpu.VMEM(shape, kind) for shape, kind in shapes.values()]
    scratch += [pltpu.SemaphoreType.DMA((COPY_SLOTS,))] * 2
    names = [*shapes, "send", "recv"]
    packed = pl.pallas_call(
        partial(fused_kernel, names, len(inputs)),
        out_shape=packed_shape,
        in_specs=in_specs,
        out_specs=[pl.BlockSpec(memory_space=pltpu.VMEM)] * len(packed_shape),
        scratch_shapes=scratch,
        compiler_params=pltpu.CompilerParams(
            collective_id=0, has_side_effects=True, vmem_limit_bytes=60 * 1024 * 1024
        ),
        name="decoder_layer",
    )(*inputs)
    square = jax.ShapeDtypeStruct((shard, width), jnp.float32)
    out_shape = [
        jax.ShapeDtypeStruct(text_in.shape, jnp.bfloat16),
        jax.ShapeDtypeStruct(text_in.shape, jnp.bfloat16),
        jax.ShapeDtypeStruct(image_in.shape, jnp.bfloat16),
        *[square] * 8,
        jax.ShapeDtypeStruct((shard, hidden * seq_count), jnp.float32),
        jax.ShapeDtypeStruct((band, width), jnp.float32),
        jax.ShapeDtypeStruct((band,), jnp.float32),
        *[jax.ShapeDtypeStruct((shard,), jnp.float32)] * 9,
    ]
    return tuple(
        pl.pallas_call(
            unpack_kernel,
            out_shape=out_shape,
            in_specs=[pl.BlockSpec(memory_space=pltpu.VMEM)] * len(packed),
            out_specs=[pl.BlockSpec(memory_space=pltpu.VMEM)] * len(out_shape),
            name="unpack",
        )(*packed)
    )


def fused_fits(mesh):
    return mesh.shape["seq"] == 4 and 768 % (8 * mesh.shape["dp"] * mesh.shape["seq"]) == 0


def solution(mesh):
    placed = (
        P("dp", "seq", None),
        P("dp", "seq", None),
        P(),
        P(),
        P("dp", "seq", None),
        P(("dp", "seq"), None),
        P(("dp", "seq"), None),
        P(("dp", "seq"), None),
        P(("dp", "seq"), None),
        P(("dp", "seq"), None),
        P(("dp", "seq"), None),
        P(("dp", "seq"), None),
        P(("dp", "seq"), None),
        P(("dp", "seq"), None),
        P(("dp", "seq"), None),
        P(("dp", "seq")),
        P(("dp", "seq")),
        P(("dp", "seq")),
        P(("dp", "seq")),
        P(("dp", "seq")),
        P(("dp", "seq")),
        P(("dp", "seq")),
        P(("dp", "seq")),
        P(("dp", "seq")),
        P(("dp", "seq")),
    )
    return jax.shard_map(
        fused_device if fused_fits(mesh) else per_device,
        mesh=mesh,
        in_specs=placed,
        out_specs=(
            P("dp", "seq", None),
            P("dp", "seq", None),
            P("dp", "seq", None),
            P(("dp", "seq"), None),
            P(("dp", "seq"), None),
            P(("dp", "seq"), None),
            P(("dp", "seq"), None),
            P(("dp", "seq"), None),
            P(("dp", "seq"), None),
            P(("dp", "seq"), None),
            P(("dp", "seq"), None),
            P(("dp", "seq"), None),
            P(("dp", "seq"), None),
            P(("dp", "seq")),
            P(("dp", "seq")),
            P(("dp", "seq")),
            P(("dp", "seq")),
            P(("dp", "seq")),
            P(("dp", "seq")),
            P(("dp", "seq")),
            P(("dp", "seq")),
            P(("dp", "seq")),
            P(("dp", "seq")),
        ),
        check_vma=False,
    )
```

```python
from functools import partial
import math
from types import SimpleNamespace

import jax
import jax.numpy as jnp
from jax import lax
from jax.experimental import pallas as pl
from jax.experimental.pallas import tpu as pltpu
from jax.sharding import PartitionSpec as P

HEAD = 64
LANES = 128
MESH = pl.DeviceIdType.MESH


EPSILON = 1e-05
MASKED_SCORE = -1e30


def combined_all(x, axis, combine):
    everything = jax.tree.map(lambda part: lax.all_gather(part, axis), x)
    initial = jax.tree.map(lambda part: part[0], everything)

    def step(k, so_far):
        return combine(so_far, jax.tree.map(lambda part: part[k], everything))

    return lax.fori_loop(1, lax.axis_size(axis), step, initial)


def norm_rows(values, gain_row, shift_row):
    average = jnp.mean(values, axis=-1, keepdims=True)
    centered = values - average
    spread = jnp.mean(centered * centered, axis=-1, keepdims=True)
    return centered * lax.rsqrt(spread + EPSILON) * gain_row + shift_row


def matmul(former, latter):
    return jnp.dot(former, latter, preferred_element_type=jnp.float32)


def matmul_trans(former, latter):
    return lax.dot_general(
        former, latter, (((1,), (1,)), ((), ())), preferred_element_type=jnp.float32
    )


def outer_sum(former, latter):
    return lax.dot_general(
        former, latter, (((0,), (0,)), ((), ())), preferred_element_type=jnp.float32
    )


def head_pair(matrix, pair_index):
    columns = lax.dynamic_slice_in_dim(matrix, pair_index * 2 * HEAD, 2 * HEAD, 1)
    return columns.reshape(columns.shape[0], 2, HEAD)


def put_pair(matrix, update, pair_index):
    return lax.dynamic_update_slice_in_dim(
        matrix, update.reshape(update.shape[0], 2 * HEAD), pair_index * 2 * HEAD, 1
    )


def pick_pair(stacked, pair_index):
    return lax.dynamic_index_in_dim(stacked, pair_index, 0, keepdims=False)


def pair_scores(query_rows, key_rows, allowed, pair_index):
    factor = 1.0 / math.sqrt(HEAD)
    scores = (
        jnp.einsum(
            "qhd,khd->hqk",
            head_pair(query_rows, pair_index),
            head_pair(key_rows, pair_index),
            preferred_element_type=jnp.float32,
        )
        * factor
    )
    return jnp.where(allowed[None], scores, MASKED_SCORE)


def attend_stats(query_rows, key_rows, allowed):
    pair_count = query_rows.shape[1] // (2 * HEAD)

    def one_pair(pair_index, state_now):
        row_max, row_sum = state_now
        scores = pair_scores(query_rows, key_rows, allowed, pair_index)
        highest = jnp.max(scores, axis=2)
        summed = jnp.sum(jnp.exp(scores - highest[..., None]), axis=2)
        return (
            lax.dynamic_update_index_in_dim(row_max, highest, pair_index, 0),
            lax.dynamic_update_index_in_dim(row_sum, summed, pair_index, 0),
        )

    empty_stats = jnp.zeros((pair_count, 2, query_rows.shape[0]), jnp.float32)
    return lax.fori_loop(0, pair_count, one_pair, (empty_stats, empty_stats))


def attend_forward(query_rows, key_rows, value_rows, allowed, maxima, totals):
    pair_count = query_rows.shape[1] // (2 * HEAD)
    stats_given = maxima is not None
    if not stats_given:
        maxima = jnp.zeros((pair_count, 2, query_rows.shape[0]), jnp.float32)
        totals = jnp.zeros_like(maxima)

    def one_pair(pair_index, state_now):
        output, row_max, row_sum = state_now
        scores = pair_scores(query_rows, key_rows, allowed, pair_index)
        if stats_given:
            highest = pick_pair(row_max, pair_index)
            exponent = jnp.exp(scores - highest[..., None])
            summed = pick_pair(row_sum, pair_index)
        else:
            highest = jnp.max(scores, axis=2)
            exponent = jnp.exp(scores - highest[..., None])
            summed = jnp.sum(exponent, axis=2)
            row_max = lax.dynamic_update_index_in_dim(row_max, highest, pair_index, 0)
            row_sum = lax.dynamic_update_index_in_dim(row_sum, summed, pair_index, 0)
        weights = (exponent / summed[..., None]).astype(jnp.bfloat16)
        mixture = jnp.einsum(
            "hqk,khd->qhd",
            weights,
            head_pair(value_rows, pair_index),
            preferred_element_type=jnp.float32,
        )
        return (put_pair(output, mixture, pair_index), row_max, row_sum)

    start_state = (jnp.zeros(query_rows.shape, jnp.float32), maxima, totals)
    return lax.fori_loop(0, pair_count, one_pair, start_state)


def attend_rowsums(query_rows, key_rows, value_rows, allowed, maxima, totals, grad_rows):
    pair_count = query_rows.shape[1] // (2 * HEAD)

    def one_pair(pair_index, row_terms):
        scores = pair_scores(query_rows, key_rows, allowed, pair_index)
        chances = (
            jnp.exp(scores - pick_pair(maxima, pair_index)[..., None])
            / pick_pair(totals, pair_index)[..., None]
        )
        grad_chances = jnp.einsum(
            "qhd,khd->hqk",
            head_pair(grad_rows, pair_index),
            head_pair(value_rows, pair_index),
            preferred_element_type=jnp.float32,
        )
        return lax.dynamic_update_index_in_dim(
            row_terms, jnp.sum(chances * grad_chances, axis=2), pair_index, 0
        )

    return lax.fori_loop(0, pair_count, one_pair, jnp.zeros_like(maxima))


def attend_backward(
    query_rows, key_rows, value_rows, allowed, maxima, totals, grad_rows, row_terms
):
    pair_count = query_rows.shape[1] // (2 * HEAD)
    factor = 1.0 / math.sqrt(HEAD)

    def one_pair(pair_index, state_now):
        grad_query, grad_key, grad_value = state_now
        scores = pair_scores(query_rows, key_rows, allowed, pair_index)
        chances = (
            jnp.exp(scores - pick_pair(maxima, pair_index)[..., None])
            / pick_pair(totals, pair_index)[..., None]
        )
        grad_heads = head_pair(grad_rows, pair_index)
        grad_chances = jnp.einsum(
            "qhd,khd->hqk",
            grad_heads,
            head_pair(value_rows, pair_index),
            preferred_element_type=jnp.float32,
        )
        if row_terms is None:
            weighted = jnp.sum(chances * grad_chances, axis=2)
        else:
            weighted = pick_pair(row_terms, pair_index)
        grad_scores = (chances * (grad_chances - weighted[..., None])).astype(jnp.bfloat16)
        query_part = (
            jnp.einsum(
                "hqk,khd->qhd",
                grad_scores,
                head_pair(key_rows, pair_index),
                preferred_element_type=jnp.float32,
            )
            * factor
        )
        key_part = (
            jnp.einsum(
                "hqk,qhd->khd",
                grad_scores,
                head_pair(query_rows, pair_index),
                preferred_element_type=jnp.float32,
            )
            * factor
        )
        value_part = jnp.einsum(
            "hqk,qhd->khd",
            chances.astype(jnp.bfloat16),
            grad_heads,
            preferred_element_type=jnp.float32,
        )
        return (
            put_pair(grad_query, query_part, pair_index),
            put_pair(grad_key, key_part, pair_index),
            put_pair(grad_value, value_part, pair_index),
        )

    start_state = (
        jnp.zeros(query_rows.shape, jnp.float32),
        jnp.zeros(key_rows.shape, jnp.float32),
        jnp.zeros(value_rows.shape, jnp.float32),
    )
    return lax.fori_loop(0, pair_count, one_pair, start_state)


def join_stats(former, latter):
    highest = jnp.maximum(former[0], latter[0])
    return (
        highest,
        former[1] * jnp.exp(former[0] - highest) + latter[1] * jnp.exp(latter[0] - highest),
    )


def split_rows(matrix, data_count, seq_count):
    return matrix.reshape(
        data_count, seq_count, matrix.shape[0] // (data_count * seq_count), matrix.shape[1]
    )


def fold_rows(pieces):
    return jnp.sum(pieces, axis=1).reshape(pieces.shape[0] * pieces.shape[2], pieces.shape[3])


def per_device(
    text_in,
    image_in,
    tile_slide,
    owner_map,
    text_cot,
    w_query,
    w_key,
    w_value,
    w_out,
    c_query,
    c_key,
    c_value,
    c_out,
    w_up,
    w_down,
    b_up,
    b_down,
    self_gain,
    self_shift,
    cross_gain,
    cross_shift,
    tile_gain,
    tile_shift,
    mlp_gain,
    mlp_shift,
):
    gathered = (
        lax.all_gather(w_query, ("dp", "seq"), axis=0, tiled=True),
        lax.all_gather(w_key, ("dp", "seq"), axis=0, tiled=True),
        lax.all_gather(w_value, ("dp", "seq"), axis=0, tiled=True),
        lax.all_gather(w_out, ("dp", "seq"), axis=0, tiled=True),
        lax.all_gather(c_query, ("dp", "seq"), axis=0, tiled=True),
        lax.all_gather(c_key, ("dp", "seq"), axis=0, tiled=True),
        lax.all_gather(c_value, ("dp", "seq"), axis=0, tiled=True),
        lax.all_gather(c_out, ("dp", "seq"), axis=0, tiled=True),
        lax.all_gather(w_up, ("dp", "seq"), axis=0, tiled=True),
        lax.all_gather(w_down, ("dp", "seq"), axis=0, tiled=True),
        lax.all_gather(b_up, ("dp", "seq"), axis=0, tiled=True),
        lax.all_gather(b_down, ("dp", "seq"), axis=0, tiled=True),
        lax.all_gather(self_gain, ("dp", "seq"), axis=0, tiled=True),
        lax.all_gather(self_shift, ("dp", "seq"), axis=0, tiled=True),
        lax.all_gather(cross_gain, ("dp", "seq"), axis=0, tiled=True),
        lax.all_gather(cross_shift, ("dp", "seq"), axis=0, tiled=True),
        lax.all_gather(tile_gain, ("dp", "seq"), axis=0, tiled=True),
        lax.all_gather(tile_shift, ("dp", "seq"), axis=0, tiled=True),
        lax.all_gather(mlp_gain, ("dp", "seq"), axis=0, tiled=True),
        lax.all_gather(mlp_shift, ("dp", "seq"), axis=0, tiled=True),
    )
    query_mat, key_mat, value_mat, proj_mat = (gathered[0], gathered[1], gathered[2], gathered[3])
    xquery_mat, xkey_mat, xvalue_mat, xproj_mat = (
        gathered[4],
        gathered[5],
        gathered[6],
        gathered[7],
    )
    up_mat, down_mat = (gathered[8], gathered[9])
    vectors = [member.astype(jnp.float32) for member in gathered[10:]]
    (
        up_bias,
        down_bias,
        gain_one,
        shift_one,
        gain_two,
        shift_two,
        gain_tile,
        shift_tile,
        gain_three,
        shift_three,
    ) = vectors
    text_rows = text_in[0].astype(jnp.float32)
    rows_here = text_rows.shape[0]
    hidden_dim = text_rows.shape[1]
    normed_one, norm_one_back = jax.vjp(norm_rows, text_rows, gain_one, shift_one)
    first_in = normed_one.astype(jnp.bfloat16)
    query_one = matmul(first_in, query_mat).astype(jnp.bfloat16)
    key_one = matmul(first_in, key_mat).astype(jnp.bfloat16)
    value_one = matmul(first_in, value_mat).astype(jnp.bfloat16)
    key_all, value_all = (
        lax.all_gather(key_one, "seq", axis=0, tiled=True),
        lax.all_gather(value_one, "seq", axis=0, tiled=True),
    )
    positions = lax.axis_index("seq") * rows_here + jnp.arange(rows_here)
    causal = positions[:, None] >= jnp.arange(key_all.shape[0])[None, :]
    attend_one, max_one, sum_one = attend_forward(query_one, key_all, value_all, causal, None, None)
    mixed_one = attend_one.astype(jnp.bfloat16)
    second = text_rows + matmul(mixed_one, proj_mat)
    normed_two, norm_two_back = jax.vjp(norm_rows, second, gain_two, shift_two)
    second_in = normed_two.astype(jnp.bfloat16)
    query_two = matmul(second_in, xquery_mat).astype(jnp.bfloat16)
    tile_rows = image_in.astype(jnp.float32)
    normed_tiles, norm_tile_back = jax.vjp(norm_rows, tile_rows, gain_tile, shift_tile)
    tiles_in = normed_tiles.astype(jnp.bfloat16)
    data_index = lax.axis_index("dp")
    data_count = lax.axis_size("dp")
    seq_count = lax.axis_size("seq")
    tile_count = image_in.shape[0]
    slot_rows = image_in.shape[1]
    slide_ids = jnp.arange(owner_map.shape[0])
    destination = jnp.sum(
        jnp.where(tile_slide[:, None] == slide_ids[None, :], owner_map[None, :], 0), axis=1
    )
    own_destination = lax.dynamic_slice_in_dim(destination, data_index * tile_count, tile_count)
    routing = (own_destination[None, :] == jnp.arange(data_count)[:, None]).astype(jnp.bfloat16)
    outgoing = jnp.einsum(
        "pt,trd->prd", routing, tiles_in, preferred_element_type=jnp.float32
    ).astype(jnp.bfloat16)
    incoming = lax.all_to_all(outgoing, "dp", split_axis=0, concat_axis=0, tiled=True)
    arrived = jnp.any(destination.reshape(data_count, tile_count) == data_index, axis=1)
    flat_in = incoming.reshape(data_count * slot_rows, hidden_dim)
    allowed_rows = jnp.broadcast_to(arrived[:, None], (data_count, slot_rows)).reshape(-1)
    key_two = matmul(flat_in, xkey_mat).astype(jnp.bfloat16)
    value_two = matmul(flat_in, xvalue_mat).astype(jnp.bfloat16)
    query_far = lax.all_gather(query_two, "seq", axis=0, tiled=True)
    allowed_near = allowed_rows[None, :]
    local_max, local_sum = attend_stats(query_far, key_two, allowed_near)
    max_two, sum_two = combined_all((local_max, local_sum), "seq", join_stats)
    partial_rows = attend_forward(query_far, key_two, value_two, allowed_near, max_two, sum_two)[0]
    attend_two = lax.psum_scatter(
        partial_rows.astype(jnp.bfloat16), "seq", scatter_dimension=0, tiled=True
    )
    third_sum = second + matmul(attend_two, xproj_mat)
    normed_three, norm_three_back = jax.vjp(norm_rows, third_sum, gain_three, shift_three)
    third_in = normed_three.astype(jnp.bfloat16)
    pre_gelu = matmul(third_in, up_mat) + up_bias
    activated, gelu_back = jax.vjp(partial(jax.nn.gelu, approximate=False), pre_gelu)
    act_in = activated.astype(jnp.bfloat16)
    result = third_sum + matmul(act_in, down_mat) + down_bias
    text_out = result.astype(jnp.bfloat16)[None]
    cot_rows = text_cot[0]
    grad_res = cot_rows.astype(jnp.float32)
    down_grad = outer_sum(act_in, cot_rows)
    downbias_grad = jnp.sum(grad_res, axis=0)
    grad_act = matmul_trans(cot_rows, down_mat).astype(jnp.bfloat16)
    grad_pre = gelu_back(grad_act.astype(jnp.float32))[0].astype(jnp.bfloat16)
    up_grad = outer_sum(third_in, grad_pre)
    upbias_grad = jnp.sum(grad_pre.astype(jnp.float32), axis=0)
    grad_mid, mgain_grad, mshift_grad = norm_three_back(matmul_trans(grad_pre, up_mat))
    grad_third = grad_res + grad_mid
    branch_two = grad_third.astype(jnp.bfloat16)
    xproj_grad = outer_sum(attend_two, branch_two)
    grad_attend_two = matmul_trans(branch_two, xproj_mat).astype(jnp.bfloat16)
    grad_far = lax.all_gather(grad_attend_two, "seq", axis=0, tiled=True)
    row_part = attend_rowsums(
        query_far, key_two, value_two, allowed_near, max_two, sum_two, grad_far
    )
    row_terms = lax.psum(row_part, "seq")
    query_grad_far, key_grad_two, value_grad_two = attend_backward(
        query_far, key_two, value_two, allowed_near, max_two, sum_two, grad_far, row_terms
    )
    query_grad_two = lax.psum_scatter(
        query_grad_far.astype(jnp.bfloat16), "seq", scatter_dimension=0, tiled=True
    )
    gkey_two = key_grad_two.astype(jnp.bfloat16)
    gvalue_two = value_grad_two.astype(jnp.bfloat16)
    xquery_grad = outer_sum(second_in, query_grad_two)
    xkey_grad = outer_sum(flat_in, gkey_two)
    xvalue_grad = outer_sum(flat_in, gvalue_two)
    grad_flat = (matmul_trans(gkey_two, xkey_mat) + matmul_trans(gvalue_two, xvalue_mat)).astype(
        jnp.bfloat16
    )
    grad_home = lax.all_to_all(
        grad_flat.reshape(data_count, slot_rows, hidden_dim),
        "dp",
        split_axis=0,
        concat_axis=0,
        tiled=True,
    )
    grad_tiles = jnp.einsum("pt,prd->trd", routing, grad_home, preferred_element_type=jnp.float32)
    image_back, tgain_grad, tshift_grad = norm_tile_back(grad_tiles)
    image_grad = image_back.astype(jnp.bfloat16)
    grad_mid_two, xgain_grad, xshift_grad = norm_two_back(matmul_trans(query_grad_two, xquery_mat))
    grad_second = grad_third + grad_mid_two
    branch_one = grad_second.astype(jnp.bfloat16)
    proj_grad = outer_sum(mixed_one, branch_one)
    grad_attend_one = matmul_trans(branch_one, proj_mat).astype(jnp.bfloat16)
    query_grad_one, key_grad_all, value_grad_all = attend_backward(
        query_one, key_all, value_all, causal, max_one, sum_one, grad_attend_one, None
    )
    key_grad_one, value_grad_one = (
        lax.psum_scatter(
            key_grad_all.astype(jnp.bfloat16), "seq", scatter_dimension=0, tiled=True
        ).astype(jnp.float32),
        lax.psum_scatter(
            value_grad_all.astype(jnp.bfloat16), "seq", scatter_dimension=0, tiled=True
        ).astype(jnp.float32),
    )
    gquery_one = query_grad_one.astype(jnp.bfloat16)
    gkey_one = key_grad_one.astype(jnp.bfloat16)
    gvalue_one = value_grad_one.astype(jnp.bfloat16)
    query_grad = outer_sum(first_in, gquery_one)
    key_grad = outer_sum(first_in, gkey_one)
    value_grad = outer_sum(first_in, gvalue_one)
    grad_norm_one = (
        matmul_trans(gquery_one, query_mat)
        + matmul_trans(gkey_one, key_mat)
        + matmul_trans(gvalue_one, value_mat)
    )
    grad_mid_one, sgain_grad, sshift_grad = norm_one_back(grad_norm_one)
    text_grad = (grad_second + grad_mid_one).astype(jnp.bfloat16)[None]
    pieces = (
        lax.all_to_all(
            split_rows(query_grad, data_count, seq_count).astype(jnp.bfloat16),
            "seq",
            split_axis=1,
            concat_axis=1,
            tiled=True,
        ).astype(jnp.float32),
        lax.all_to_all(
            split_rows(key_grad, data_count, seq_count).astype(jnp.bfloat16),
            "seq",
            split_axis=1,
            concat_axis=1,
            tiled=True,
        ).astype(jnp.float32),
        lax.all_to_all(
            split_rows(value_grad, data_count, seq_count).astype(jnp.bfloat16),
            "seq",
            split_axis=1,
            concat_axis=1,
            tiled=True,
        ).astype(jnp.float32),
        lax.all_to_all(
            split_rows(proj_grad, data_count, seq_count).astype(jnp.bfloat16),
            "seq",
            split_axis=1,
            concat_axis=1,
            tiled=True,
        ).astype(jnp.float32),
        lax.all_to_all(
            split_rows(xquery_grad, data_count, seq_count).astype(jnp.bfloat16),
            "seq",
            split_axis=1,
            concat_axis=1,
            tiled=True,
        ).astype(jnp.float32),
        lax.all_to_all(
            split_rows(xkey_grad, data_count, seq_count).astype(jnp.bfloat16),
            "seq",
            split_axis=1,
            concat_axis=1,
            tiled=True,
        ).astype(jnp.float32),
        lax.all_to_all(
            split_rows(xvalue_grad, data_count, seq_count).astype(jnp.bfloat16),
            "seq",
            split_axis=1,
            concat_axis=1,
            tiled=True,
        ).astype(jnp.float32),
        lax.all_to_all(
            split_rows(xproj_grad, data_count, seq_count).astype(jnp.bfloat16),
            "seq",
            split_axis=1,
            concat_axis=1,
            tiled=True,
        ).astype(jnp.float32),
        lax.all_to_all(
            split_rows(up_grad, data_count, seq_count).astype(jnp.bfloat16),
            "seq",
            split_axis=1,
            concat_axis=1,
            tiled=True,
        ).astype(jnp.float32),
        lax.all_to_all(
            split_rows(down_grad, data_count, seq_count).astype(jnp.bfloat16),
            "seq",
            split_axis=1,
            concat_axis=1,
            tiled=True,
        ).astype(jnp.float32),
    )
    folded = [fold_rows(member) for member in pieces]
    summed_mats = (
        lax.psum_scatter(folded[0], "dp", scatter_dimension=0, tiled=True),
        lax.psum_scatter(folded[1], "dp", scatter_dimension=0, tiled=True),
        lax.psum_scatter(folded[2], "dp", scatter_dimension=0, tiled=True),
        lax.psum_scatter(folded[3], "dp", scatter_dimension=0, tiled=True),
        lax.psum_scatter(folded[4], "dp", scatter_dimension=0, tiled=True),
        lax.psum_scatter(folded[5], "dp", scatter_dimension=0, tiled=True),
        lax.psum_scatter(folded[6], "dp", scatter_dimension=0, tiled=True),
        lax.psum_scatter(folded[7], "dp", scatter_dimension=0, tiled=True),
        lax.psum_scatter(folded[8], "dp", scatter_dimension=0, tiled=True),
        lax.psum_scatter(folded[9], "dp", scatter_dimension=0, tiled=True),
    )
    summed_vecs = (
        lax.psum_scatter(upbias_grad, ("dp", "seq"), scatter_dimension=0, tiled=True),
        lax.psum_scatter(downbias_grad, ("dp", "seq"), scatter_dimension=0, tiled=True),
        lax.psum_scatter(sgain_grad, ("dp", "seq"), scatter_dimension=0, tiled=True),
        lax.psum_scatter(sshift_grad, ("dp", "seq"), scatter_dimension=0, tiled=True),
        lax.psum_scatter(xgain_grad, ("dp", "seq"), scatter_dimension=0, tiled=True),
        lax.psum_scatter(xshift_grad, ("dp", "seq"), scatter_dimension=0, tiled=True),
        lax.psum_scatter(tgain_grad, ("dp", "seq"), scatter_dimension=0, tiled=True),
        lax.psum_scatter(tshift_grad, ("dp", "seq"), scatter_dimension=0, tiled=True),
        lax.psum_scatter(mgain_grad, ("dp", "seq"), scatter_dimension=0, tiled=True),
        lax.psum_scatter(mshift_grad, ("dp", "seq"), scatter_dimension=0, tiled=True),
    )
    return (text_out, text_grad, image_grad) + tuple(summed_mats) + tuple(summed_vecs)


def dot_plain(former, latter):
    return jnp.dot(former, latter, preferred_element_type=jnp.float32)


def dot_right(former, latter):
    return lax.dot_general(
        former, latter, (((1,), (1,)), ((), ())), preferred_element_type=jnp.float32
    )


def dot_left(former, latter):
    return lax.dot_general(
        former, latter, (((0,), (0,)), ((), ())), preferred_element_type=jnp.float32
    )


def low(values):
    return values.astype(jnp.bfloat16)


def wide(values):
    return values.astype(jnp.float32)


def block(index, size):
    if isinstance(index, int):
        return pl.ds(index * size, size)
    return pl.ds(pl.multiple_of(index * size, size), size)


def lanes(start, size):
    return pl.ds(start, size)


def norm_parts(values):
    average = jnp.mean(values, axis=-1, keepdims=True)
    centered = values - average
    spread = jnp.mean(centered * centered, axis=-1, keepdims=True)
    inverse = lax.rsqrt(spread + EPSILON)
    return centered * inverse, inverse


def norm_back(unit, inverse, gain_row, grad):
    scaled = grad * gain_row
    first = jnp.mean(scaled, axis=-1, keepdims=True)
    second = jnp.mean(scaled * unit, axis=-1, keepdims=True)
    return (scaled - first - unit * second) * inverse


def column_sum(values):
    return jnp.sum(values, axis=0, keepdims=True)


class Copies:
    def __init__(self, send_sems, recv_sems):
        self.send_sems, self.recv_sems = send_sems, recv_sems
        self.count = 0
        self.started = []

    def make(self, source, target, device):
        index = self.count
        self.count += 1
        return pltpu.make_async_remote_copy(
            src_ref=source,
            dst_ref=target,
            send_sem=self.send_sems.at[index],
            recv_sem=self.recv_sems.at[index],
            device_id=device,
            device_id_type=MESH,
        )

    def begin(self, source, target, device):
        copy = self.make(source, target, device)
        copy.start()
        self.started.append(copy)
        return copy


COPY_SLOTS = 256


def scratch_of(width, tokens, seq_count, data_count, hidden, main, shard):
    length = tokens * seq_count
    band = shard * seq_count
    inbox = data_count * main
    rests = seq_count * data_count
    keys = inbox * seq_count + rests
    bf16, f32 = jnp.bfloat16, jnp.float32
    return dict(
        vec_own=((16, LANES), f32),
        vec_all=((data_count, seq_count, 16, LANES), bf16),
        vec=((16, width), f32),
        up_bias=((1, hidden), f32),
        key_bias=((1, keys), f32),
        slab_out=((seq_count, shard, 1536 + hidden), bf16),
        slab_in=((seq_count, shard, 1536 + hidden), bf16),
        cols=((width, 768 + hidden), bf16),
        halves=((data_count, 2, band // 2, 768), bf16),
        cot_all=((length, width), bf16),
        h1=((length, width), bf16),
        h2=((length, width), bf16),
        h3=((length, width), bf16),
        e1=((length, width), bf16),
        e2=((length, width), bf16),
        out_all=((data_count, shard, 2 * width), bf16),
        out_in=((seq_count, data_count // seq_count, shard, 2 * width), bf16),
        out_rows=((256, 2 * width), bf16),
        down_all=((hidden, width), bf16),
        outbox=((inbox, width), bf16),
        units=((inbox, width), bf16),
        rest_rows=((data_count, width), f32),
        rest_wide=((rests * 16, LANES), f32),
        rest_out=((data_count, 16, LANES), bf16),
        rest_in=((seq_count, data_count, 16, LANES), bf16),
        tiles=((keys, width), bf16),
        kv2=((keys, 512), bf16),
        dkv2=((keys, 512), bf16),
        qm1=((3 * length, LANES), bf16),
        qm2=((3 * length, LANES), bf16),
        dom=((3 * length, LANES), bf16),
        qkv1=((length, 768), bf16),
        p1=((3 * length, length), f32),
        o1=((length, 256), bf16),
        o2=((length, 256), bf16),
        o_acc=((length, 256), f32),
        ds=((3 * length, keys), bf16),
        pr=((3 * length, keys), bf16),
        sums_out=((6, 3, tokens, width), bf16),
        sums_in=((6, 3, tokens, width), bf16),
        x2=((tokens, width), f32),
        x3=((tokens, width), f32),
        dx=((tokens, width), f32),
        act=((length, hidden), bf16),
        slope=((length, hidden), f32),
        du=((length, hidden), bf16),
        dqkv=((length, 768), bf16),
        dq2=((length, 256), bf16),
        dn=((keys, width), bf16),
        dn_pair=((2, inbox, width), bf16),
        dn_far=((inbox, width), bf16),
        dn_home=((inbox, width), bf16),
        dr_out=((seq_count, data_count, 16, LANES), bf16),
        dr_pair=((2, data_count, 16, LANES), bf16),
        dr_far=((data_count, 16, LANES), bf16),
        dr_home=((data_count, 16, LANES), bf16),
        g_cols=((width, 768 + hidden), bf16),
        g_half=((data_count, 2, band // 2, 768), bf16),
        half_in=((data_count, band // 2, 768), bf16),
        g_cross=((width, 256), bf16),
        g_down=((hidden, width), bf16),
        g_out=((data_count, shard, 2 * width), bf16),
        g_out_send=((2, seq_count, data_count // seq_count, shard, width), bf16),
        y_up=((4, band, hidden), bf16),
        z_up=((3, band, hidden), bf16),
        y_down=((4, band, width), bf16),
        z_down=((3, band, width), bf16),
        y_full=((4, band, 768), bf16),
        z_full=((3, band, 768), bf16),
        y_half=((4, band // 2, 768), bf16),
        z_half=((3, band // 2, 768), bf16),
        y_xout=((4, shard, width), bf16),
        z_xout=((3, shard, width), bf16),
        y_sout=((4, shard, width), bf16),
        z_sout=((3, shard, width), bf16),
        cols_out=((seq_count, shard, 768 + hidden), bf16),
        cols_in=((seq_count, shard, 768 + hidden), bf16),
        ends_out=((2, shard, 768), bf16),
        ends_in=((seq_count, shard, 768), bf16),
        vv=((16, width), f32),
        vv_out=((data_count, 16, LANES), f32),
        vv_in=((data_count, 16, LANES), f32),
        vq=((seq_count, 16, LANES), f32),
    )


def lane_pick(parts, lane):
    result = None
    for source, first, place, size in parts:
        start = first // LANES * LANES
        stop = start + LANES * (1 if first + size <= start + LANES else 2)
        window = source[:, start:stop]
        turn = (place - first + start) % (stop - start)
        if turn:
            window = pltpu.roll(window, turn, 1)
        window = window[:, 0:LANES]
        if result is None:
            result = window
        else:
            result = jnp.where((lane >= place) & (lane < place + size), window, result)
    return result


def spans(start, stop, size):
    while start < stop:
        end = min(stop, (start // size + 1) * size)
        yield start, end - start
        start = end


def fused_kernel(names, n_in, *refs):
    (
        slide, owner, text, img, cot, w_query, w_key, w_value, w_out, c_query, c_key, c_value,
        c_out, w_up, w_down, b_up, b_down, *gains,
    ) = refs[:n_in]
    r_text, r_tgrad, r_igrad, r_cols, r_half, r_outs, r_down, r_vec = refs[n_in : n_in + 8]
    m = SimpleNamespace(**dict(zip(names, refs[n_in + 8 :])))
    links = Copies(m.send, m.recv)
    begin = links.begin

    _, tokens, width = text.shape
    seq_count = m.slab_out.shape[0]
    length = tokens * seq_count
    shard = w_out.shape[0]
    data_count = m.vec_all.shape[0]
    hidden = m.down_all.shape[0]
    band = shard * seq_count
    tile_count, real_rows, _ = img.shape
    slides = owner.shape[0]
    main = real_rows // 16 * 16
    inbox = data_count * main
    keys_main = inbox * seq_count
    rests = seq_count * data_count
    keys = keys_main + rests
    columns = width // LANES
    factor = 1.0 / math.sqrt(HEAD)
    z_count = data_count // 2

    d = lax.axis_index("dp")
    s = lax.axis_index("seq")
    z, y = d // 2, d % 2
    core = s % 2
    sibling = s + 1 - 2 * core
    across = (s + 2) % 4
    corner = 3 - s
    seq_peers = [sibling, across, corner]
    z_pair = z + 1 - 2 * (z % 2)
    z_across = (z + 2) % 4
    z_corner = 3 - z
    near = (z * 2 + 1 - y, s)
    beside = (z_pair * 2 + y, s)
    beyond = (z_across * 2 + y, s)

    barrier = pltpu.get_barrier_semaphore()
    for peer in seq_peers:
        pl.semaphore_signal(barrier, inc=1, device_id=(d, peer), device_id_type=MESH)
    for k in range(1, data_count):
        pl.semaphore_signal(
            barrier, inc=1, device_id=((d + k) % data_count, s), device_id_type=MESH
        )

    lane = lax.broadcasted_iota(jnp.int32, (1, LANES), 1)
    head_masks = [
        jnp.where(lane < HEAD, 1.0, 0.0),
        jnp.where(lane >= HEAD, 1.0, 0.0),
        jnp.where(lane // HEAD == core, 1.0, 0.0),
    ]

    def arrive(copies):
        for copy in copies:
            copy.wait_recv()

    def seq_gather(views):
        own = [view(s) for view in views]
        pair = [begin(part, part, (d, sibling)) for part in own]
        far = [begin(part, part, (d, across)) for part in own]
        return views, pair, far

    def seq_pass(state):
        arrive(state[2])
        for part in [view(across) for view in state[0]]:
            state[1].append(begin(part, part, (d, sibling)))

    def seq_end(state):
        arrive(state[1])

    def rows_of(ref):
        return [lambda index: ref.at[block(index, tokens)]]

    def send_all(refs, device):
        return [begin(ref, ref, device) for ref in refs]

    def gather_open(view):
        return view, [], []

    def gather_far(state):
        own = state[0](d)
        state[1].extend([send_all(own, beyond), send_all(own, beside)])

    def gather_near(state):
        state[2].extend(send_all(state[0](d), near))

    def gather_step(state, k):
        view, far, close = state
        arrive(far[k])
        part = view((z_across, z_pair, z_corner)[k] * 2 + y)
        if k == 0:
            far.append(send_all(part, beside))
        close.extend(send_all(part, near))

    def gather_end(state):
        arrive(state[2])

    def seq_sum_begin(slot, produce):
        both = low(produce(sibling, corner))
        m.sums_out[slot, 0] = both[0:tokens]
        m.sums_out[slot, 1] = both[tokens : 2 * tokens]
        pair = pl.ds(0, 2)
        copy = begin(m.sums_out.at[slot, pair], m.sums_in.at[slot, pair], (d, sibling))
        both = produce(across, s)
        return slot, copy, both[0:tokens], both[tokens : 2 * tokens]

    def seq_sum_pass(state):
        slot, copy, far, own = state
        copy.wait_recv()
        m.sums_out[slot, 2] = low(far + wide(m.sums_in[slot, 1]))
        return slot, begin(m.sums_out.at[slot, 2], m.sums_in.at[slot, 2], (d, across)), own

    def seq_sum_end(state):
        slot, copy, own = state
        own = own + wide(m.sums_in[slot, 0])
        copy.wait_recv()
        return own + wide(m.sums_in[slot, 2])

    def pick(ref, first, second, place=slice(None)):
        return jnp.concatenate(
            [ref[block(first, tokens), place], ref[block(second, tokens), place]], axis=0
        )

    sum_targets = (z_corner, z_pair, z_across, z)

    def sum_begin(view, y_in, z_in):
        close = [
            [
                begin(part, ref.at[k], near)
                for part, ref in zip(view(target * 2 + 1 - y), y_in, strict=True)
            ]
            for k, target in enumerate(sum_targets)
        ]
        return SimpleNamespace(view=view, y_in=y_in, z_in=z_in, close=close, far=[], own=[])

    def sum_step(state, k):
        arrive(state.close[k])
        if k == 2:
            arrive(state.far[0])
        copies = []
        for index, part in enumerate(state.view(sum_targets[k] * 2 + y)):
            total = wide(part[...]) + wide(state.y_in[index][k])
            if k == 3:
                state.own.append(total)
                continue
            if k == 2:
                total = total + wide(state.z_in[index][0])
            part[...] = low(total)
            target = state.z_in[index].at[k]
            copies.append(begin(part, target, beyond if k == 2 else beside))
        state.far.append(copies)

    def sum_middle(state):
        for k in range(4):
            sum_step(state, k)

    def sum_end(state):
        arrive(state.far[1] + state.far[2])
        return [
            own + wide(ref[1]) + wide(ref[2])
            for own, ref in zip(state.own, state.z_in, strict=True)
        ]

    cross, own = (c_query, c_key, c_value), (w_query, w_key, w_value)
    up_wide = wide(w_up[...])
    slab_out, slab_in = m.slab_out, m.slab_in
    for j in range(seq_count):
        full, half = 3 * (j // 2) + 2 * (j % 2), 3 * (j // 2) + 1
        sources = [(matrix, full) for matrix in cross + own]
        sources += [(matrix, half) for matrix in cross + own]
        for k, (matrix, index) in enumerate(sources):
            place = slice(LANES * k, LANES * k + LANES)
            slab_out[j, :, place] = matrix[:, LANES * index : LANES * index + LANES]
        for tile in range(hidden // LANES):
            pieces = [
                (up_wide, band * (seq_count * (at // band) + j) + at % band, at % LANES, size)
                for at, size in spans(LANES * tile, LANES * tile + LANES, band)
            ]
            slab_out[j, :, 1536 + LANES * tile : 1536 + LANES * (tile + 1)] = low(
                lane_pick(pieces, lane)
            )
    vec_own = m.vec_own
    vec_own[...] = jnp.zeros(vec_own.shape, jnp.float32)
    for k, ref in enumerate((b_down, *gains)):
        vec_own[k : k + 1, 0:shard] = wide(ref[...])
    vec_own[9:10, 0:band] = wide(b_up[...])
    vec_all = m.vec_all
    vec_all[d, s] = low(vec_own[...])
    slab_in[s] = slab_out[s]
    out_all, down_all, cot_all = m.out_all, m.down_all, m.cot_all
    out_all[d, :, 0:width] = w_out[...]
    out_all[d, :, width : 2 * width] = c_out[...]
    down_all[block(d, band)] = w_down[...]
    cot_all[block(s, tokens)] = cot[0]
    m.rest_wide[...] = jnp.zeros(m.rest_wide.shape, jnp.float32)


    def destination(index):
        total = jnp.int32(0)
        for k in range(slides):
            total = total + jnp.where(slide[index] == k, owner[k], 0)
        return total

    own_places = [destination(d * tile_count + t) for t in range(tile_count)]
    route = [
        [jnp.where(place == p, 1.0, 0.0) for place in own_places] for p in range(data_count)
    ]
    spot = lax.broadcasted_iota(jnp.int32, (1, keys), 1)
    slot_of = jnp.where(spot < keys_main, spot % inbox // main, (spot - keys_main) % data_count)
    bias = jnp.zeros((1, keys), jnp.float32)
    for p in range(data_count):
        hits = jnp.int32(0)
        for t in range(tile_count):
            hits = hits + jnp.where(destination(p * tile_count + t) == d, 1, 0)
        bias = jnp.where(slot_of == p, jnp.where(hits > 0, 0.0, MASKED_SCORE), bias)
    m.key_bias[...] = bias
    text_unit, _ = norm_parts(wide(text[0]))

    outbox, tiles = m.outbox, m.tiles
    rest_rows, rest_wide, rest_out, rest_in = m.rest_rows, m.rest_wide, m.rest_out, m.rest_in
    units = [wide(low(norm_parts(wide(img[t]))[0])) for t in range(tile_count)]
    for p in range(data_count):
        total = units[0] * route[p][0]
        for t in range(1, tile_count):
            total = total + units[t] * route[p][t]
        outbox[block(p, main)] = low(total[0:main])
        rest_rows[p : p + 1] = total[main:real_rows]
    for k in range(columns):
        rest_wide[pl.ds(k, data_count, stride=16), :] = rest_rows[:, LANES * k : LANES * (k + 1)]
    rest_out[...] = low(rest_wide[0 : 16 * data_count]).reshape(rest_out.shape)
    own_slot = block(s * data_count + d, main)
    tiles[own_slot] = outbox[block(d, main)]
    rest_in[s, d] = rest_out[d]
    tile_dp = []

    def tile_out(k):
        peer = (d + k) % data_count
        tile_dp.append(begin(outbox.at[block(peer, main)], tiles.at[own_slot], (peer, s)))
        tile_dp.append(begin(rest_out.at[peer], rest_in.at[s, d], (peer, s)))

    pl.semaphore_wait(barrier, seq_count - 1 + data_count - 1)

    own_vec = vec_all.at[d, s]
    vec_dp = [begin(own_vec, own_vec, ((d + k) % data_count, s)) for k in range(1, data_count)]
    slab_seq = [begin(slab_out.at[peer], slab_in.at[s], (d, peer)) for peer in seq_peers]
    for k in (2, 1, 4, 3, 6, 5, 7):
        tile_out(k)
    out_view = lambda index: [out_all.at[index]]
    out_ag = gather_open(out_view)
    gather_far(out_ag)
    gather_near(out_ag)
    arrive(vec_dp)
    vec_column = vec_all.at[:, s]
    vec_seq = [begin(vec_column, vec_column, (d, peer)) for peer in seq_peers]
    arrive(slab_seq)
    cols, halves = m.cols, m.halves
    rows = jnp.concatenate([wide(slab_in[j]) for j in range(seq_count)], axis=0)
    cols[block(d, band), 0:768] = low(rows[:, 0:768])
    cols[block(d, band), 768 : 768 + hidden] = low(rows[:, 1536 : 1536 + hidden])
    rows = rows[:, 768:1536]
    rows = jnp.where(core == 0, rows[0 : band // 2], rows[band // 2 : band])
    halves[d, core] = low(rows)

    def group_view(full, half, first):
        place = lanes(first, 384)
        return lambda index: [
            full.at[block(index, band), place],
            half.at[index, core, :, place],
        ]

    def half_cols(first, size):
        return halves[:, :, :, first : first + size].reshape(width, size)

    def half_swap(first):
        part = halves.at[:, core, :, lanes(first, 384)]
        return begin(part, part, (d, sibling))

    self_view, cross_view = group_view(cols, halves, 384), group_view(cols, halves, 0)
    up_view = lambda index: [cols.at[block(index, band), lanes(768, hidden)]]
    down_view = lambda index: [down_all.at[block(index, band)]]
    self_ag, cross_ag = gather_open(self_view), gather_open(cross_view)
    up_ag, down_ag = gather_open(up_view), gather_open(down_view)
    gather_far(self_ag)
    for state in (self_ag, cross_ag, up_ag, down_ag):
        gather_near(state)
    arrive(vec_seq)
    stacked = vec_all[...].reshape(data_count * seq_count * 16, LANES)
    row_of = lax.broadcasted_iota(jnp.int32, (LANES, width), 0)
    col_of = lax.broadcasted_iota(jnp.int32, (LANES, width), 1)
    spread = dot_plain(stacked, jnp.where(row_of == col_of % shard, 1.0, 0.0).astype(jnp.bfloat16))
    spread = spread.reshape(data_count * seq_count, 16, width)
    which = lax.broadcasted_iota(jnp.int32, spread.shape, 0)
    column = lax.broadcasted_iota(jnp.int32, spread.shape, 2)
    vec = m.vec
    vec[...] = jnp.sum(jnp.where(which == column // shard, spread, 0.0), axis=0)

    def vector(index):
        return vec[index : index + 1, :]

    h1, h2, h3, e1, e2 = m.h1, m.h2, m.h3, m.e1, m.e2
    h1[block(s, tokens)] = low(text_unit * vector(1) + vector(2))
    h1_ag = seq_gather(rows_of(h1))

    arrive(tile_dp)
    whole_place = block(s, inbox)
    m.units[...] = tiles[whole_place]
    tiles[whole_place] = low(wide(m.units[...]) * vector(5) + vector(6))
    whole_own = tiles.at[block(s, inbox)]
    tile_pair = [
        begin(whole_own, whole_own, (d, sibling)),
        begin(rest_in.at[s], rest_in.at[s], (d, sibling)),
    ]
    rest_far = begin(rest_in.at[s], rest_in.at[s], (d, across))
    quarter = inbox // 4

    def quarter_of(index, k):
        return tiles.at[pl.ds(pl.multiple_of(index * inbox + k * quarter, quarter), quarter)]

    def tile_send(k):
        part = quarter_of(s, k)
        return begin(part, part, (d, across))

    def tile_pass(k):
        tile_far[k].wait_recv()
        part = quarter_of(across, k)
        tile_pair.append(begin(part, part, (d, sibling)))

    tile_far = [tile_send(k) for k in range(4)]
    gather_step(out_ag, 0)
    gather_step(out_ag, 1)
    gather_step(self_ag, 0)
    gather_step(self_ag, 1)
    gather_step(out_ag, 2)
    gather_far(cross_ag)
    gather_far(up_ag)
    seq_pass(h1_ag)
    gather_end(out_ag)
    per_seq = data_count // seq_count
    out_in = m.out_in
    out_seq = []
    for peer in (across, corner, sibling):
        out_seq.append(
            begin(out_all.at[pl.ds(peer * per_seq, per_seq)], out_in.at[s], (d, peer))
        )
    out_in[s] = out_all[pl.ds(s * per_seq, per_seq)]
    gather_step(self_ag, 2)
    gather_end(self_ag)
    half_copy = half_swap(384)
    seq_end(h1_ag)
    qkv1, qm1, p1, o1 = m.qkv1, m.qm1, m.p1, m.o1
    qkv1[:, 0:384] = low(dot_plain(h1[...], cols[:, 384:768]))
    arrive([half_copy])
    qkv1[:, 384:768] = low(dot_plain(h1[...], half_cols(384, 384)))
    gather_step(cross_ag, 0)
    gather_step(cross_ag, 1)
    gather_far(down_ag)

    spot_q = lax.broadcasted_iota(jnp.int32, (length, length), 0)
    spot_k = lax.broadcasted_iota(jnp.int32, (length, length), 1)
    causal = spot_q >= spot_k
    mixed = []
    for head in range(3):
        base = 384 * (head // 2)
        qm = low(wide(qkv1[:, base : base + 128]) * head_masks[head])
        qm1[block(head, length)] = qm
        scores = dot_right(qm, qkv1[:, base + 128 : base + 256]) * factor
        scores = jnp.where(causal, scores, MASKED_SCORE)
        exponent = jnp.exp(scores - jnp.max(scores, axis=1, keepdims=True))
        chances = exponent / jnp.sum(exponent, axis=1, keepdims=True)
        p1[block(head, length)] = chances
        mixed.append(
            dot_plain(low(chances), qkv1[:, base + 256 : base + 384]) * head_masks[head]
        )
    o1[:, 0:128] = low(mixed[0] + mixed[1])
    o1[:, 128:256] = low(mixed[2])

    arrive(out_seq)
    out_rows = m.out_rows
    natural = jnp.concatenate(
        [wide(out_in[j, i]) for i in range(per_seq) for j in range(seq_count)], axis=0
    )
    blank = jnp.zeros((64, 2 * width), jnp.float32)
    even = jnp.concatenate([natural, blank], axis=0)
    odd = jnp.concatenate([natural[64:192], blank, natural[0:64]], axis=0)
    out_rows[...] = low(jnp.where(core == 0, even, odd))

    state = seq_sum_begin(0, lambda i, j: dot_plain(pick(o1, i, j), out_rows[:, 0:width]))
    state = seq_sum_pass(state)
    gather_step(cross_ag, 2)
    x2, x3, dx = m.x2, m.x3, m.dx
    second = wide(text[0]) + seq_sum_end(state)
    x2[...] = second
    unit, _ = norm_parts(second)
    h2[block(s, tokens)] = low(unit * vector(3) + vector(4))
    h2_ag = seq_gather(rows_of(h2))
    cot_ag = seq_gather(rows_of(cot_all))
    gather_step(up_ag, 0)
    gather_step(up_ag, 1)
    row_up = lax.broadcasted_iota(jnp.int32, (LANES, hidden), 0)
    col_up = lax.broadcasted_iota(jnp.int32, (LANES, hidden), 1)
    spread = dot_plain(stacked, jnp.where(row_up == col_up % band, 1.0, 0.0).astype(jnp.bfloat16))
    spread = spread.reshape(data_count * seq_count, 16, hidden)
    which = lax.broadcasted_iota(jnp.int32, spread.shape, 0)
    column = lax.broadcasted_iota(jnp.int32, spread.shape, 2)
    picked = jnp.where(which == (column // band) * seq_count + s, spread, 0.0)
    m.up_bias[...] = jnp.sum(picked, axis=0)[9:10]


    kv2, qm2, pr, o2, o_acc = m.kv2, m.qm2, m.pr, m.o2, m.o_acc

    def keys_values(here):
        rows = tiles[here]
        kv2[here, 0:256] = low(dot_plain(rows, cols[:, 128:384]))
        kv2[here, 256:512] = low(dot_plain(rows, half_cols(128, 256)))

    gather_end(cross_ag)
    half_copy = half_swap(0)
    arrive([half_copy])
    keys_values(block(s, inbox))
    tile_pass(0)
    seq_pass(h2_ag)
    arrive(tile_pair[0:2])
    keys_values(block(sibling, inbox))
    tile_pass(1)
    rest_far.wait_recv()
    tile_pair.append(begin(rest_in.at[across], rest_in.at[across], (d, sibling)))
    seq_end(h2_ag)
    query_full = dot_plain(h2[...], cols[:, 0:128])
    query_half = dot_plain(h2[...], half_cols(0, 128))
    for head in range(3):
        source = query_full if head < 2 else query_half
        qm2[block(head, length)] = low(wide(low(source)) * (head_masks[head] * factor))
    tile_pass(2)
    tile_pass(3)
    gather_step(up_ag, 2)
    gather_step(down_ag, 0)
    keys_values(block(across, inbox))
    arrive(tile_pair[2:])
    keys_values(block(corner, inbox))
    rest_wide[...] = wide(rest_in[...]).reshape(rest_wide.shape)
    for k in range(columns):
        place = slice(LANES * k, LANES * (k + 1))
        tiles[keys_main:keys, place] = low(
            rest_wide[pl.ds(k, rests, stride=16), :] * vec[5:6, place] + vec[6:7, place]
        )
    keys_values(pl.ds(keys_main, rests))
    gather_step(down_ag, 1)
    for head in range(3):
        base = 256 * (head // 2)
        place = 128 * (head // 2)

        here = block(head, length)
        scores = dot_right(qm2[here], kv2[:, base : base + 128]) + m.key_bias[...]
        exponent = jnp.exp(scores - jnp.max(scores, axis=1, keepdims=True))
        chances = low(exponent * (1.0 / jnp.sum(exponent, axis=1, keepdims=True)))
        pr[here] = chances
        result = dot_plain(chances, kv2[:, base + 128 : base + 256]) * head_masks[head]
        if head == 1:
            result = result + o_acc[:, place : place + 128]
        o_acc[:, place : place + 128] = result
        if head == 0:
            gather_step(down_ag, 2)

    o2[...] = low(o_acc[...])
    state = seq_sum_begin(
        1, lambda i, j: dot_plain(pick(o2, i, j), out_rows[:, width : 2 * width])
    )
    state = seq_sum_pass(state)
    third = x2[...] + seq_sum_end(state)
    x3[...] = third
    unit, _ = norm_parts(third)
    h3[block(s, tokens)] = low(unit * vector(7) + vector(8))
    h3_ag = seq_gather(rows_of(h3))
    seq_pass(cot_ag)
    seq_end(cot_ag)
    seq_pass(h3_ag)
    gather_end(down_ag)
    act, slope, du = m.act, m.slope, m.du
    slope[...] = dot_right(cot_all[...], down_all[...])
    gather_end(up_ag)
    seq_end(h3_ag)

    @pl.loop(0, seq_count)
    def _(i):
        here = block(i, tokens)
        pre = dot_plain(h3[here], cols[:, 768 : 768 + hidden]) + m.up_bias[...]
        cdf = 0.5 * (1.0 + lax.erf(pre * (1.0 / math.sqrt(2.0))))
        density = jnp.exp(-0.5 * pre * pre) * (1.0 / math.sqrt(2.0 * math.pi))
        act[here] = low(pre * cdf)
        grad = wide(low(slope[here]))
        du[here] = low(grad * (cdf + pre * density))

    state = seq_sum_begin(
        2, lambda i, j: dot_right(pick(du, i, j), cols[:, 768 : 768 + hidden])
    )
    state = seq_sum_pass(state)
    g_cols, g_down = m.g_cols, m.g_down
    g_down[...] = low(dot_left(act[...], cot_all[...]))
    g_down_view = lambda index: [g_down.at[block(index, band)]]
    down_rs = sum_begin(g_down_view, [m.y_down], [m.z_down])
    grad_mid = seq_sum_end(state)
    unit, inverse = norm_parts(x3[...])
    vv = m.vv
    vv[...] = jnp.zeros(vv.shape, jnp.float32)
    grad_out = wide(cot[0])
    dx3 = grad_out + norm_back(unit, inverse, vector(7), grad_mid)
    dx[...] = dx3
    e2[block(s, tokens)] = low(dx3)
    e2_ag = seq_gather(rows_of(e2))
    vv[0:1] = column_sum(grad_out)
    vv[7:8] = column_sum(grad_mid * unit)
    vv[8:9] = column_sum(grad_mid)
    vv[9:10, 0:hidden] = column_sum(wide(du[...]))

    g_cols[:, 768 : 768 + hidden] = low(dot_left(h3[...], du[...]))
    g_up_view = lambda index: [g_cols.at[block(index, band), lanes(768, hidden)]]
    up_rs = sum_begin(g_up_view, [m.y_up], [m.z_up])
    sum_step(down_rs, 0)
    seq_pass(e2_ag)
    sum_step(down_rs, 1)
    seq_end(e2_ag)

    dom = m.dom
    grad_o = low(dot_right(e2[...], out_rows[:, width : 2 * width]))
    for head in range(3):
        place = 128 * (head // 2)
        dom[block(head, length)] = low(wide(grad_o[:, place : place + 128]) * head_masks[head])
    ds, dkv2, dq2 = m.ds, m.dkv2, m.dq2
    for head in range(3):
        base = 256 * (head // 2)
        place = 128 * (head // 2)

        here = block(head, length)
        chances = wide(pr[here])
        grad_p = dot_right(dom[here], kv2[:, base + 128 : base + 256])
        weighted = jnp.sum(chances * grad_p, axis=1, keepdims=True)
        grad_s = low(chances * (grad_p - weighted))
        ds[here] = grad_s
        result = dot_plain(grad_s, kv2[:, base : base + 128]) * (head_masks[head] * factor)
        if head == 1:
            result = result + o_acc[:, place : place + 128]
        o_acc[:, place : place + 128] = result
        if head < 2:
            sum_step(down_rs, 2 + head)

    dq2[...] = low(o_acc[...])
    sum_step(up_rs, 0)
    state = seq_sum_begin(
        4,
        lambda i, j: dot_right(pick(dq2, i, j, slice(0, 128)), cols[:, 0:128])
        + dot_right(pick(dq2, i, j, slice(128, 256)), half_cols(0, 128)),
    )

    g_out, g_out_send = m.g_out, m.g_out_send

    def out_grad(slot, value):
        odd = jnp.concatenate([value[192:256], value[0:128]], axis=0)
        natural = jnp.where(core == 0, value[0:192], odd)
        for i in range(per_seq):
            for j in range(seq_count):
                start = shard * (i * seq_count + j)
                g_out_send[slot, j, i] = low(natural[start : start + shard])
        target = g_out.at[pl.ds(s * per_seq, per_seq), :, lanes(slot * width, width)]
        copies = [begin(g_out_send.at[slot, peer], target, (d, peer)) for peer in seq_peers]
        g_out[pl.ds(s * per_seq, per_seq), :, slot * width : (slot + 1) * width] = g_out_send[
            slot, s
        ]
        return copies

    xout_seq = out_grad(1, dot_left(o2[...], e2[...]))
    state = seq_sum_pass(state)
    for tile in range(2):
        first, count = (0, 2 * length) if tile == 0 else (2 * length, length)
        base = 256 * tile
        for start, size in spans(0, keys, 512):
            cut = slice(start, start + size)
            dkv2[cut, base : base + 128] = low(
                dot_left(ds[first : first + count, cut], qm2[first : first + count])
            )
            dkv2[cut, base + 128 : base + 256] = low(
                dot_left(pr[first : first + count, cut], dom[first : first + count])
            )
    sum_step(up_rs, 1)
    second_grad = seq_sum_end(state)
    unit, inverse = norm_parts(x2[...])
    dx2 = dx[...] + norm_back(unit, inverse, vector(3), second_grad)
    dx[...] = dx2
    e1[block(s, tokens)] = low(dx2)
    e1_ag = seq_gather(rows_of(e1))
    vv[3:4] = column_sum(second_grad * unit)
    vv[4:5] = column_sum(second_grad)
    sum_step(up_rs, 2)
    arrive(xout_seq)
    xout_view = lambda index: [g_out.at[index, :, lanes(width, width)]]
    xout_rs = sum_begin(xout_view, [m.y_xout], [m.z_xout])

    dn = m.dn

    def tile_grads(here):
        dn[here] = low(
            dot_right(dkv2[here, 0:256], cols[:, 128:384])
            + dot_right(dkv2[here, 256:512], half_cols(128, 256))
        )

    dr_out, dr_pair, dr_far, dr_home = m.dr_out, m.dr_pair, m.dr_far, m.dr_home
    dn_pair, dn_far, dn_home = m.dn_pair, m.dn_far, m.dn_home
    tile_grads(block(corner, inbox))
    pair_far = begin(dn.at[block(corner, inbox)], dn_pair.at[1], (d, sibling))
    tile_grads(pl.ds(keys_main, rests))
    rest_wide[...] = jnp.zeros(rest_wide.shape, jnp.float32)
    for k in range(columns):
        rest_wide[pl.ds(k, rests, stride=16), :] = wide(
            dn[keys_main:keys, LANES * k : LANES * (k + 1)]
        )
    dr_out[...] = low(rest_wide[...]).reshape(dr_out.shape)
    rest_pair = [
        begin(dr_out.at[peer], dr_pair.at[k], (d, sibling))
        for k, peer in enumerate((sibling, corner))
    ]
    tile_grads(block(across, inbox))
    seq_pass(e1_ag)
    pair_far.wait_recv()
    fold = dn.at[block(across, inbox)]
    fold[...] = low(wide(fold[...]) + wide(dn_pair[1]))
    arrive(rest_pair)
    dr_out[across] = low(wide(dr_out[across]) + wide(dr_pair[1]))
    rest_far = begin(dr_out.at[across], dr_far, (d, across))

    def far_send(k):
        return begin(quarter_in(dn, across, k), dn_far.at[block(k, quarter)], (d, across))

    def quarter_in(ref, index, k):
        return ref.at[pl.ds(pl.multiple_of(index * inbox + k * quarter, quarter), quarter)]

    far_copies = [far_send(k) for k in range(4)]
    sum_step(up_rs, 3)
    g_half, half_in, g_cross = m.g_half, m.half_in, m.g_cross
    half_shape = (data_count, 2, band // 2)

    def half_send(first):
        place = lanes(first, 384)
        return begin(g_half.at[:, 1 - core, :, place], half_in.at[:, :, place], (d, sibling))

    def half_add(first, copy):
        copy.wait_recv()
        place = lanes(first, 384)
        g_half[:, core, :, place] = low(
            wide(g_half[:, core, :, place]) + wide(half_in[:, :, place])
        )

    seq_end(e1_ag)
    grad_o = low(dot_right(e1[...], out_rows[:, 0:width]))
    grads = []
    dqkv = m.dqkv
    for head in range(3):
        base = 384 * (head // 2)
        place = 128 * (head // 2)
        here = block(head, length)
        dm = low(wide(grad_o[:, place : place + 128]) * head_masks[head])
        chances = p1[here]
        grad_p = dot_right(dm, qkv1[:, base + 256 : base + 384])
        weighted = jnp.sum(chances * grad_p, axis=1, keepdims=True)
        grad_s = low(chances * (grad_p - weighted))
        grads.append(
            (
                dot_plain(grad_s, qkv1[:, base + 128 : base + 256]) * (head_masks[head] * factor),
                dot_left(grad_s, qm1[here]) * factor,
                dot_left(low(chances), dm),
            )
        )
    for k in range(3):
        dqkv[:, 128 * k : 128 * k + 128] = low(grads[0][k] + grads[1][k])
        dqkv[:, 384 + 128 * k : 512 + 128 * k] = low(grads[2][k])
    state = seq_sum_begin(
        5,
        lambda i, j: dot_right(pick(dqkv, i, j, slice(0, 384)), cols[:, 384:768])
        + dot_right(pick(dqkv, i, j, slice(384, 768)), half_cols(384, 384)),
    )

    grad = dot_left(h1[...], dqkv[...])
    g_cols[:, 384:768] = low(grad[:, 0:384])
    g_half[:, :, :, 384:768] = low(grad[:, 384:768]).reshape(*half_shape, 384)
    half_copy = half_send(384)
    state = seq_sum_pass(state)
    sout_seq = out_grad(0, dot_left(o1[...], e1[...]))
    half_add(384, half_copy)
    self_rs = sum_begin(
        group_view(g_cols, g_half, 384),
        [m.y_full.at[:, :, lanes(384, 384)], m.y_half.at[:, :, lanes(384, 384)]],
        [m.z_full.at[:, :, lanes(384, 384)], m.z_half.at[:, :, lanes(384, 384)]],
    )
    out_state = seq_sum_begin(3, lambda i, j: dot_plain(pick(act, i, j), down_all[...]))
    tile_grads(block(sibling, inbox))
    pair_own = begin(dn.at[block(sibling, inbox)], dn_pair.at[0], (d, sibling))
    tile_grads(block(s, inbox))

    sum_middle(xout_rs)
    out_state = seq_sum_pass(out_state)
    grad = dot_left(h2[...], dq2[...])
    g_cols[:, 0:128] = low(grad[:, 0:128])
    g_half[:, :, :, 0:128] = low(grad[:, 128:256]).reshape(*half_shape, 128)
    for cut in range(3):
        span = slice(256 * cut, 256 * cut + 256)
        grad = dot_left(tiles[:, span], dkv2[...])
        g_cols[span, 128:384] = low(grad[:, 0:256])
        g_cross[span] = low(grad[:, 256:512])
    g_half[:, :, :, 128:384] = g_cross[...].reshape(*half_shape, 256)
    half_copy = half_send(0)
    sum_step(self_rs, 0)
    half_add(0, half_copy)
    cross_rs = sum_begin(
        group_view(g_cols, g_half, 0),
        [m.y_full.at[:, :, lanes(0, 384)], m.y_half.at[:, :, lanes(0, 384)]],
        [m.z_full.at[:, :, lanes(0, 384)], m.z_half.at[:, :, lanes(0, 384)]],
    )
    sum_step(self_rs, 1)
    arrive(sout_seq)
    sout_view = lambda index: [g_out.at[index, :, lanes(0, width)]]
    sout_rs = sum_begin(sout_view, [m.y_sout], [m.z_sout])
    arrive([pair_own, rest_far])
    dr_out[s] = low(wide(dr_out[s]) + wide(dr_pair[0]) + wide(dr_far[...]))

    home_dp = []
    own_home = block(d, main)
    for k in range(4):
        far_copies[k].wait_recv()
        mine = quarter_in(dn, s, k)
        there = block(k, quarter)
        mine[...] = low(wide(mine[...]) + wide(dn_pair[0, there]) + wide(dn_far[there]))

    def home_send(k):
        peer = (d + k) % data_count
        source = dn.at[block(s * data_count + peer, main)]
        home_dp.append(begin(source, dn_home.at[own_home], (peer, s)))
        home_dp.append(begin(dr_out.at[s, peer], dr_home.at[d], (peer, s)))

    sum_step(self_rs, 2)
    for k in (2, 4, 6):
        home_send(k)
    sum_step(self_rs, 3)
    sum_step(cross_rs, 0)
    sum_step(cross_rs, 1)
    for k in (1, 3, 5, 7):
        home_send(k)
    dn_home[own_home] = dn[block(s * data_count + d, main)]
    dr_home[d] = dr_out[s, d]
    grad = wide(dn[block(s, inbox)])
    vv[5:6] = column_sum(grad * wide(m.units[...]))
    vv[6:7] = column_sum(grad)
    rest = wide(dr_out[s])
    for row, total in ((5, rest * wide(rest_in[s])), (6, rest)):
        total = jnp.sum(total, axis=0)
        total = jnp.concatenate([total[k : k + 1] for k in range(columns)], axis=1)
        vv[row : row + 1] = vv[row : row + 1] + total
    first_grad = seq_sum_end(state)
    unit, inverse = norm_parts(wide(text[0]))
    vv[1:2] = column_sum(first_grad * unit)
    vv[2:3] = column_sum(first_grad)
    r_tgrad[...] = low(dx[...] + norm_back(unit, inverse, vector(1), first_grad))
    vv_out, vv_in, vq = m.vv_out, m.vv_in, m.vq
    everything = vv[...]
    for p in range(data_count):
        turned = everything if p == 0 else pltpu.roll(everything, width - band * p, 1)
        vv_out[p] = turned[:, 0:LANES]
    vv_dp = []
    for k in range(1, data_count):
        peer = (d + k) % data_count
        vv_dp.append(begin(vv_out.at[peer], vv_in.at[d], (peer, s)))
    vv_in[d] = vv_out[d]
    sum_step(cross_rs, 2)
    sum_step(cross_rs, 3)
    sum_middle(sout_rs)
    arrive(vv_dp)
    total = vv_in[0]
    for p in range(1, data_count):
        total = total + vv_in[p]
    vq[s] = total
    vq_seq = [begin(vq.at[s], vq.at[s], (d, peer)) for peer in seq_peers]
    bias_grad = total[9:10]
    r_text[...] = low(x3[...] + seq_sum_end(out_state) + vector(0))

    cols_out, cols_in, ends_out, ends_in = m.cols_out, m.cols_in, m.ends_out, m.ends_in

    def finish_cols(first, size, total):
        place = lanes(first, size)
        for j in range(seq_count):
            cols_out[j, :, place] = low(total[shard * j : shard * (j + 1)])
        cols_in[s, :, place] = cols_out[s, :, place]
        return [
            begin(cols_out.at[peer, :, place], cols_in.at[s, :, place], (d, peer))
            for peer in seq_peers
        ]

    def finish_half(first, total):
        place = lanes(first, 384)
        for j in range(2):
            ends_out[j, :, place] = low(total[shard * j : shard * (j + 1)])
        ends_in[s, :, place] = ends_out[core, :, place]
        return [
            begin(ends_out.at[peer % 2, :, place], ends_in.at[s, :, place], (d, peer))
            for peer in seq_peers
        ]

    (r_down[...],) = sum_end(down_rs)
    ends = finish_cols(768, hidden, sum_end(up_rs)[0])
    (r_outs[1],) = sum_end(xout_rs)
    full, half = sum_end(self_rs)
    ends += finish_cols(384, 384, full) + finish_half(384, half)

    arrive(home_dp)
    for t in range(tile_count):
        grad = wide(dn_home[block(0, main)]) * route[0][t]
        rest = wide(dr_home[0]) * route[0][t]
        for p in range(1, data_count):
            grad = grad + wide(dn_home[block(p, main)]) * route[p][t]
            rest = rest + wide(dr_home[p]) * route[p][t]
        rest = jnp.concatenate([rest[k : k + 1] for k in range(columns)], axis=1)
        unit, inverse = norm_parts(wide(img[t, 0:main]))
        r_igrad[t, 0:main] = low(norm_back(unit, inverse, vector(5), grad))
        unit, inverse = norm_parts(wide(img[t, main:real_rows]))
        r_igrad[t, main:real_rows] = low(norm_back(unit, inverse, vector(5), rest))


    full, half = sum_end(cross_rs)
    ends += finish_cols(0, 384, full) + finish_half(0, half)
    (r_outs[0],) = sum_end(sout_rs)

    arrive(ends)
    r_cols[...] = cols_in[...]
    r_half[...] = ends_in[...]
    arrive(vq_seq)
    total = vq[0] + vq[1] + vq[2] + vq[3]
    r_vec[...] = pltpu.roll(total, (LANES - shard * s) % LANES, 1)
    r_vec[9:10] = bias_grad

    for copy in links.started:
        copy.wait_send()


def unpack_kernel(t_out, t_grad, i_grad, cols, ends, outs, down, vec, *results):
    o_text, o_tgrad, o_igrad, o_q, o_k, o_v, o_o, o_xq, o_xk, o_xv, o_xo, o_up, o_down, *vectors = (
        results
    )
    seq_count, shard, total = cols.shape
    hidden = total - 768
    core = lax.axis_index("seq") // 2
    band = down.shape[0]
    o_text[0] = t_out[...]
    o_tgrad[0] = t_grad[...]
    o_igrad[...] = i_grad[...]
    for k, result in enumerate((o_xq, o_xk, o_xv, o_q, o_k, o_v)):
        here = slice(LANES * k, LANES * (k + 1))
        for j, tile in ((0, 0), (1, 2), (2, 3), (3, 5)):
            result[:, LANES * tile : LANES * (tile + 1)] = wide(cols[j, :, here])
        for j, tile in ((0, 1), (2, 4)):
            result[:, LANES * tile : LANES * (tile + 1)] = wide(ends[j + core, :, here])
    o_o[...] = outs[0]
    o_xo[...] = outs[1]
    o_down[...] = down[...]
    lane = lax.broadcasted_iota(jnp.int32, (1, LANES), 1)
    parts = [wide(cols[j, :, 768:total]) for j in range(seq_count)]
    for tile in range(hidden * seq_count // LANES):
        pieces = []
        for at, size in spans(LANES * tile, LANES * tile + LANES, band):
            group = at // band
            first = band * (group // seq_count) + at % band
            pieces.append((parts[group % seq_count], first, at % LANES, size))
        o_up[:, LANES * tile : LANES * (tile + 1)] = lane_pick(pieces, lane)
    vectors[0][...] = vec[9, 0:band]
    for k, result in enumerate(vectors[1:]):
        result[...] = vec[k, 0:shard]


def fused_device(
    text_in, image_in, tile_slide, owner_map, text_cot,
    w_query, w_key, w_value, w_out, c_query, c_key, c_value, c_out, w_up, w_down, b_up, b_down,
    self_gain, self_shift, cross_gain, cross_shift, tile_gain, tile_shift, mlp_gain, mlp_shift,
):
    data_count, seq_count = lax.axis_size("dp"), lax.axis_size("seq")
    tile_count, real_rows, width = image_in.shape
    tokens = text_in.shape[1]
    shard = w_query.shape[0]
    band = shard * seq_count
    hidden = w_up.shape[1] // seq_count
    main = real_rows // 16 * 16

    gains = (
        self_gain, self_shift, cross_gain, cross_shift, tile_gain, tile_shift, mlp_gain, mlp_shift,
    )
    inputs = (
        tile_slide, owner_map, text_in, image_in, text_cot, w_query, w_key, w_value, w_out,
        c_query, c_key, c_value, c_out, w_up, w_down,
        *[member.reshape(1, -1) for member in (b_up, b_down, *gains)],
    )
    in_specs = [pl.BlockSpec(memory_space=pltpu.SMEM)] * 2
    in_specs += [pl.BlockSpec(memory_space=pltpu.VMEM)] * (len(inputs) - 2)
    row_out = jax.ShapeDtypeStruct((tokens, width), jnp.bfloat16)
    packed_shape = [
        row_out,
        row_out,
        jax.ShapeDtypeStruct(image_in.shape, jnp.bfloat16),
        jax.ShapeDtypeStruct((seq_count, shard, 768 + hidden), jnp.bfloat16),
        jax.ShapeDtypeStruct((seq_count, shard, 768), jnp.bfloat16),
        jax.ShapeDtypeStruct((2, shard, width), jnp.float32),
        jax.ShapeDtypeStruct((band, width), jnp.float32),
        jax.ShapeDtypeStruct((16, LANES), jnp.float32),
    ]
    shapes = scratch_of(width, tokens, seq_count, data_count, hidden, main, shard)
    scratch = [pltpu.VMEM(shape, kind) for shape, kind in shapes.values()]
    scratch += [pltpu.SemaphoreType.DMA((COPY_SLOTS,))] * 2
    names = [*shapes, "send", "recv"]
    packed = pl.pallas_call(
        partial(fused_kernel, names, len(inputs)),
        out_shape=packed_shape,
        in_specs=in_specs,
        out_specs=[pl.BlockSpec(memory_space=pltpu.VMEM)] * len(packed_shape),
        scratch_shapes=scratch,
        compiler_params=pltpu.CompilerParams(
            collective_id=0, has_side_effects=True, vmem_limit_bytes=60 * 1024 * 1024
        ),
        name="decoder_layer",
    )(*inputs)
    square = jax.ShapeDtypeStruct((shard, width), jnp.float32)
    out_shape = [
        jax.ShapeDtypeStruct(text_in.shape, jnp.bfloat16),
        jax.ShapeDtypeStruct(text_in.shape, jnp.bfloat16),
        jax.ShapeDtypeStruct(image_in.shape, jnp.bfloat16),
        *[square] * 8,
        jax.ShapeDtypeStruct((shard, hidden * seq_count), jnp.float32),
        jax.ShapeDtypeStruct((band, width), jnp.float32),
        jax.ShapeDtypeStruct((band,), jnp.float32),
        *[jax.ShapeDtypeStruct((shard,), jnp.float32)] * 9,
    ]
    return tuple(
        pl.pallas_call(
            unpack_kernel,
            out_shape=out_shape,
            in_specs=[pl.BlockSpec(memory_space=pltpu.VMEM)] * len(packed),
            out_specs=[pl.BlockSpec(memory_space=pltpu.VMEM)] * len(out_shape),
            name="unpack",
        )(*packed)
    )


def fused_fits(mesh):
    return mesh.shape["seq"] == 4 and 768 % (8 * mesh.shape["dp"] * mesh.shape["seq"]) == 0


def solution(mesh):
    placed = (
        P("dp", "seq", None),
        P("dp", "seq", None),
        P(),
        P(),
        P("dp", "seq", None),
        P(("dp", "seq"), None),
        P(("dp", "seq"), None),
        P(("dp", "seq"), None),
        P(("dp", "seq"), None),
        P(("dp", "seq"), None),
        P(("dp", "seq"), None),
        P(("dp", "seq"), None),
        P(("dp", "seq"), None),
        P(("dp", "seq"), None),
        P(("dp", "seq"), None),
        P(("dp", "seq")),
        P(("dp", "seq")),
        P(("dp", "seq")),
        P(("dp", "seq")),
        P(("dp", "seq")),
        P(("dp", "seq")),
        P(("dp", "seq")),
        P(("dp", "seq")),
        P(("dp", "seq")),
        P(("dp", "seq")),
    )
    return jax.shard_map(
        fused_device if fused_fits(mesh) else per_device,
        mesh=mesh,
        in_specs=placed,
        out_specs=(
            P("dp", "seq", None),
            P("dp", "seq", None),
            P("dp", "seq", None),
            P(("dp", "seq"), None),
            P(("dp", "seq"), None),
            P(("dp", "seq"), None),
            P(("dp", "seq"), None),
            P(("dp", "seq"), None),
            P(("dp", "seq"), None),
            P(("dp", "seq"), None),
            P(("dp", "seq"), None),
            P(("dp", "seq"), None),
            P(("dp", "seq"), None),
            P(("dp", "seq")),
            P(("dp", "seq")),
            P(("dp", "seq")),
            P(("dp", "seq")),
            P(("dp", "seq")),
            P(("dp", "seq")),
            P(("dp", "seq")),
            P(("dp", "seq")),
            P(("dp", "seq")),
            P(("dp", "seq")),
        ),
        check_vma=False,
    )
```

```python
from functools import partial
import math
from types import SimpleNamespace

import jax
import jax.numpy as jnp
from jax import lax
from jax.experimental import pallas as pl
from jax.experimental.pallas import tpu as pltpu
from jax.sharding import PartitionSpec as P

HEAD = 64
LANES = 128
MESH = pl.DeviceIdType.MESH


EPSILON = 1e-05
MASKED_SCORE = -1e30


def combined_all(x, axis, combine):
    everything = jax.tree.map(lambda part: lax.all_gather(part, axis), x)
    initial = jax.tree.map(lambda part: part[0], everything)

    def step(k, so_far):
        return combine(so_far, jax.tree.map(lambda part: part[k], everything))

    return lax.fori_loop(1, lax.axis_size(axis), step, initial)


def norm_rows(values, gain_row, shift_row):
    average = jnp.mean(values, axis=-1, keepdims=True)
    centered = values - average
    spread = jnp.mean(centered * centered, axis=-1, keepdims=True)
    return centered * lax.rsqrt(spread + EPSILON) * gain_row + shift_row


def matmul(former, latter):
    return jnp.dot(former, latter, preferred_element_type=jnp.float32)


def matmul_trans(former, latter):
    return lax.dot_general(
        former, latter, (((1,), (1,)), ((), ())), preferred_element_type=jnp.float32
    )


def outer_sum(former, latter):
    return lax.dot_general(
        former, latter, (((0,), (0,)), ((), ())), preferred_element_type=jnp.float32
    )


def head_pair(matrix, pair_index):
    columns = lax.dynamic_slice_in_dim(matrix, pair_index * 2 * HEAD, 2 * HEAD, 1)
    return columns.reshape(columns.shape[0], 2, HEAD)


def put_pair(matrix, update, pair_index):
    return lax.dynamic_update_slice_in_dim(
        matrix, update.reshape(update.shape[0], 2 * HEAD), pair_index * 2 * HEAD, 1
    )


def pick_pair(stacked, pair_index):
    return lax.dynamic_index_in_dim(stacked, pair_index, 0, keepdims=False)


def pair_scores(query_rows, key_rows, allowed, pair_index):
    factor = 1.0 / math.sqrt(HEAD)
    scores = (
        jnp.einsum(
            "qhd,khd->hqk",
            head_pair(query_rows, pair_index),
            head_pair(key_rows, pair_index),
            preferred_element_type=jnp.float32,
        )
        * factor
    )
    return jnp.where(allowed[None], scores, MASKED_SCORE)


def attend_stats(query_rows, key_rows, allowed):
    pair_count = query_rows.shape[1] // (2 * HEAD)

    def one_pair(pair_index, state_now):
        row_max, row_sum = state_now
        scores = pair_scores(query_rows, key_rows, allowed, pair_index)
        highest = jnp.max(scores, axis=2)
        summed = jnp.sum(jnp.exp(scores - highest[..., None]), axis=2)
        return (
            lax.dynamic_update_index_in_dim(row_max, highest, pair_index, 0),
            lax.dynamic_update_index_in_dim(row_sum, summed, pair_index, 0),
        )

    empty_stats = jnp.zeros((pair_count, 2, query_rows.shape[0]), jnp.float32)
    return lax.fori_loop(0, pair_count, one_pair, (empty_stats, empty_stats))


def attend_forward(query_rows, key_rows, value_rows, allowed, maxima, totals):
    pair_count = query_rows.shape[1] // (2 * HEAD)
    stats_given = maxima is not None
    if not stats_given:
        maxima = jnp.zeros((pair_count, 2, query_rows.shape[0]), jnp.float32)
        totals = jnp.zeros_like(maxima)

    def one_pair(pair_index, state_now):
        output, row_max, row_sum = state_now
        scores = pair_scores(query_rows, key_rows, allowed, pair_index)
        if stats_given:
            highest = pick_pair(row_max, pair_index)
            exponent = jnp.exp(scores - highest[..., None])
            summed = pick_pair(row_sum, pair_index)
        else:
            highest = jnp.max(scores, axis=2)
            exponent = jnp.exp(scores - highest[..., None])
            summed = jnp.sum(exponent, axis=2)
            row_max = lax.dynamic_update_index_in_dim(row_max, highest, pair_index, 0)
            row_sum = lax.dynamic_update_index_in_dim(row_sum, summed, pair_index, 0)
        weights = (exponent / summed[..., None]).astype(jnp.bfloat16)
        mixture = jnp.einsum(
            "hqk,khd->qhd",
            weights,
            head_pair(value_rows, pair_index),
            preferred_element_type=jnp.float32,
        )
        return (put_pair(output, mixture, pair_index), row_max, row_sum)

    start_state = (jnp.zeros(query_rows.shape, jnp.float32), maxima, totals)
    return lax.fori_loop(0, pair_count, one_pair, start_state)


def attend_rowsums(query_rows, key_rows, value_rows, allowed, maxima, totals, grad_rows):
    pair_count = query_rows.shape[1] // (2 * HEAD)

    def one_pair(pair_index, row_terms):
        scores = pair_scores(query_rows, key_rows, allowed, pair_index)
        chances = (
            jnp.exp(scores - pick_pair(maxima, pair_index)[..., None])
            / pick_pair(totals, pair_index)[..., None]
        )
        grad_chances = jnp.einsum(
            "qhd,khd->hqk",
            head_pair(grad_rows, pair_index),
            head_pair(value_rows, pair_index),
            preferred_element_type=jnp.float32,
        )
        return lax.dynamic_update_index_in_dim(
            row_terms, jnp.sum(chances * grad_chances, axis=2), pair_index, 0
        )

    return lax.fori_loop(0, pair_count, one_pair, jnp.zeros_like(maxima))


def attend_backward(
    query_rows, key_rows, value_rows, allowed, maxima, totals, grad_rows, row_terms
):
    pair_count = query_rows.shape[1] // (2 * HEAD)
    factor = 1.0 / math.sqrt(HEAD)

    def one_pair(pair_index, state_now):
        grad_query, grad_key, grad_value = state_now
        scores = pair_scores(query_rows, key_rows, allowed, pair_index)
        chances = (
            jnp.exp(scores - pick_pair(maxima, pair_index)[..., None])
            / pick_pair(totals, pair_index)[..., None]
        )
        grad_heads = head_pair(grad_rows, pair_index)
        grad_chances = jnp.einsum(
            "qhd,khd->hqk",
            grad_heads,
            head_pair(value_rows, pair_index),
            preferred_element_type=jnp.float32,
        )
        if row_terms is None:
            weighted = jnp.sum(chances * grad_chances, axis=2)
        else:
            weighted = pick_pair(row_terms, pair_index)
        grad_scores = (chances * (grad_chances - weighted[..., None])).astype(jnp.bfloat16)
        query_part = (
            jnp.einsum(
                "hqk,khd->qhd",
                grad_scores,
                head_pair(key_rows, pair_index),
                preferred_element_type=jnp.float32,
            )
            * factor
        )
        key_part = (
            jnp.einsum(
                "hqk,qhd->khd",
                grad_scores,
                head_pair(query_rows, pair_index),
                preferred_element_type=jnp.float32,
            )
            * factor
        )
        value_part = jnp.einsum(
            "hqk,qhd->khd",
            chances.astype(jnp.bfloat16),
            grad_heads,
            preferred_element_type=jnp.float32,
        )
        return (
            put_pair(grad_query, query_part, pair_index),
            put_pair(grad_key, key_part, pair_index),
            put_pair(grad_value, value_part, pair_index),
        )

    start_state = (
        jnp.zeros(query_rows.shape, jnp.float32),
        jnp.zeros(key_rows.shape, jnp.float32),
        jnp.zeros(value_rows.shape, jnp.float32),
    )
    return lax.fori_loop(0, pair_count, one_pair, start_state)


def join_stats(former, latter):
    highest = jnp.maximum(former[0], latter[0])
    return (
        highest,
        former[1] * jnp.exp(former[0] - highest) + latter[1] * jnp.exp(latter[0] - highest),
    )


def split_rows(matrix, data_count, seq_count):
    return matrix.reshape(
        data_count, seq_count, matrix.shape[0] // (data_count * seq_count), matrix.shape[1]
    )


def fold_rows(pieces):
    return jnp.sum(pieces, axis=1).reshape(pieces.shape[0] * pieces.shape[2], pieces.shape[3])


def per_device(
    text_in,
    image_in,
    tile_slide,
    owner_map,
    text_cot,
    w_query,
    w_key,
    w_value,
    w_out,
    c_query,
    c_key,
    c_value,
    c_out,
    w_up,
    w_down,
    b_up,
    b_down,
    self_gain,
    self_shift,
    cross_gain,
    cross_shift,
    tile_gain,
    tile_shift,
    mlp_gain,
    mlp_shift,
):
    gathered = (
        lax.all_gather(w_query, ("dp", "seq"), axis=0, tiled=True),
        lax.all_gather(w_key, ("dp", "seq"), axis=0, tiled=True),
        lax.all_gather(w_value, ("dp", "seq"), axis=0, tiled=True),
        lax.all_gather(w_out, ("dp", "seq"), axis=0, tiled=True),
        lax.all_gather(c_query, ("dp", "seq"), axis=0, tiled=True),
        lax.all_gather(c_key, ("dp", "seq"), axis=0, tiled=True),
        lax.all_gather(c_value, ("dp", "seq"), axis=0, tiled=True),
        lax.all_gather(c_out, ("dp", "seq"), axis=0, tiled=True),
        lax.all_gather(w_up, ("dp", "seq"), axis=0, tiled=True),
        lax.all_gather(w_down, ("dp", "seq"), axis=0, tiled=True),
        lax.all_gather(b_up, ("dp", "seq"), axis=0, tiled=True),
        lax.all_gather(b_down, ("dp", "seq"), axis=0, tiled=True),
        lax.all_gather(self_gain, ("dp", "seq"), axis=0, tiled=True),
        lax.all_gather(self_shift, ("dp", "seq"), axis=0, tiled=True),
        lax.all_gather(cross_gain, ("dp", "seq"), axis=0, tiled=True),
        lax.all_gather(cross_shift, ("dp", "seq"), axis=0, tiled=True),
        lax.all_gather(tile_gain, ("dp", "seq"), axis=0, tiled=True),
        lax.all_gather(tile_shift, ("dp", "seq"), axis=0, tiled=True),
        lax.all_gather(mlp_gain, ("dp", "seq"), axis=0, tiled=True),
        lax.all_gather(mlp_shift, ("dp", "seq"), axis=0, tiled=True),
    )
    query_mat, key_mat, value_mat, proj_mat = (gathered[0], gathered[1], gathered[2], gathered[3])
    xquery_mat, xkey_mat, xvalue_mat, xproj_mat = (
        gathered[4],
        gathered[5],
        gathered[6],
        gathered[7],
    )
    up_mat, down_mat = (gathered[8], gathered[9])
    vectors = [member.astype(jnp.float32) for member in gathered[10:]]
    (
        up_bias,
        down_bias,
        gain_one,
        shift_one,
        gain_two,
        shift_two,
        gain_tile,
        shift_tile,
        gain_three,
        shift_three,
    ) = vectors
    text_rows = text_in[0].astype(jnp.float32)
    rows_here = text_rows.shape[0]
    hidden_dim = text_rows.shape[1]
    normed_one, norm_one_back = jax.vjp(norm_rows, text_rows, gain_one, shift_one)
    first_in = normed_one.astype(jnp.bfloat16)
    query_one = matmul(first_in, query_mat).astype(jnp.bfloat16)
    key_one = matmul(first_in, key_mat).astype(jnp.bfloat16)
    value_one = matmul(first_in, value_mat).astype(jnp.bfloat16)
    key_all, value_all = (
        lax.all_gather(key_one, "seq", axis=0, tiled=True),
        lax.all_gather(value_one, "seq", axis=0, tiled=True),
    )
    positions = lax.axis_index("seq") * rows_here + jnp.arange(rows_here)
    causal = positions[:, None] >= jnp.arange(key_all.shape[0])[None, :]
    attend_one, max_one, sum_one = attend_forward(query_one, key_all, value_all, causal, None, None)
    mixed_one = attend_one.astype(jnp.bfloat16)
    second = text_rows + matmul(mixed_one, proj_mat)
    normed_two, norm_two_back = jax.vjp(norm_rows, second, gain_two, shift_two)
    second_in = normed_two.astype(jnp.bfloat16)
    query_two = matmul(second_in, xquery_mat).astype(jnp.bfloat16)
    tile_rows = image_in.astype(jnp.float32)
    normed_tiles, norm_tile_back = jax.vjp(norm_rows, tile_rows, gain_tile, shift_tile)
    tiles_in = normed_tiles.astype(jnp.bfloat16)
    data_index = lax.axis_index("dp")
    data_count = lax.axis_size("dp")
    seq_count = lax.axis_size("seq")
    tile_count = image_in.shape[0]
    slot_rows = image_in.shape[1]
    slide_ids = jnp.arange(owner_map.shape[0])
    destination = jnp.sum(
        jnp.where(tile_slide[:, None] == slide_ids[None, :], owner_map[None, :], 0), axis=1
    )
    own_destination = lax.dynamic_slice_in_dim(destination, data_index * tile_count, tile_count)
    routing = (own_destination[None, :] == jnp.arange(data_count)[:, None]).astype(jnp.bfloat16)
    outgoing = jnp.einsum(
        "pt,trd->prd", routing, tiles_in, preferred_element_type=jnp.float32
    ).astype(jnp.bfloat16)
    incoming = lax.all_to_all(outgoing, "dp", split_axis=0, concat_axis=0, tiled=True)
    arrived = jnp.any(destination.reshape(data_count, tile_count) == data_index, axis=1)
    flat_in = incoming.reshape(data_count * slot_rows, hidden_dim)
    allowed_rows = jnp.broadcast_to(arrived[:, None], (data_count, slot_rows)).reshape(-1)
    key_two = matmul(flat_in, xkey_mat).astype(jnp.bfloat16)
    value_two = matmul(flat_in, xvalue_mat).astype(jnp.bfloat16)
    query_far = lax.all_gather(query_two, "seq", axis=0, tiled=True)
    allowed_near = allowed_rows[None, :]
    local_max, local_sum = attend_stats(query_far, key_two, allowed_near)
    max_two, sum_two = combined_all((local_max, local_sum), "seq", join_stats)
    partial_rows = attend_forward(query_far, key_two, value_two, allowed_near, max_two, sum_two)[0]
    attend_two = lax.psum_scatter(
        partial_rows.astype(jnp.bfloat16), "seq", scatter_dimension=0, tiled=True
    )
    third_sum = second + matmul(attend_two, xproj_mat)
    normed_three, norm_three_back = jax.vjp(norm_rows, third_sum, gain_three, shift_three)
    third_in = normed_three.astype(jnp.bfloat16)
    pre_gelu = matmul(third_in, up_mat) + up_bias
    activated, gelu_back = jax.vjp(partial(jax.nn.gelu, approximate=False), pre_gelu)
    act_in = activated.astype(jnp.bfloat16)
    result = third_sum + matmul(act_in, down_mat) + down_bias
    text_out = result.astype(jnp.bfloat16)[None]
    cot_rows = text_cot[0]
    grad_res = cot_rows.astype(jnp.float32)
    down_grad = outer_sum(act_in, cot_rows)
    downbias_grad = jnp.sum(grad_res, axis=0)
    grad_act = matmul_trans(cot_rows, down_mat).astype(jnp.bfloat16)
    grad_pre = gelu_back(grad_act.astype(jnp.float32))[0].astype(jnp.bfloat16)
    up_grad = outer_sum(third_in, grad_pre)
    upbias_grad = jnp.sum(grad_pre.astype(jnp.float32), axis=0)
    grad_mid, mgain_grad, mshift_grad = norm_three_back(matmul_trans(grad_pre, up_mat))
    grad_third = grad_res + grad_mid
    branch_two = grad_third.astype(jnp.bfloat16)
    xproj_grad = outer_sum(attend_two, branch_two)
    grad_attend_two = matmul_trans(branch_two, xproj_mat).astype(jnp.bfloat16)
    grad_far = lax.all_gather(grad_attend_two, "seq", axis=0, tiled=True)
    row_part = attend_rowsums(
        query_far, key_two, value_two, allowed_near, max_two, sum_two, grad_far
    )
    row_terms = lax.psum(row_part, "seq")
    query_grad_far, key_grad_two, value_grad_two = attend_backward(
        query_far, key_two, value_two, allowed_near, max_two, sum_two, grad_far, row_terms
    )
    query_grad_two = lax.psum_scatter(
        query_grad_far.astype(jnp.bfloat16), "seq", scatter_dimension=0, tiled=True
    )
    gkey_two = key_grad_two.astype(jnp.bfloat16)
    gvalue_two = value_grad_two.astype(jnp.bfloat16)
    xquery_grad = outer_sum(second_in, query_grad_two)
    xkey_grad = outer_sum(flat_in, gkey_two)
    xvalue_grad = outer_sum(flat_in, gvalue_two)
    grad_flat = (matmul_trans(gkey_two, xkey_mat) + matmul_trans(gvalue_two, xvalue_mat)).astype(
        jnp.bfloat16
    )
    grad_home = lax.all_to_all(
        grad_flat.reshape(data_count, slot_rows, hidden_dim),
        "dp",
        split_axis=0,
        concat_axis=0,
        tiled=True,
    )
    grad_tiles = jnp.einsum("pt,prd->trd", routing, grad_home, preferred_element_type=jnp.float32)
    image_back, tgain_grad, tshift_grad = norm_tile_back(grad_tiles)
    image_grad = image_back.astype(jnp.bfloat16)
    grad_mid_two, xgain_grad, xshift_grad = norm_two_back(matmul_trans(query_grad_two, xquery_mat))
    grad_second = grad_third + grad_mid_two
    branch_one = grad_second.astype(jnp.bfloat16)
    proj_grad = outer_sum(mixed_one, branch_one)
    grad_attend_one = matmul_trans(branch_one, proj_mat).astype(jnp.bfloat16)
    query_grad_one, key_grad_all, value_grad_all = attend_backward(
        query_one, key_all, value_all, causal, max_one, sum_one, grad_attend_one, None
    )
    key_grad_one, value_grad_one = (
        lax.psum_scatter(
            key_grad_all.astype(jnp.bfloat16), "seq", scatter_dimension=0, tiled=True
        ).astype(jnp.float32),
        lax.psum_scatter(
            value_grad_all.astype(jnp.bfloat16), "seq", scatter_dimension=0, tiled=True
        ).astype(jnp.float32),
    )
    gquery_one = query_grad_one.astype(jnp.bfloat16)
    gkey_one = key_grad_one.astype(jnp.bfloat16)
    gvalue_one = value_grad_one.astype(jnp.bfloat16)
    query_grad = outer_sum(first_in, gquery_one)
    key_grad = outer_sum(first_in, gkey_one)
    value_grad = outer_sum(first_in, gvalue_one)
    grad_norm_one = (
        matmul_trans(gquery_one, query_mat)
        + matmul_trans(gkey_one, key_mat)
        + matmul_trans(gvalue_one, value_mat)
    )
    grad_mid_one, sgain_grad, sshift_grad = norm_one_back(grad_norm_one)
    text_grad = (grad_second + grad_mid_one).astype(jnp.bfloat16)[None]
    pieces = (
        lax.all_to_all(
            split_rows(query_grad, data_count, seq_count).astype(jnp.bfloat16),
            "seq",
            split_axis=1,
            concat_axis=1,
            tiled=True,
        ).astype(jnp.float32),
        lax.all_to_all(
            split_rows(key_grad, data_count, seq_count).astype(jnp.bfloat16),
            "seq",
            split_axis=1,
            concat_axis=1,
            tiled=True,
        ).astype(jnp.float32),
        lax.all_to_all(
            split_rows(value_grad, data_count, seq_count).astype(jnp.bfloat16),
            "seq",
            split_axis=1,
            concat_axis=1,
            tiled=True,
        ).astype(jnp.float32),
        lax.all_to_all(
            split_rows(proj_grad, data_count, seq_count).astype(jnp.bfloat16),
            "seq",
            split_axis=1,
            concat_axis=1,
            tiled=True,
        ).astype(jnp.float32),
        lax.all_to_all(
            split_rows(xquery_grad, data_count, seq_count).astype(jnp.bfloat16),
            "seq",
            split_axis=1,
            concat_axis=1,
            tiled=True,
        ).astype(jnp.float32),
        lax.all_to_all(
            split_rows(xkey_grad, data_count, seq_count).astype(jnp.bfloat16),
            "seq",
            split_axis=1,
            concat_axis=1,
            tiled=True,
        ).astype(jnp.float32),
        lax.all_to_all(
            split_rows(xvalue_grad, data_count, seq_count).astype(jnp.bfloat16),
            "seq",
            split_axis=1,
            concat_axis=1,
            tiled=True,
        ).astype(jnp.float32),
        lax.all_to_all(
            split_rows(xproj_grad, data_count, seq_count).astype(jnp.bfloat16),
            "seq",
            split_axis=1,
            concat_axis=1,
            tiled=True,
        ).astype(jnp.float32),
        lax.all_to_all(
            split_rows(up_grad, data_count, seq_count).astype(jnp.bfloat16),
            "seq",
            split_axis=1,
            concat_axis=1,
            tiled=True,
        ).astype(jnp.float32),
        lax.all_to_all(
            split_rows(down_grad, data_count, seq_count).astype(jnp.bfloat16),
            "seq",
            split_axis=1,
            concat_axis=1,
            tiled=True,
        ).astype(jnp.float32),
    )
    folded = [fold_rows(member) for member in pieces]
    summed_mats = (
        lax.psum_scatter(folded[0], "dp", scatter_dimension=0, tiled=True),
        lax.psum_scatter(folded[1], "dp", scatter_dimension=0, tiled=True),
        lax.psum_scatter(folded[2], "dp", scatter_dimension=0, tiled=True),
        lax.psum_scatter(folded[3], "dp", scatter_dimension=0, tiled=True),
        lax.psum_scatter(folded[4], "dp", scatter_dimension=0, tiled=True),
        lax.psum_scatter(folded[5], "dp", scatter_dimension=0, tiled=True),
        lax.psum_scatter(folded[6], "dp", scatter_dimension=0, tiled=True),
        lax.psum_scatter(folded[7], "dp", scatter_dimension=0, tiled=True),
        lax.psum_scatter(folded[8], "dp", scatter_dimension=0, tiled=True),
        lax.psum_scatter(folded[9], "dp", scatter_dimension=0, tiled=True),
    )
    summed_vecs = (
        lax.psum_scatter(upbias_grad, ("dp", "seq"), scatter_dimension=0, tiled=True),
        lax.psum_scatter(downbias_grad, ("dp", "seq"), scatter_dimension=0, tiled=True),
        lax.psum_scatter(sgain_grad, ("dp", "seq"), scatter_dimension=0, tiled=True),
        lax.psum_scatter(sshift_grad, ("dp", "seq"), scatter_dimension=0, tiled=True),
        lax.psum_scatter(xgain_grad, ("dp", "seq"), scatter_dimension=0, tiled=True),
        lax.psum_scatter(xshift_grad, ("dp", "seq"), scatter_dimension=0, tiled=True),
        lax.psum_scatter(tgain_grad, ("dp", "seq"), scatter_dimension=0, tiled=True),
        lax.psum_scatter(tshift_grad, ("dp", "seq"), scatter_dimension=0, tiled=True),
        lax.psum_scatter(mgain_grad, ("dp", "seq"), scatter_dimension=0, tiled=True),
        lax.psum_scatter(mshift_grad, ("dp", "seq"), scatter_dimension=0, tiled=True),
    )
    return (text_out, text_grad, image_grad) + tuple(summed_mats) + tuple(summed_vecs)


def dot_plain(former, latter):
    return jnp.dot(former, latter, preferred_element_type=jnp.float32)


def dot_right(former, latter):
    return lax.dot_general(
        former, latter, (((1,), (1,)), ((), ())), preferred_element_type=jnp.float32
    )


def dot_left(former, latter):
    return lax.dot_general(
        former, latter, (((0,), (0,)), ((), ())), preferred_element_type=jnp.float32
    )


def low(values):
    return values.astype(jnp.bfloat16)


def wide(values):
    return values.astype(jnp.float32)


def block(index, size):
    if isinstance(index, int):
        return pl.ds(index * size, size)
    return pl.ds(pl.multiple_of(index * size, size), size)


def lanes(start, size):
    return pl.ds(start, size)


def norm_parts(values):
    average = jnp.mean(values, axis=-1, keepdims=True)
    centered = values - average
    spread = jnp.mean(centered * centered, axis=-1, keepdims=True)
    inverse = lax.rsqrt(spread + EPSILON)
    return centered * inverse, inverse


def norm_back(unit, inverse, gain_row, grad):
    scaled = grad * gain_row
    first = jnp.mean(scaled, axis=-1, keepdims=True)
    second = jnp.mean(scaled * unit, axis=-1, keepdims=True)
    return (scaled - first - unit * second) * inverse


def column_sum(values):
    return jnp.sum(values, axis=0, keepdims=True)


class Copies:
    def __init__(self, send_sems, recv_sems):
        self.send_sems, self.recv_sems = send_sems, recv_sems
        self.count = 0
        self.started = []

    def make(self, source, target, device):
        index = self.count
        self.count += 1
        return pltpu.make_async_remote_copy(
            src_ref=source,
            dst_ref=target,
            send_sem=self.send_sems.at[index],
            recv_sem=self.recv_sems.at[index],
            device_id=device,
            device_id_type=MESH,
        )

    def begin(self, source, target, device):
        copy = self.make(source, target, device)
        copy.start()
        self.started.append(copy)
        return copy


COPY_SLOTS = 256


def scratch_of(width, tokens, seq_count, data_count, hidden, main, shard):
    length = tokens * seq_count
    band = shard * seq_count
    inbox = data_count * main
    rests = seq_count * data_count
    keys = inbox * seq_count + rests
    bf16, f32 = jnp.bfloat16, jnp.float32
    return dict(
        vec_own=((16, LANES), f32),
        vec_all=((data_count, seq_count, 16, LANES), bf16),
        vec=((16, width), f32),
        up_bias=((1, hidden), f32),
        key_bias=((1, keys), f32),
        slab_out=((seq_count, shard, 1536 + hidden), bf16),
        slab_in=((seq_count, shard, 1536 + hidden), bf16),
        cols=((width, 768 + hidden), bf16),
        halves=((data_count, 2, band // 2, 768), bf16),
        cot_all=((length, width), bf16),
        h1=((length, width), bf16),
        h2=((length, width), bf16),
        h3=((length, width), bf16),
        e1=((length, width), bf16),
        e2=((length, width), bf16),
        out_all=((data_count, shard, 2 * width), bf16),
        out_in=((seq_count, data_count // seq_count, shard, 2 * width), bf16),
        out_rows=((256, 2 * width), bf16),
        down_all=((hidden, width), bf16),
        outbox=((inbox, width), bf16),
        units=((inbox, width), bf16),
        rest_rows=((data_count, width), f32),
        rest_wide=((rests * 16, LANES), f32),
        rest_out=((data_count, 16, LANES), bf16),
        rest_in=((seq_count, data_count, 16, LANES), bf16),
        tiles=((keys, width), bf16),
        kv2=((keys, 512), bf16),
        dkv2=((keys, 512), bf16),
        qm1=((3 * length, LANES), bf16),
        qm2=((3 * length, LANES), bf16),
        dom=((3 * length, LANES), bf16),
        qkv1=((length, 768), bf16),
        p1=((3 * length, length), f32),
        o1=((length, 256), bf16),
        o2=((length, 256), bf16),
        o_acc=((length, 256), f32),
        ds=((3 * length, keys), bf16),
        pr=((3 * length, keys), bf16),
        sums_out=((6, 3, tokens, width), bf16),
        sums_in=((6, 3, tokens, width), bf16),
        x2=((tokens, width), f32),
        x3=((tokens, width), f32),
        dx=((tokens, width), f32),
        act=((length, hidden), bf16),
        slope=((length, hidden), f32),
        du=((length, hidden), bf16),
        dqkv=((length, 768), bf16),
        dq2=((length, 256), bf16),
        dn=((keys, width), bf16),
        dn_pair=((2, inbox, width), bf16),
        dn_far=((inbox, width), bf16),
        dn_home=((inbox, width), bf16),
        dr_out=((seq_count, data_count, 16, LANES), bf16),
        dr_pair=((2, data_count, 16, LANES), bf16),
        dr_far=((data_count, 16, LANES), bf16),
        dr_home=((data_count, 16, LANES), bf16),
        g_cols=((width, 768 + hidden), bf16),
        g_half=((data_count, 2, band // 2, 768), bf16),
        half_in=((data_count, band // 2, 768), bf16),
        g_cross=((width, 256), bf16),
        g_down=((hidden, width), bf16),
        g_out=((data_count, shard, 2 * width), bf16),
        g_out_send=((2, seq_count, data_count // seq_count, shard, width), bf16),
        y_up=((4, band, hidden), bf16),
        z_up=((3, band, hidden), bf16),
        y_down=((4, band, width), bf16),
        z_down=((3, band, width), bf16),
        y_full=((4, band, 768), bf16),
        z_full=((3, band, 768), bf16),
        y_half=((4, band // 2, 768), bf16),
        z_half=((3, band // 2, 768), bf16),
        y_xout=((4, shard, width), bf16),
        z_xout=((3, shard, width), bf16),
        y_sout=((4, shard, width), bf16),
        z_sout=((3, shard, width), bf16),
        cols_out=((seq_count, shard, 768 + hidden), bf16),
        cols_in=((seq_count, shard, 768 + hidden), bf16),
        ends_out=((2, shard, 768), bf16),
        ends_in=((seq_count, shard, 768), bf16),
        vv=((16, width), f32),
        vv_out=((data_count, 16, LANES), f32),
        vv_in=((data_count, 16, LANES), f32),
        vq=((seq_count, 16, LANES), f32),
    )


def lane_pick(parts, lane):
    result = None
    for source, first, place, size in parts:
        start = first // LANES * LANES
        stop = start + LANES * (1 if first + size <= start + LANES else 2)
        window = source[:, start:stop]
        turn = (place - first + start) % (stop - start)
        if turn:
            window = pltpu.roll(window, turn, 1)
        window = window[:, 0:LANES]
        if result is None:
            result = window
        else:
            result = jnp.where((lane >= place) & (lane < place + size), window, result)
    return result


def spans(start, stop, size):
    while start < stop:
        end = min(stop, (start // size + 1) * size)
        yield start, end - start
        start = end


def fused_kernel(names, n_in, *refs):
    (
        slide, owner, text, img, cot, w_query, w_key, w_value, w_out, c_query, c_key, c_value,
        c_out, w_up, w_down, b_up, b_down, *gains,
    ) = refs[:n_in]
    r_text, r_tgrad, r_igrad, r_cols, r_half, r_outs, r_down, r_vec = refs[n_in : n_in + 8]
    m = SimpleNamespace(**dict(zip(names, refs[n_in + 8 :])))
    links = Copies(m.send, m.recv)
    begin = links.begin

    _, tokens, width = text.shape
    seq_count = m.slab_out.shape[0]
    length = tokens * seq_count
    shard = w_out.shape[0]
    data_count = m.vec_all.shape[0]
    hidden = m.down_all.shape[0]
    band = shard * seq_count
    tile_count, real_rows, _ = img.shape
    slides = owner.shape[0]
    main = real_rows // 16 * 16
    inbox = data_count * main
    keys_main = inbox * seq_count
    rests = seq_count * data_count
    keys = keys_main + rests
    columns = width // LANES
    factor = 1.0 / math.sqrt(HEAD)
    z_count = data_count // 2

    d = lax.axis_index("dp")
    s = lax.axis_index("seq")
    z, y = d // 2, d % 2
    core = s % 2
    sibling = s + 1 - 2 * core
    across = (s + 2) % 4
    corner = 3 - s
    seq_peers = [sibling, across, corner]
    z_pair = z + 1 - 2 * (z % 2)
    z_across = (z + 2) % 4
    z_corner = 3 - z
    near = (z * 2 + 1 - y, s)
    beside = (z_pair * 2 + y, s)
    beyond = (z_across * 2 + y, s)

    barrier = pltpu.get_barrier_semaphore()
    for peer in seq_peers:
        pl.semaphore_signal(barrier, inc=1, device_id=(d, peer), device_id_type=MESH)
    for k in range(1, data_count):
        pl.semaphore_signal(
            barrier, inc=1, device_id=((d + k) % data_count, s), device_id_type=MESH
        )

    lane = lax.broadcasted_iota(jnp.int32, (1, LANES), 1)
    head_masks = [
        jnp.where(lane < HEAD, 1.0, 0.0),
        jnp.where(lane >= HEAD, 1.0, 0.0),
        jnp.where(lane // HEAD == core, 1.0, 0.0),
    ]

    def arrive(copies):
        for copy in copies:
            copy.wait_recv()

    def seq_gather(views):
        own = [view(s) for view in views]
        pair = [begin(part, part, (d, sibling)) for part in own]
        far = [begin(part, part, (d, across)) for part in own]
        return views, pair, far

    def seq_pass(state):
        arrive(state[2])
        for part in [view(across) for view in state[0]]:
            state[1].append(begin(part, part, (d, sibling)))

    def seq_end(state):
        arrive(state[1])

    def rows_of(ref):
        return [lambda index: ref.at[block(index, tokens)]]

    def send_all(refs, device):
        return [begin(ref, ref, device) for ref in refs]

    def gather_open(view):
        return view, [], []

    def gather_far(state):
        own = state[0](d)
        state[1].extend([send_all(own, beyond), send_all(own, beside)])

    def gather_near(state):
        state[2].extend(send_all(state[0](d), near))

    def gather_step(state, k):
        view, far, close = state
        arrive(far[k])
        part = view((z_across, z_pair, z_corner)[k] * 2 + y)
        if k == 0:
            far.append(send_all(part, beside))
        close.extend(send_all(part, near))

    def gather_end(state):
        arrive(state[2])

    def seq_sum_begin(slot, produce):
        both = low(produce(sibling, corner))
        m.sums_out[slot, 0] = both[0:tokens]
        m.sums_out[slot, 1] = both[tokens : 2 * tokens]
        pair = pl.ds(0, 2)
        copy = begin(m.sums_out.at[slot, pair], m.sums_in.at[slot, pair], (d, sibling))
        both = produce(across, s)
        return slot, copy, both[0:tokens], both[tokens : 2 * tokens]

    def seq_sum_pass(state):
        slot, copy, far, own = state
        copy.wait_recv()
        m.sums_out[slot, 2] = low(far + wide(m.sums_in[slot, 1]))
        return slot, begin(m.sums_out.at[slot, 2], m.sums_in.at[slot, 2], (d, across)), own

    def seq_sum_end(state):
        slot, copy, own = state
        own = own + wide(m.sums_in[slot, 0])
        copy.wait_recv()
        return own + wide(m.sums_in[slot, 2])

    def pick(ref, first, second, place=slice(None)):
        return jnp.concatenate(
            [ref[block(first, tokens), place], ref[block(second, tokens), place]], axis=0
        )

    sum_targets = (z_corner, z_pair, z_across, z)

    def sum_begin(view, y_in, z_in):
        close = [
            [
                begin(part, ref.at[k], near)
                for part, ref in zip(view(target * 2 + 1 - y), y_in, strict=True)
            ]
            for k, target in enumerate(sum_targets)
        ]
        return SimpleNamespace(view=view, y_in=y_in, z_in=z_in, close=close, far=[], own=[])

    def sum_step(state, k):
        arrive(state.close[k])
        if k == 2:
            arrive(state.far[0])
        copies = []
        for index, part in enumerate(state.view(sum_targets[k] * 2 + y)):
            total = wide(part[...]) + wide(state.y_in[index][k])
            if k == 3:
                state.own.append(total)
                continue
            if k == 2:
                total = total + wide(state.z_in[index][0])
            part[...] = low(total)
            target = state.z_in[index].at[k]
            copies.append(begin(part, target, beyond if k == 2 else beside))
        state.far.append(copies)

    def sum_middle(state):
        for k in range(4):
            sum_step(state, k)

    def sum_end(state):
        arrive(state.far[1] + state.far[2])
        return [
            own + wide(ref[1]) + wide(ref[2])
            for own, ref in zip(state.own, state.z_in, strict=True)
        ]

    cross, own = (c_query, c_key, c_value), (w_query, w_key, w_value)
    up_wide = wide(w_up[...])
    slab_out, slab_in = m.slab_out, m.slab_in
    for j in range(seq_count):
        full, half = 3 * (j // 2) + 2 * (j % 2), 3 * (j // 2) + 1
        sources = [(matrix, full) for matrix in cross + own]
        sources += [(matrix, half) for matrix in cross + own]
        for k, (matrix, index) in enumerate(sources):
            place = slice(LANES * k, LANES * k + LANES)
            slab_out[j, :, place] = matrix[:, LANES * index : LANES * index + LANES]
        for tile in range(hidden // LANES):
            pieces = [
                (up_wide, band * (seq_count * (at // band) + j) + at % band, at % LANES, size)
                for at, size in spans(LANES * tile, LANES * tile + LANES, band)
            ]
            slab_out[j, :, 1536 + LANES * tile : 1536 + LANES * (tile + 1)] = low(
                lane_pick(pieces, lane)
            )
    vec_own = m.vec_own
    vec_own[...] = jnp.zeros(vec_own.shape, jnp.float32)
    for k, ref in enumerate((b_down, *gains)):
        vec_own[k : k + 1, 0:shard] = wide(ref[...])
    vec_own[9:10, 0:band] = wide(b_up[...])
    vec_all = m.vec_all
    vec_all[d, s] = low(vec_own[...])
    slab_in[s] = slab_out[s]
    out_all, down_all, cot_all = m.out_all, m.down_all, m.cot_all
    out_all[d, :, 0:width] = w_out[...]
    out_all[d, :, width : 2 * width] = c_out[...]
    down_all[block(d, band)] = w_down[...]
    cot_all[block(s, tokens)] = cot[0]
    m.rest_wide[...] = jnp.zeros(m.rest_wide.shape, jnp.float32)


    def destination(index):
        total = jnp.int32(0)
        for k in range(slides):
            total = total + jnp.where(slide[index] == k, owner[k], 0)
        return total

    own_places = [destination(d * tile_count + t) for t in range(tile_count)]
    route = [
        [jnp.where(place == p, 1.0, 0.0) for place in own_places] for p in range(data_count)
    ]
    spot = lax.broadcasted_iota(jnp.int32, (1, keys), 1)
    slot_of = jnp.where(spot < keys_main, spot % inbox // main, (spot - keys_main) % data_count)
    bias = jnp.zeros((1, keys), jnp.float32)
    for p in range(data_count):
        hits = jnp.int32(0)
        for t in range(tile_count):
            hits = hits + jnp.where(destination(p * tile_count + t) == d, 1, 0)
        bias = jnp.where(slot_of == p, jnp.where(hits > 0, 0.0, MASKED_SCORE), bias)
    m.key_bias[...] = bias
    text_unit, _ = norm_parts(wide(text[0]))

    outbox, tiles = m.outbox, m.tiles
    rest_rows, rest_wide, rest_out, rest_in = m.rest_rows, m.rest_wide, m.rest_out, m.rest_in
    units = [wide(low(norm_parts(wide(img[t]))[0])) for t in range(tile_count)]
    for p in range(data_count):
        total = units[0] * route[p][0]
        for t in range(1, tile_count):
            total = total + units[t] * route[p][t]
        outbox[block(p, main)] = low(total[0:main])
        rest_rows[p : p + 1] = total[main:real_rows]
    for k in range(columns):
        rest_wide[pl.ds(k, data_count, stride=16), :] = rest_rows[:, LANES * k : LANES * (k + 1)]
    rest_out[...] = low(rest_wide[0 : 16 * data_count]).reshape(rest_out.shape)
    own_slot = block(s * data_count + d, main)
    tiles[own_slot] = outbox[block(d, main)]
    rest_in[s, d] = rest_out[d]
    tile_dp = []

    def tile_out(k):
        peer = (d + k) % data_count
        tile_dp.append(begin(outbox.at[block(peer, main)], tiles.at[own_slot], (peer, s)))
        tile_dp.append(begin(rest_out.at[peer], rest_in.at[s, d], (peer, s)))

    pl.semaphore_wait(barrier, seq_count - 1 + data_count - 1)

    own_vec = vec_all.at[d, s]
    vec_dp = [begin(own_vec, own_vec, ((d + k) % data_count, s)) for k in range(1, data_count)]
    slab_seq = [begin(slab_out.at[peer], slab_in.at[s], (d, peer)) for peer in seq_peers]
    for k in (2, 1, 4, 3, 6, 5, 7):
        tile_out(k)
    out_view = lambda index: [out_all.at[index]]
    out_ag = gather_open(out_view)
    gather_far(out_ag)
    gather_near(out_ag)
    arrive(vec_dp)
    vec_column = vec_all.at[:, s]
    vec_seq = [begin(vec_column, vec_column, (d, peer)) for peer in seq_peers]
    arrive(slab_seq)
    cols, halves = m.cols, m.halves
    rows = jnp.concatenate([wide(slab_in[j]) for j in range(seq_count)], axis=0)
    cols[block(d, band), 0:768] = low(rows[:, 0:768])
    cols[block(d, band), 768 : 768 + hidden] = low(rows[:, 1536 : 1536 + hidden])
    rows = rows[:, 768:1536]
    rows = jnp.where(core == 0, rows[0 : band // 2], rows[band // 2 : band])
    halves[d, core] = low(rows)

    def group_view(full, half, first):
        place = lanes(first, 384)
        return lambda index: [
            full.at[block(index, band), place],
            half.at[index, core, :, place],
        ]

    def half_cols(first, size):
        return halves[:, :, :, first : first + size].reshape(width, size)

    def half_swap(first):
        part = halves.at[:, core, :, lanes(first, 384)]
        return begin(part, part, (d, sibling))

    self_view, cross_view = group_view(cols, halves, 384), group_view(cols, halves, 0)
    up_view = lambda index: [cols.at[block(index, band), lanes(768, hidden)]]
    down_view = lambda index: [down_all.at[block(index, band)]]
    self_ag, cross_ag = gather_open(self_view), gather_open(cross_view)
    up_ag, down_ag = gather_open(up_view), gather_open(down_view)
    gather_far(self_ag)
    for state in (self_ag, cross_ag, up_ag, down_ag):
        gather_near(state)
    arrive(vec_seq)
    stacked = vec_all[...].reshape(data_count * seq_count * 16, LANES)
    row_of = lax.broadcasted_iota(jnp.int32, (LANES, width), 0)
    col_of = lax.broadcasted_iota(jnp.int32, (LANES, width), 1)
    spread = dot_plain(stacked, jnp.where(row_of == col_of % shard, 1.0, 0.0).astype(jnp.bfloat16))
    spread = spread.reshape(data_count * seq_count, 16, width)
    which = lax.broadcasted_iota(jnp.int32, spread.shape, 0)
    column = lax.broadcasted_iota(jnp.int32, spread.shape, 2)
    vec = m.vec
    vec[...] = jnp.sum(jnp.where(which == column // shard, spread, 0.0), axis=0)

    def vector(index):
        return vec[index : index + 1, :]

    h1, h2, h3, e1, e2 = m.h1, m.h2, m.h3, m.e1, m.e2
    h1[block(s, tokens)] = low(text_unit * vector(1) + vector(2))
    h1_ag = seq_gather(rows_of(h1))

    arrive(tile_dp)
    whole_place = block(s, inbox)
    m.units[...] = tiles[whole_place]
    tiles[whole_place] = low(wide(m.units[...]) * vector(5) + vector(6))
    whole_own = tiles.at[block(s, inbox)]
    tile_pair = [
        begin(whole_own, whole_own, (d, sibling)),
        begin(rest_in.at[s], rest_in.at[s], (d, sibling)),
    ]
    rest_far = begin(rest_in.at[s], rest_in.at[s], (d, across))
    quarter = inbox // 4

    def quarter_of(index, k):
        return tiles.at[pl.ds(pl.multiple_of(index * inbox + k * quarter, quarter), quarter)]

    def tile_send(k):
        part = quarter_of(s, k)
        return begin(part, part, (d, across))

    def tile_pass(k):
        tile_far[k].wait_recv()
        part = quarter_of(across, k)
        tile_pair.append(begin(part, part, (d, sibling)))

    tile_far = [tile_send(k) for k in range(4)]
    gather_step(out_ag, 0)
    gather_step(out_ag, 1)
    gather_step(self_ag, 0)
    gather_step(self_ag, 1)
    gather_step(out_ag, 2)
    gather_far(cross_ag)
    gather_far(up_ag)
    seq_pass(h1_ag)
    gather_end(out_ag)
    per_seq = data_count // seq_count
    out_in = m.out_in
    out_seq = []
    for peer in (across, corner, sibling):
        out_seq.append(
            begin(out_all.at[pl.ds(peer * per_seq, per_seq)], out_in.at[s], (d, peer))
        )
    out_in[s] = out_all[pl.ds(s * per_seq, per_seq)]
    gather_step(self_ag, 2)
    gather_end(self_ag)
    half_copy = half_swap(384)
    seq_end(h1_ag)
    qkv1, qm1, p1, o1 = m.qkv1, m.qm1, m.p1, m.o1
    qkv1[:, 0:384] = low(dot_plain(h1[...], cols[:, 384:768]))
    arrive([half_copy])
    qkv1[:, 384:768] = low(dot_plain(h1[...], half_cols(384, 384)))
    gather_step(cross_ag, 0)
    gather_step(cross_ag, 1)
    gather_far(down_ag)

    spot_q = lax.broadcasted_iota(jnp.int32, (length, length), 0)
    spot_k = lax.broadcasted_iota(jnp.int32, (length, length), 1)
    causal = spot_q >= spot_k
    mixed = []
    for head in range(3):
        base = 384 * (head // 2)
        qm = low(wide(qkv1[:, base : base + 128]) * head_masks[head])
        qm1[block(head, length)] = qm
        scores = dot_right(qm, qkv1[:, base + 128 : base + 256]) * factor
        scores = jnp.where(causal, scores, MASKED_SCORE)
        exponent = jnp.exp(scores - jnp.max(scores, axis=1, keepdims=True))
        chances = exponent / jnp.sum(exponent, axis=1, keepdims=True)
        p1[block(head, length)] = chances
        mixed.append(
            dot_plain(low(chances), qkv1[:, base + 256 : base + 384]) * head_masks[head]
        )
    o1[:, 0:128] = low(mixed[0] + mixed[1])
    o1[:, 128:256] = low(mixed[2])

    arrive(out_seq)
    out_rows = m.out_rows
    natural = jnp.concatenate(
        [wide(out_in[j, i]) for i in range(per_seq) for j in range(seq_count)], axis=0
    )
    blank = jnp.zeros((64, 2 * width), jnp.float32)
    even = jnp.concatenate([natural, blank], axis=0)
    odd = jnp.concatenate([natural[64:192], blank, natural[0:64]], axis=0)
    out_rows[...] = low(jnp.where(core == 0, even, odd))

    state = seq_sum_begin(0, lambda i, j: dot_plain(pick(o1, i, j), out_rows[:, 0:width]))
    state = seq_sum_pass(state)
    gather_step(cross_ag, 2)
    x2, x3, dx = m.x2, m.x3, m.dx
    second = wide(text[0]) + seq_sum_end(state)
    x2[...] = second
    unit, _ = norm_parts(second)
    h2[block(s, tokens)] = low(unit * vector(3) + vector(4))
    h2_ag = seq_gather(rows_of(h2))
    cot_ag = seq_gather(rows_of(cot_all))
    gather_step(up_ag, 0)
    gather_step(up_ag, 1)
    row_up = lax.broadcasted_iota(jnp.int32, (LANES, hidden), 0)
    col_up = lax.broadcasted_iota(jnp.int32, (LANES, hidden), 1)
    spread = dot_plain(stacked, jnp.where(row_up == col_up % band, 1.0, 0.0).astype(jnp.bfloat16))
    spread = spread.reshape(data_count * seq_count, 16, hidden)
    which = lax.broadcasted_iota(jnp.int32, spread.shape, 0)
    column = lax.broadcasted_iota(jnp.int32, spread.shape, 2)
    picked = jnp.where(which == (column // band) * seq_count + s, spread, 0.0)
    m.up_bias[...] = jnp.sum(picked, axis=0)[9:10]


    kv2, qm2, pr, o2, o_acc = m.kv2, m.qm2, m.pr, m.o2, m.o_acc

    def keys_values(here):
        rows = tiles[here]
        kv2[here, 0:256] = low(dot_plain(rows, cols[:, 128:384]))
        kv2[here, 256:512] = low(dot_plain(rows, half_cols(128, 256)))

    gather_end(cross_ag)
    half_copy = half_swap(0)
    arrive([half_copy])
    keys_values(block(s, inbox))
    tile_pass(0)
    seq_pass(h2_ag)
    arrive(tile_pair[0:2])
    keys_values(block(sibling, inbox))
    tile_pass(1)
    rest_far.wait_recv()
    tile_pair.append(begin(rest_in.at[across], rest_in.at[across], (d, sibling)))
    seq_end(h2_ag)
    query_full = dot_plain(h2[...], cols[:, 0:128])
    query_half = dot_plain(h2[...], half_cols(0, 128))
    for head in range(3):
        source = query_full if head < 2 else query_half
        qm2[block(head, length)] = low(wide(low(source)) * (head_masks[head] * factor))
    tile_pass(2)
    tile_pass(3)
    gather_step(up_ag, 2)
    gather_step(down_ag, 0)
    keys_values(block(across, inbox))
    arrive(tile_pair[2:])
    keys_values(block(corner, inbox))
    rest_wide[...] = wide(rest_in[...]).reshape(rest_wide.shape)
    for k in range(columns):
        place = slice(LANES * k, LANES * (k + 1))
        tiles[keys_main:keys, place] = low(
            rest_wide[pl.ds(k, rests, stride=16), :] * vec[5:6, place] + vec[6:7, place]
        )
    keys_values(pl.ds(keys_main, rests))
    gather_step(down_ag, 1)
    for head in range(3):
        base = 256 * (head // 2)
        place = 128 * (head // 2)

        here = block(head, length)
        scores = dot_right(qm2[here], kv2[:, base : base + 128]) + m.key_bias[...]
        exponent = jnp.exp(scores - jnp.max(scores, axis=1, keepdims=True))
        chances = low(exponent * (1.0 / jnp.sum(exponent, axis=1, keepdims=True)))
        pr[here] = chances
        result = dot_plain(chances, kv2[:, base + 128 : base + 256]) * head_masks[head]
        if head == 1:
            result = result + o_acc[:, place : place + 128]
        o_acc[:, place : place + 128] = result
        if head == 0:
            gather_step(down_ag, 2)

    o2[...] = low(o_acc[...])
    state = seq_sum_begin(
        1, lambda i, j: dot_plain(pick(o2, i, j), out_rows[:, width : 2 * width])
    )
    state = seq_sum_pass(state)
    third = x2[...] + seq_sum_end(state)
    x3[...] = third
    unit, _ = norm_parts(third)
    h3[block(s, tokens)] = low(unit * vector(7) + vector(8))
    h3_ag = seq_gather(rows_of(h3))
    seq_pass(cot_ag)
    seq_end(cot_ag)
    seq_pass(h3_ag)
    gather_end(down_ag)
    act, slope, du = m.act, m.slope, m.du
    slope[...] = dot_right(cot_all[...], down_all[...])
    gather_end(up_ag)
    seq_end(h3_ag)

    @pl.loop(0, seq_count)
    def _(i):
        here = block(i, tokens)
        pre = dot_plain(h3[here], cols[:, 768 : 768 + hidden]) + m.up_bias[...]
        cdf = 0.5 * (1.0 + lax.erf(pre * (1.0 / math.sqrt(2.0))))
        density = jnp.exp(-0.5 * pre * pre) * (1.0 / math.sqrt(2.0 * math.pi))
        act[here] = low(pre * cdf)
        grad = wide(low(slope[here]))
        du[here] = low(grad * (cdf + pre * density))

    state = seq_sum_begin(
        2, lambda i, j: dot_right(pick(du, i, j), cols[:, 768 : 768 + hidden])
    )
    state = seq_sum_pass(state)
    g_cols, g_down = m.g_cols, m.g_down
    g_down[...] = low(dot_left(act[...], cot_all[...]))
    g_down_view = lambda index: [g_down.at[block(index, band)]]
    down_rs = sum_begin(g_down_view, [m.y_down], [m.z_down])
    grad_mid = seq_sum_end(state)
    unit, inverse = norm_parts(x3[...])
    vv = m.vv
    vv[...] = jnp.zeros(vv.shape, jnp.float32)
    grad_out = wide(cot[0])
    dx3 = grad_out + norm_back(unit, inverse, vector(7), grad_mid)
    dx[...] = dx3
    e2[block(s, tokens)] = low(dx3)
    e2_ag = seq_gather(rows_of(e2))
    vv[0:1] = column_sum(grad_out)
    vv[7:8] = column_sum(grad_mid * unit)
    vv[8:9] = column_sum(grad_mid)
    vv[9:10, 0:hidden] = column_sum(wide(du[...]))

    g_cols[:, 768 : 768 + hidden] = low(dot_left(h3[...], du[...]))
    g_up_view = lambda index: [g_cols.at[block(index, band), lanes(768, hidden)]]
    up_rs = sum_begin(g_up_view, [m.y_up], [m.z_up])
    sum_step(down_rs, 0)
    seq_pass(e2_ag)
    sum_step(down_rs, 1)
    seq_end(e2_ag)

    dom = m.dom
    grad_o = low(dot_right(e2[...], out_rows[:, width : 2 * width]))
    for head in range(3):
        place = 128 * (head // 2)
        dom[block(head, length)] = low(wide(grad_o[:, place : place + 128]) * head_masks[head])
    ds, dkv2, dq2 = m.ds, m.dkv2, m.dq2
    for head in range(3):
        base = 256 * (head // 2)
        place = 128 * (head // 2)

        here = block(head, length)
        chances = wide(pr[here])
        grad_p = dot_right(dom[here], kv2[:, base + 128 : base + 256])
        weighted = jnp.sum(chances * grad_p, axis=1, keepdims=True)
        grad_s = low(chances * (grad_p - weighted))
        ds[here] = grad_s
        result = dot_plain(grad_s, kv2[:, base : base + 128]) * (head_masks[head] * factor)
        if head == 1:
            result = result + o_acc[:, place : place + 128]
        o_acc[:, place : place + 128] = result
        if head < 2:
            sum_step(down_rs, 2 + head)

    dq2[...] = low(o_acc[...])
    sum_step(up_rs, 0)
    state = seq_sum_begin(
        4,
        lambda i, j: dot_right(pick(dq2, i, j, slice(0, 128)), cols[:, 0:128])
        + dot_right(pick(dq2, i, j, slice(128, 256)), half_cols(0, 128)),
    )

    g_out, g_out_send = m.g_out, m.g_out_send

    def out_grad(slot, value):
        odd = jnp.concatenate([value[192:256], value[0:128]], axis=0)
        natural = jnp.where(core == 0, value[0:192], odd)
        for i in range(per_seq):
            for j in range(seq_count):
                start = shard * (i * seq_count + j)
                g_out_send[slot, j, i] = low(natural[start : start + shard])
        target = g_out.at[pl.ds(s * per_seq, per_seq), :, lanes(slot * width, width)]
        copies = [begin(g_out_send.at[slot, peer], target, (d, peer)) for peer in seq_peers]
        g_out[pl.ds(s * per_seq, per_seq), :, slot * width : (slot + 1) * width] = g_out_send[
            slot, s
        ]
        return copies

    xout_seq = out_grad(1, dot_left(o2[...], e2[...]))
    state = seq_sum_pass(state)
    for tile in range(2):
        first, count = (0, 2 * length) if tile == 0 else (2 * length, length)
        base = 256 * tile
        for start, size in spans(0, keys, 512):
            cut = slice(start, start + size)
            dkv2[cut, base : base + 128] = low(
                dot_left(ds[first : first + count, cut], qm2[first : first + count])
            )
            dkv2[cut, base + 128 : base + 256] = low(
                dot_left(pr[first : first + count, cut], dom[first : first + count])
            )
    sum_step(up_rs, 1)
    second_grad = seq_sum_end(state)
    unit, inverse = norm_parts(x2[...])
    dx2 = dx[...] + norm_back(unit, inverse, vector(3), second_grad)
    dx[...] = dx2
    e1[block(s, tokens)] = low(dx2)
    e1_ag = seq_gather(rows_of(e1))
    vv[3:4] = column_sum(second_grad * unit)
    vv[4:5] = column_sum(second_grad)
    sum_step(up_rs, 2)
    arrive(xout_seq)
    xout_view = lambda index: [g_out.at[index, :, lanes(width, width)]]
    xout_rs = sum_begin(xout_view, [m.y_xout], [m.z_xout])

    dn = m.dn

    def tile_grads(here):
        dn[here] = low(
            dot_right(dkv2[here, 0:256], cols[:, 128:384])
            + dot_right(dkv2[here, 256:512], half_cols(128, 256))
        )

    dr_out, dr_pair, dr_far, dr_home = m.dr_out, m.dr_pair, m.dr_far, m.dr_home
    dn_pair, dn_far, dn_home = m.dn_pair, m.dn_far, m.dn_home
    tile_grads(block(corner, inbox))
    pair_far = begin(dn.at[block(corner, inbox)], dn_pair.at[1], (d, sibling))
    tile_grads(pl.ds(keys_main, rests))
    rest_wide[...] = jnp.zeros(rest_wide.shape, jnp.float32)
    for k in range(columns):
        rest_wide[pl.ds(k, rests, stride=16), :] = wide(
            dn[keys_main:keys, LANES * k : LANES * (k + 1)]
        )
    dr_out[...] = low(rest_wide[...]).reshape(dr_out.shape)
    rest_pair = [
        begin(dr_out.at[peer], dr_pair.at[k], (d, sibling))
        for k, peer in enumerate((sibling, corner))
    ]
    tile_grads(block(across, inbox))
    seq_pass(e1_ag)
    pair_far.wait_recv()
    fold = dn.at[block(across, inbox)]
    fold[...] = low(wide(fold[...]) + wide(dn_pair[1]))
    arrive(rest_pair)
    dr_out[across] = low(wide(dr_out[across]) + wide(dr_pair[1]))
    rest_far = begin(dr_out.at[across], dr_far, (d, across))

    def far_send(k):
        return begin(quarter_in(dn, across, k), dn_far.at[block(k, quarter)], (d, across))

    def quarter_in(ref, index, k):
        return ref.at[pl.ds(pl.multiple_of(index * inbox + k * quarter, quarter), quarter)]

    far_copies = [far_send(k) for k in range(4)]
    sum_step(up_rs, 3)
    g_half, half_in, g_cross = m.g_half, m.half_in, m.g_cross
    half_shape = (data_count, 2, band // 2)

    def half_send(first):
        place = lanes(first, 384)
        return begin(g_half.at[:, 1 - core, :, place], half_in.at[:, :, place], (d, sibling))

    def half_add(first, copy):
        copy.wait_recv()
        place = lanes(first, 384)
        g_half[:, core, :, place] = low(
            wide(g_half[:, core, :, place]) + wide(half_in[:, :, place])
        )

    seq_end(e1_ag)
    grad_o = low(dot_right(e1[...], out_rows[:, 0:width]))
    grads = []
    dqkv = m.dqkv
    for head in range(3):
        base = 384 * (head // 2)
        place = 128 * (head // 2)
        here = block(head, length)
        dm = low(wide(grad_o[:, place : place + 128]) * head_masks[head])
        chances = p1[here]
        grad_p = dot_right(dm, qkv1[:, base + 256 : base + 384])
        weighted = jnp.sum(chances * grad_p, axis=1, keepdims=True)
        grad_s = low(chances * (grad_p - weighted))
        grads.append(
            (
                dot_plain(grad_s, qkv1[:, base + 128 : base + 256]) * (head_masks[head] * factor),
                dot_left(grad_s, qm1[here]) * factor,
                dot_left(low(chances), dm),
            )
        )
    for k in range(3):
        dqkv[:, 128 * k : 128 * k + 128] = low(grads[0][k] + grads[1][k])
        dqkv[:, 384 + 128 * k : 512 + 128 * k] = low(grads[2][k])
    state = seq_sum_begin(
        5,
        lambda i, j: dot_right(pick(dqkv, i, j, slice(0, 384)), cols[:, 384:768])
        + dot_right(pick(dqkv, i, j, slice(384, 768)), half_cols(384, 384)),
    )

    grad = dot_left(h1[...], dqkv[...])
    g_cols[:, 384:768] = low(grad[:, 0:384])
    g_half[:, :, :, 384:768] = low(grad[:, 384:768]).reshape(*half_shape, 384)
    half_copy = half_send(384)
    state = seq_sum_pass(state)
    sout_seq = out_grad(0, dot_left(o1[...], e1[...]))
    half_add(384, half_copy)
    self_rs = sum_begin(
        group_view(g_cols, g_half, 384),
        [m.y_full.at[:, :, lanes(384, 384)], m.y_half.at[:, :, lanes(384, 384)]],
        [m.z_full.at[:, :, lanes(384, 384)], m.z_half.at[:, :, lanes(384, 384)]],
    )
    tile_grads(block(sibling, inbox))
    pair_own = begin(dn.at[block(sibling, inbox)], dn_pair.at[0], (d, sibling))
    tile_grads(block(s, inbox))

    sum_middle(xout_rs)
    grad = dot_left(h2[...], dq2[...])
    g_cols[:, 0:128] = low(grad[:, 0:128])
    g_half[:, :, :, 0:128] = low(grad[:, 128:256]).reshape(*half_shape, 128)
    for cut in range(3):
        span = slice(256 * cut, 256 * cut + 256)
        grad = dot_left(tiles[:, span], dkv2[...])
        g_cols[span, 128:384] = low(grad[:, 0:256])
        g_cross[span] = low(grad[:, 256:512])
    g_half[:, :, :, 128:384] = g_cross[...].reshape(*half_shape, 256)
    half_copy = half_send(0)
    sum_step(self_rs, 0)
    half_add(0, half_copy)
    cross_rs = sum_begin(
        group_view(g_cols, g_half, 0),
        [m.y_full.at[:, :, lanes(0, 384)], m.y_half.at[:, :, lanes(0, 384)]],
        [m.z_full.at[:, :, lanes(0, 384)], m.z_half.at[:, :, lanes(0, 384)]],
    )
    sum_step(self_rs, 1)
    arrive([pair_own, rest_far])
    dr_out[s] = low(wide(dr_out[s]) + wide(dr_pair[0]) + wide(dr_far[...]))

    home_dp = []
    own_home = block(d, main)
    for k in range(4):
        far_copies[k].wait_recv()
        mine = quarter_in(dn, s, k)
        there = block(k, quarter)
        mine[...] = low(wide(mine[...]) + wide(dn_pair[0, there]) + wide(dn_far[there]))

    def home_send(k):
        peer = (d + k) % data_count
        source = dn.at[block(s * data_count + peer, main)]
        home_dp.append(begin(source, dn_home.at[own_home], (peer, s)))
        home_dp.append(begin(dr_out.at[s, peer], dr_home.at[d], (peer, s)))

    sum_step(self_rs, 2)
    for k in (2, 4, 6):
        home_send(k)
    sum_step(self_rs, 3)
    sum_step(cross_rs, 0)
    sum_step(cross_rs, 1)
    for k in (1, 3, 5, 7):
        home_send(k)
    dn_home[own_home] = dn[block(s * data_count + d, main)]
    dr_home[d] = dr_out[s, d]
    out_state = seq_sum_begin(3, lambda i, j: dot_plain(pick(act, i, j), down_all[...]))
    grad = wide(dn[block(s, inbox)])
    vv[5:6] = column_sum(grad * wide(m.units[...]))
    vv[6:7] = column_sum(grad)
    rest = wide(dr_out[s])
    for row, total in ((5, rest * wide(rest_in[s])), (6, rest)):
        total = jnp.sum(total, axis=0)
        total = jnp.concatenate([total[k : k + 1] for k in range(columns)], axis=1)
        vv[row : row + 1] = vv[row : row + 1] + total
    first_grad = seq_sum_end(state)
    unit, inverse = norm_parts(wide(text[0]))
    vv[1:2] = column_sum(first_grad * unit)
    vv[2:3] = column_sum(first_grad)
    r_tgrad[...] = low(dx[...] + norm_back(unit, inverse, vector(1), first_grad))
    vv_out, vv_in, vq = m.vv_out, m.vv_in, m.vq
    everything = vv[...]
    for p in range(data_count):
        turned = everything if p == 0 else pltpu.roll(everything, width - band * p, 1)
        vv_out[p] = turned[:, 0:LANES]
    vv_dp = []
    for k in range(1, data_count):
        peer = (d + k) % data_count
        vv_dp.append(begin(vv_out.at[peer], vv_in.at[d], (peer, s)))
    vv_in[d] = vv_out[d]
    arrive(sout_seq)
    sout_view = lambda index: [g_out.at[index, :, lanes(0, width)]]
    sout_rs = sum_begin(sout_view, [m.y_sout], [m.z_sout])
    out_state = seq_sum_pass(out_state)
    sum_step(cross_rs, 2)
    sum_step(cross_rs, 3)
    sum_middle(sout_rs)
    arrive(vv_dp)
    total = vv_in[0]
    for p in range(1, data_count):
        total = total + vv_in[p]
    vq[s] = total
    vq_seq = [begin(vq.at[s], vq.at[s], (d, peer)) for peer in seq_peers]
    bias_grad = total[9:10]
    r_text[...] = low(x3[...] + seq_sum_end(out_state) + vector(0))

    cols_out, cols_in, ends_out, ends_in = m.cols_out, m.cols_in, m.ends_out, m.ends_in

    def finish_cols(first, size, total):
        place = lanes(first, size)
        for j in range(seq_count):
            cols_out[j, :, place] = low(total[shard * j : shard * (j + 1)])
        cols_in[s, :, place] = cols_out[s, :, place]
        return [
            begin(cols_out.at[peer, :, place], cols_in.at[s, :, place], (d, peer))
            for peer in seq_peers
        ]

    def finish_half(first, total):
        place = lanes(first, 384)
        for j in range(2):
            ends_out[j, :, place] = low(total[shard * j : shard * (j + 1)])
        ends_in[s, :, place] = ends_out[core, :, place]
        return [
            begin(ends_out.at[peer % 2, :, place], ends_in.at[s, :, place], (d, peer))
            for peer in seq_peers
        ]

    (r_down[...],) = sum_end(down_rs)
    ends = finish_cols(768, hidden, sum_end(up_rs)[0])
    (r_outs[1],) = sum_end(xout_rs)
    full, half = sum_end(self_rs)
    ends += finish_cols(384, 384, full) + finish_half(384, half)

    arrive(home_dp)
    for t in range(tile_count):
        grad = wide(dn_home[block(0, main)]) * route[0][t]
        rest = wide(dr_home[0]) * route[0][t]
        for p in range(1, data_count):
            grad = grad + wide(dn_home[block(p, main)]) * route[p][t]
            rest = rest + wide(dr_home[p]) * route[p][t]
        rest = jnp.concatenate([rest[k : k + 1] for k in range(columns)], axis=1)
        unit, inverse = norm_parts(wide(img[t, 0:main]))
        r_igrad[t, 0:main] = low(norm_back(unit, inverse, vector(5), grad))
        unit, inverse = norm_parts(wide(img[t, main:real_rows]))
        r_igrad[t, main:real_rows] = low(norm_back(unit, inverse, vector(5), rest))


    full, half = sum_end(cross_rs)
    ends += finish_cols(0, 384, full) + finish_half(0, half)
    (r_outs[0],) = sum_end(sout_rs)

    arrive(ends)
    r_cols[...] = cols_in[...]
    r_half[...] = ends_in[...]
    arrive(vq_seq)
    total = vq[0] + vq[1] + vq[2] + vq[3]
    r_vec[...] = pltpu.roll(total, (LANES - shard * s) % LANES, 1)
    r_vec[9:10] = bias_grad

    for copy in links.started:
        copy.wait_send()


def unpack_kernel(t_out, t_grad, i_grad, cols, ends, outs, down, vec, *results):
    o_text, o_tgrad, o_igrad, o_q, o_k, o_v, o_o, o_xq, o_xk, o_xv, o_xo, o_up, o_down, *vectors = (
        results
    )
    seq_count, shard, total = cols.shape
    hidden = total - 768
    core = lax.axis_index("seq") // 2
    band = down.shape[0]
    o_text[0] = t_out[...]
    o_tgrad[0] = t_grad[...]
    o_igrad[...] = i_grad[...]
    for k, result in enumerate((o_xq, o_xk, o_xv, o_q, o_k, o_v)):
        here = slice(LANES * k, LANES * (k + 1))
        for j, tile in ((0, 0), (1, 2), (2, 3), (3, 5)):
            result[:, LANES * tile : LANES * (tile + 1)] = wide(cols[j, :, here])
        for j, tile in ((0, 1), (2, 4)):
            result[:, LANES * tile : LANES * (tile + 1)] = wide(ends[j + core, :, here])
    o_o[...] = outs[0]
    o_xo[...] = outs[1]
    o_down[...] = down[...]
    lane = lax.broadcasted_iota(jnp.int32, (1, LANES), 1)
    parts = [wide(cols[j, :, 768:total]) for j in range(seq_count)]
    for tile in range(hidden * seq_count // LANES):
        pieces = []
        for at, size in spans(LANES * tile, LANES * tile + LANES, band):
            group = at // band
            first = band * (group // seq_count) + at % band
            pieces.append((parts[group % seq_count], first, at % LANES, size))
        o_up[:, LANES * tile : LANES * (tile + 1)] = lane_pick(pieces, lane)
    vectors[0][...] = vec[9, 0:band]
    for k, result in enumerate(vectors[1:]):
        result[...] = vec[k, 0:shard]


def fused_device(
    text_in, image_in, tile_slide, owner_map, text_cot,
    w_query, w_key, w_value, w_out, c_query, c_key, c_value, c_out, w_up, w_down, b_up, b_down,
    self_gain, self_shift, cross_gain, cross_shift, tile_gain, tile_shift, mlp_gain, mlp_shift,
):
    data_count, seq_count = lax.axis_size("dp"), lax.axis_size("seq")
    tile_count, real_rows, width = image_in.shape
    tokens = text_in.shape[1]
    shard = w_query.shape[0]
    band = shard * seq_count
    hidden = w_up.shape[1] // seq_count
    main = real_rows // 16 * 16

    gains = (
        self_gain, self_shift, cross_gain, cross_shift, tile_gain, tile_shift, mlp_gain, mlp_shift,
    )
    inputs = (
        tile_slide, owner_map, text_in, image_in, text_cot, w_query, w_key, w_value, w_out,
        c_query, c_key, c_value, c_out, w_up, w_down,
        *[member.reshape(1, -1) for member in (b_up, b_down, *gains)],
    )
    in_specs = [pl.BlockSpec(memory_space=pltpu.SMEM)] * 2
    in_specs += [pl.BlockSpec(memory_space=pltpu.VMEM)] * (len(inputs) - 2)
    row_out = jax.ShapeDtypeStruct((tokens, width), jnp.bfloat16)
    packed_shape = [
        row_out,
        row_out,
        jax.ShapeDtypeStruct(image_in.shape, jnp.bfloat16),
        jax.ShapeDtypeStruct((seq_count, shard, 768 + hidden), jnp.bfloat16),
        jax.ShapeDtypeStruct((seq_count, shard, 768), jnp.bfloat16),
        jax.ShapeDtypeStruct((2, shard, width), jnp.float32),
        jax.ShapeDtypeStruct((band, width), jnp.float32),
        jax.ShapeDtypeStruct((16, LANES), jnp.float32),
    ]
    shapes = scratch_of(width, tokens, seq_count, data_count, hidden, main, shard)
    scratch = [pltpu.VMEM(shape, kind) for shape, kind in shapes.values()]
    scratch += [pltpu.SemaphoreType.DMA((COPY_SLOTS,))] * 2
    names = [*shapes, "send", "recv"]
    packed = pl.pallas_call(
        partial(fused_kernel, names, len(inputs)),
        out_shape=packed_shape,
        in_specs=in_specs,
        out_specs=[pl.BlockSpec(memory_space=pltpu.VMEM)] * len(packed_shape),
        scratch_shapes=scratch,
        compiler_params=pltpu.CompilerParams(
            collective_id=0, has_side_effects=True, vmem_limit_bytes=60 * 1024 * 1024
        ),
        name="decoder_layer",
    )(*inputs)
    square = jax.ShapeDtypeStruct((shard, width), jnp.float32)
    out_shape = [
        jax.ShapeDtypeStruct(text_in.shape, jnp.bfloat16),
        jax.ShapeDtypeStruct(text_in.shape, jnp.bfloat16),
        jax.ShapeDtypeStruct(image_in.shape, jnp.bfloat16),
        *[square] * 8,
        jax.ShapeDtypeStruct((shard, hidden * seq_count), jnp.float32),
        jax.ShapeDtypeStruct((band, width), jnp.float32),
        jax.ShapeDtypeStruct((band,), jnp.float32),
        *[jax.ShapeDtypeStruct((shard,), jnp.float32)] * 9,
    ]
    return tuple(
        pl.pallas_call(
            unpack_kernel,
            out_shape=out_shape,
            in_specs=[pl.BlockSpec(memory_space=pltpu.VMEM)] * len(packed),
            out_specs=[pl.BlockSpec(memory_space=pltpu.VMEM)] * len(out_shape),
            name="unpack",
        )(*packed)
    )


def fused_fits(mesh):
    return mesh.shape["seq"] == 4 and 768 % (8 * mesh.shape["dp"] * mesh.shape["seq"]) == 0


def solution(mesh):
    placed = (
        P("dp", "seq", None),
        P("dp", "seq", None),
        P(),
        P(),
        P("dp", "seq", None),
        P(("dp", "seq"), None),
        P(("dp", "seq"), None),
        P(("dp", "seq"), None),
        P(("dp", "seq"), None),
        P(("dp", "seq"), None),
        P(("dp", "seq"), None),
        P(("dp", "seq"), None),
        P(("dp", "seq"), None),
        P(("dp", "seq"), None),
        P(("dp", "seq"), None),
        P(("dp", "seq")),
        P(("dp", "seq")),
        P(("dp", "seq")),
        P(("dp", "seq")),
        P(("dp", "seq")),
        P(("dp", "seq")),
        P(("dp", "seq")),
        P(("dp", "seq")),
        P(("dp", "seq")),
        P(("dp", "seq")),
    )
    return jax.shard_map(
        fused_device if fused_fits(mesh) else per_device,
        mesh=mesh,
        in_specs=placed,
        out_specs=(
            P("dp", "seq", None),
            P("dp", "seq", None),
            P("dp", "seq", None),
            P(("dp", "seq"), None),
            P(("dp", "seq"), None),
            P(("dp", "seq"), None),
            P(("dp", "seq"), None),
            P(("dp", "seq"), None),
            P(("dp", "seq"), None),
            P(("dp", "seq"), None),
            P(("dp", "seq"), None),
            P(("dp", "seq"), None),
            P(("dp", "seq"), None),
            P(("dp", "seq")),
            P(("dp", "seq")),
            P(("dp", "seq")),
            P(("dp", "seq")),
            P(("dp", "seq")),
            P(("dp", "seq")),
            P(("dp", "seq")),
            P(("dp", "seq")),
            P(("dp", "seq")),
            P(("dp", "seq")),
        ),
        check_vma=False,
    )
```

```python
from functools import partial
import math
from types import SimpleNamespace

import jax
import jax.numpy as jnp
from jax import lax
from jax.experimental import pallas as pl
from jax.experimental.pallas import tpu as pltpu
from jax.sharding import PartitionSpec as P

HEAD = 64
LANES = 128
MESH = pl.DeviceIdType.MESH


EPSILON = 1e-05
MASKED_SCORE = -1e30


def combined_all(x, axis, combine):
    everything = jax.tree.map(lambda part: lax.all_gather(part, axis), x)
    initial = jax.tree.map(lambda part: part[0], everything)

    def step(k, so_far):
        return combine(so_far, jax.tree.map(lambda part: part[k], everything))

    return lax.fori_loop(1, lax.axis_size(axis), step, initial)


def norm_rows(values, gain_row, shift_row):
    average = jnp.mean(values, axis=-1, keepdims=True)
    centered = values - average
    spread = jnp.mean(centered * centered, axis=-1, keepdims=True)
    return centered * lax.rsqrt(spread + EPSILON) * gain_row + shift_row


def matmul(former, latter):
    return jnp.dot(former, latter, preferred_element_type=jnp.float32)


def matmul_trans(former, latter):
    return lax.dot_general(
        former, latter, (((1,), (1,)), ((), ())), preferred_element_type=jnp.float32
    )


def outer_sum(former, latter):
    return lax.dot_general(
        former, latter, (((0,), (0,)), ((), ())), preferred_element_type=jnp.float32
    )


def head_pair(matrix, pair_index):
    columns = lax.dynamic_slice_in_dim(matrix, pair_index * 2 * HEAD, 2 * HEAD, 1)
    return columns.reshape(columns.shape[0], 2, HEAD)


def put_pair(matrix, update, pair_index):
    return lax.dynamic_update_slice_in_dim(
        matrix, update.reshape(update.shape[0], 2 * HEAD), pair_index * 2 * HEAD, 1
    )


def pick_pair(stacked, pair_index):
    return lax.dynamic_index_in_dim(stacked, pair_index, 0, keepdims=False)


def pair_scores(query_rows, key_rows, allowed, pair_index):
    factor = 1.0 / math.sqrt(HEAD)
    scores = (
        jnp.einsum(
            "qhd,khd->hqk",
            head_pair(query_rows, pair_index),
            head_pair(key_rows, pair_index),
            preferred_element_type=jnp.float32,
        )
        * factor
    )
    return jnp.where(allowed[None], scores, MASKED_SCORE)


def attend_stats(query_rows, key_rows, allowed):
    pair_count = query_rows.shape[1] // (2 * HEAD)

    def one_pair(pair_index, state_now):
        row_max, row_sum = state_now
        scores = pair_scores(query_rows, key_rows, allowed, pair_index)
        highest = jnp.max(scores, axis=2)
        summed = jnp.sum(jnp.exp(scores - highest[..., None]), axis=2)
        return (
            lax.dynamic_update_index_in_dim(row_max, highest, pair_index, 0),
            lax.dynamic_update_index_in_dim(row_sum, summed, pair_index, 0),
        )

    empty_stats = jnp.zeros((pair_count, 2, query_rows.shape[0]), jnp.float32)
    return lax.fori_loop(0, pair_count, one_pair, (empty_stats, empty_stats))


def attend_forward(query_rows, key_rows, value_rows, allowed, maxima, totals):
    pair_count = query_rows.shape[1] // (2 * HEAD)
    stats_given = maxima is not None
    if not stats_given:
        maxima = jnp.zeros((pair_count, 2, query_rows.shape[0]), jnp.float32)
        totals = jnp.zeros_like(maxima)

    def one_pair(pair_index, state_now):
        output, row_max, row_sum = state_now
        scores = pair_scores(query_rows, key_rows, allowed, pair_index)
        if stats_given:
            highest = pick_pair(row_max, pair_index)
            exponent = jnp.exp(scores - highest[..., None])
            summed = pick_pair(row_sum, pair_index)
        else:
            highest = jnp.max(scores, axis=2)
            exponent = jnp.exp(scores - highest[..., None])
            summed = jnp.sum(exponent, axis=2)
            row_max = lax.dynamic_update_index_in_dim(row_max, highest, pair_index, 0)
            row_sum = lax.dynamic_update_index_in_dim(row_sum, summed, pair_index, 0)
        weights = (exponent / summed[..., None]).astype(jnp.bfloat16)
        mixture = jnp.einsum(
            "hqk,khd->qhd",
            weights,
            head_pair(value_rows, pair_index),
            preferred_element_type=jnp.float32,
        )
        return (put_pair(output, mixture, pair_index), row_max, row_sum)

    start_state = (jnp.zeros(query_rows.shape, jnp.float32), maxima, totals)
    return lax.fori_loop(0, pair_count, one_pair, start_state)


def attend_rowsums(query_rows, key_rows, value_rows, allowed, maxima, totals, grad_rows):
    pair_count = query_rows.shape[1] // (2 * HEAD)

    def one_pair(pair_index, row_terms):
        scores = pair_scores(query_rows, key_rows, allowed, pair_index)
        chances = (
            jnp.exp(scores - pick_pair(maxima, pair_index)[..., None])
            / pick_pair(totals, pair_index)[..., None]
        )
        grad_chances = jnp.einsum(
            "qhd,khd->hqk",
            head_pair(grad_rows, pair_index),
            head_pair(value_rows, pair_index),
            preferred_element_type=jnp.float32,
        )
        return lax.dynamic_update_index_in_dim(
            row_terms, jnp.sum(chances * grad_chances, axis=2), pair_index, 0
        )

    return lax.fori_loop(0, pair_count, one_pair, jnp.zeros_like(maxima))


def attend_backward(
    query_rows, key_rows, value_rows, allowed, maxima, totals, grad_rows, row_terms
):
    pair_count = query_rows.shape[1] // (2 * HEAD)
    factor = 1.0 / math.sqrt(HEAD)

    def one_pair(pair_index, state_now):
        grad_query, grad_key, grad_value = state_now
        scores = pair_scores(query_rows, key_rows, allowed, pair_index)
        chances = (
            jnp.exp(scores - pick_pair(maxima, pair_index)[..., None])
            / pick_pair(totals, pair_index)[..., None]
        )
        grad_heads = head_pair(grad_rows, pair_index)
        grad_chances = jnp.einsum(
            "qhd,khd->hqk",
            grad_heads,
            head_pair(value_rows, pair_index),
            preferred_element_type=jnp.float32,
        )
        if row_terms is None:
            weighted = jnp.sum(chances * grad_chances, axis=2)
        else:
            weighted = pick_pair(row_terms, pair_index)
        grad_scores = (chances * (grad_chances - weighted[..., None])).astype(jnp.bfloat16)
        query_part = (
            jnp.einsum(
                "hqk,khd->qhd",
                grad_scores,
                head_pair(key_rows, pair_index),
                preferred_element_type=jnp.float32,
            )
            * factor
        )
        key_part = (
            jnp.einsum(
                "hqk,qhd->khd",
                grad_scores,
                head_pair(query_rows, pair_index),
                preferred_element_type=jnp.float32,
            )
            * factor
        )
        value_part = jnp.einsum(
            "hqk,qhd->khd",
            chances.astype(jnp.bfloat16),
            grad_heads,
            preferred_element_type=jnp.float32,
        )
        return (
            put_pair(grad_query, query_part, pair_index),
            put_pair(grad_key, key_part, pair_index),
            put_pair(grad_value, value_part, pair_index),
        )

    start_state = (
        jnp.zeros(query_rows.shape, jnp.float32),
        jnp.zeros(key_rows.shape, jnp.float32),
        jnp.zeros(value_rows.shape, jnp.float32),
    )
    return lax.fori_loop(0, pair_count, one_pair, start_state)


def join_stats(former, latter):
    highest = jnp.maximum(former[0], latter[0])
    return (
        highest,
        former[1] * jnp.exp(former[0] - highest) + latter[1] * jnp.exp(latter[0] - highest),
    )


def split_rows(matrix, data_count, seq_count):
    return matrix.reshape(
        data_count, seq_count, matrix.shape[0] // (data_count * seq_count), matrix.shape[1]
    )


def fold_rows(pieces):
    return jnp.sum(pieces, axis=1).reshape(pieces.shape[0] * pieces.shape[2], pieces.shape[3])


def per_device(
    text_in,
    image_in,
    tile_slide,
    owner_map,
    text_cot,
    w_query,
    w_key,
    w_value,
    w_out,
    c_query,
    c_key,
    c_value,
    c_out,
    w_up,
    w_down,
    b_up,
    b_down,
    self_gain,
    self_shift,
    cross_gain,
    cross_shift,
    tile_gain,
    tile_shift,
    mlp_gain,
    mlp_shift,
):
    gathered = (
        lax.all_gather(w_query, ("dp", "seq"), axis=0, tiled=True),
        lax.all_gather(w_key, ("dp", "seq"), axis=0, tiled=True),
        lax.all_gather(w_value, ("dp", "seq"), axis=0, tiled=True),
        lax.all_gather(w_out, ("dp", "seq"), axis=0, tiled=True),
        lax.all_gather(c_query, ("dp", "seq"), axis=0, tiled=True),
        lax.all_gather(c_key, ("dp", "seq"), axis=0, tiled=True),
        lax.all_gather(c_value, ("dp", "seq"), axis=0, tiled=True),
        lax.all_gather(c_out, ("dp", "seq"), axis=0, tiled=True),
        lax.all_gather(w_up, ("dp", "seq"), axis=0, tiled=True),
        lax.all_gather(w_down, ("dp", "seq"), axis=0, tiled=True),
        lax.all_gather(b_up, ("dp", "seq"), axis=0, tiled=True),
        lax.all_gather(b_down, ("dp", "seq"), axis=0, tiled=True),
        lax.all_gather(self_gain, ("dp", "seq"), axis=0, tiled=True),
        lax.all_gather(self_shift, ("dp", "seq"), axis=0, tiled=True),
        lax.all_gather(cross_gain, ("dp", "seq"), axis=0, tiled=True),
        lax.all_gather(cross_shift, ("dp", "seq"), axis=0, tiled=True),
        lax.all_gather(tile_gain, ("dp", "seq"), axis=0, tiled=True),
        lax.all_gather(tile_shift, ("dp", "seq"), axis=0, tiled=True),
        lax.all_gather(mlp_gain, ("dp", "seq"), axis=0, tiled=True),
        lax.all_gather(mlp_shift, ("dp", "seq"), axis=0, tiled=True),
    )
    query_mat, key_mat, value_mat, proj_mat = (gathered[0], gathered[1], gathered[2], gathered[3])
    xquery_mat, xkey_mat, xvalue_mat, xproj_mat = (
        gathered[4],
        gathered[5],
        gathered[6],
        gathered[7],
    )
    up_mat, down_mat = (gathered[8], gathered[9])
    vectors = [member.astype(jnp.float32) for member in gathered[10:]]
    (
        up_bias,
        down_bias,
        gain_one,
        shift_one,
        gain_two,
        shift_two,
        gain_tile,
        shift_tile,
        gain_three,
        shift_three,
    ) = vectors
    text_rows = text_in[0].astype(jnp.float32)
    rows_here = text_rows.shape[0]
    hidden_dim = text_rows.shape[1]
    normed_one, norm_one_back = jax.vjp(norm_rows, text_rows, gain_one, shift_one)
    first_in = normed_one.astype(jnp.bfloat16)
    query_one = matmul(first_in, query_mat).astype(jnp.bfloat16)
    key_one = matmul(first_in, key_mat).astype(jnp.bfloat16)
    value_one = matmul(first_in, value_mat).astype(jnp.bfloat16)
    key_all, value_all = (
        lax.all_gather(key_one, "seq", axis=0, tiled=True),
        lax.all_gather(value_one, "seq", axis=0, tiled=True),
    )
    positions = lax.axis_index("seq") * rows_here + jnp.arange(rows_here)
    causal = positions[:, None] >= jnp.arange(key_all.shape[0])[None, :]
    attend_one, max_one, sum_one = attend_forward(query_one, key_all, value_all, causal, None, None)
    mixed_one = attend_one.astype(jnp.bfloat16)
    second = text_rows + matmul(mixed_one, proj_mat)
    normed_two, norm_two_back = jax.vjp(norm_rows, second, gain_two, shift_two)
    second_in = normed_two.astype(jnp.bfloat16)
    query_two = matmul(second_in, xquery_mat).astype(jnp.bfloat16)
    tile_rows = image_in.astype(jnp.float32)
    normed_tiles, norm_tile_back = jax.vjp(norm_rows, tile_rows, gain_tile, shift_tile)
    tiles_in = normed_tiles.astype(jnp.bfloat16)
    data_index = lax.axis_index("dp")
    data_count = lax.axis_size("dp")
    seq_count = lax.axis_size("seq")
    tile_count = image_in.shape[0]
    slot_rows = image_in.shape[1]
    slide_ids = jnp.arange(owner_map.shape[0])
    destination = jnp.sum(
        jnp.where(tile_slide[:, None] == slide_ids[None, :], owner_map[None, :], 0), axis=1
    )
    own_destination = lax.dynamic_slice_in_dim(destination, data_index * tile_count, tile_count)
    routing = (own_destination[None, :] == jnp.arange(data_count)[:, None]).astype(jnp.bfloat16)
    outgoing = jnp.einsum(
        "pt,trd->prd", routing, tiles_in, preferred_element_type=jnp.float32
    ).astype(jnp.bfloat16)
    incoming = lax.all_to_all(outgoing, "dp", split_axis=0, concat_axis=0, tiled=True)
    arrived = jnp.any(destination.reshape(data_count, tile_count) == data_index, axis=1)
    flat_in = incoming.reshape(data_count * slot_rows, hidden_dim)
    allowed_rows = jnp.broadcast_to(arrived[:, None], (data_count, slot_rows)).reshape(-1)
    key_two = matmul(flat_in, xkey_mat).astype(jnp.bfloat16)
    value_two = matmul(flat_in, xvalue_mat).astype(jnp.bfloat16)
    query_far = lax.all_gather(query_two, "seq", axis=0, tiled=True)
    allowed_near = allowed_rows[None, :]
    local_max, local_sum = attend_stats(query_far, key_two, allowed_near)
    max_two, sum_two = combined_all((local_max, local_sum), "seq", join_stats)
    partial_rows = attend_forward(query_far, key_two, value_two, allowed_near, max_two, sum_two)[0]
    attend_two = lax.psum_scatter(
        partial_rows.astype(jnp.bfloat16), "seq", scatter_dimension=0, tiled=True
    )
    third_sum = second + matmul(attend_two, xproj_mat)
    normed_three, norm_three_back = jax.vjp(norm_rows, third_sum, gain_three, shift_three)
    third_in = normed_three.astype(jnp.bfloat16)
    pre_gelu = matmul(third_in, up_mat) + up_bias
    activated, gelu_back = jax.vjp(partial(jax.nn.gelu, approximate=False), pre_gelu)
    act_in = activated.astype(jnp.bfloat16)
    result = third_sum + matmul(act_in, down_mat) + down_bias
    text_out = result.astype(jnp.bfloat16)[None]
    cot_rows = text_cot[0]
    grad_res = cot_rows.astype(jnp.float32)
    down_grad = outer_sum(act_in, cot_rows)
    downbias_grad = jnp.sum(grad_res, axis=0)
    grad_act = matmul_trans(cot_rows, down_mat).astype(jnp.bfloat16)
    grad_pre = gelu_back(grad_act.astype(jnp.float32))[0].astype(jnp.bfloat16)
    up_grad = outer_sum(third_in, grad_pre)
    upbias_grad = jnp.sum(grad_pre.astype(jnp.float32), axis=0)
    grad_mid, mgain_grad, mshift_grad = norm_three_back(matmul_trans(grad_pre, up_mat))
    grad_third = grad_res + grad_mid
    branch_two = grad_third.astype(jnp.bfloat16)
    xproj_grad = outer_sum(attend_two, branch_two)
    grad_attend_two = matmul_trans(branch_two, xproj_mat).astype(jnp.bfloat16)
    grad_far = lax.all_gather(grad_attend_two, "seq", axis=0, tiled=True)
    row_part = attend_rowsums(
        query_far, key_two, value_two, allowed_near, max_two, sum_two, grad_far
    )
    row_terms = lax.psum(row_part, "seq")
    query_grad_far, key_grad_two, value_grad_two = attend_backward(
        query_far, key_two, value_two, allowed_near, max_two, sum_two, grad_far, row_terms
    )
    query_grad_two = lax.psum_scatter(
        query_grad_far.astype(jnp.bfloat16), "seq", scatter_dimension=0, tiled=True
    )
    gkey_two = key_grad_two.astype(jnp.bfloat16)
    gvalue_two = value_grad_two.astype(jnp.bfloat16)
    xquery_grad = outer_sum(second_in, query_grad_two)
    xkey_grad = outer_sum(flat_in, gkey_two)
    xvalue_grad = outer_sum(flat_in, gvalue_two)
    grad_flat = (matmul_trans(gkey_two, xkey_mat) + matmul_trans(gvalue_two, xvalue_mat)).astype(
        jnp.bfloat16
    )
    grad_home = lax.all_to_all(
        grad_flat.reshape(data_count, slot_rows, hidden_dim),
        "dp",
        split_axis=0,
        concat_axis=0,
        tiled=True,
    )
    grad_tiles = jnp.einsum("pt,prd->trd", routing, grad_home, preferred_element_type=jnp.float32)
    image_back, tgain_grad, tshift_grad = norm_tile_back(grad_tiles)
    image_grad = image_back.astype(jnp.bfloat16)
    grad_mid_two, xgain_grad, xshift_grad = norm_two_back(matmul_trans(query_grad_two, xquery_mat))
    grad_second = grad_third + grad_mid_two
    branch_one = grad_second.astype(jnp.bfloat16)
    proj_grad = outer_sum(mixed_one, branch_one)
    grad_attend_one = matmul_trans(branch_one, proj_mat).astype(jnp.bfloat16)
    query_grad_one, key_grad_all, value_grad_all = attend_backward(
        query_one, key_all, value_all, causal, max_one, sum_one, grad_attend_one, None
    )
    key_grad_one, value_grad_one = (
        lax.psum_scatter(
            key_grad_all.astype(jnp.bfloat16), "seq", scatter_dimension=0, tiled=True
        ).astype(jnp.float32),
        lax.psum_scatter(
            value_grad_all.astype(jnp.bfloat16), "seq", scatter_dimension=0, tiled=True
        ).astype(jnp.float32),
    )
    gquery_one = query_grad_one.astype(jnp.bfloat16)
    gkey_one = key_grad_one.astype(jnp.bfloat16)
    gvalue_one = value_grad_one.astype(jnp.bfloat16)
    query_grad = outer_sum(first_in, gquery_one)
    key_grad = outer_sum(first_in, gkey_one)
    value_grad = outer_sum(first_in, gvalue_one)
    grad_norm_one = (
        matmul_trans(gquery_one, query_mat)
        + matmul_trans(gkey_one, key_mat)
        + matmul_trans(gvalue_one, value_mat)
    )
    grad_mid_one, sgain_grad, sshift_grad = norm_one_back(grad_norm_one)
    text_grad = (grad_second + grad_mid_one).astype(jnp.bfloat16)[None]
    pieces = (
        lax.all_to_all(
            split_rows(query_grad, data_count, seq_count).astype(jnp.bfloat16),
            "seq",
            split_axis=1,
            concat_axis=1,
            tiled=True,
        ).astype(jnp.float32),
        lax.all_to_all(
            split_rows(key_grad, data_count, seq_count).astype(jnp.bfloat16),
            "seq",
            split_axis=1,
            concat_axis=1,
            tiled=True,
        ).astype(jnp.float32),
        lax.all_to_all(
            split_rows(value_grad, data_count, seq_count).astype(jnp.bfloat16),
            "seq",
            split_axis=1,
            concat_axis=1,
            tiled=True,
        ).astype(jnp.float32),
        lax.all_to_all(
            split_rows(proj_grad, data_count, seq_count).astype(jnp.bfloat16),
            "seq",
            split_axis=1,
            concat_axis=1,
            tiled=True,
        ).astype(jnp.float32),
        lax.all_to_all(
            split_rows(xquery_grad, data_count, seq_count).astype(jnp.bfloat16),
            "seq",
            split_axis=1,
            concat_axis=1,
            tiled=True,
        ).astype(jnp.float32),
        lax.all_to_all(
            split_rows(xkey_grad, data_count, seq_count).astype(jnp.bfloat16),
            "seq",
            split_axis=1,
            concat_axis=1,
            tiled=True,
        ).astype(jnp.float32),
        lax.all_to_all(
            split_rows(xvalue_grad, data_count, seq_count).astype(jnp.bfloat16),
            "seq",
            split_axis=1,
            concat_axis=1,
            tiled=True,
        ).astype(jnp.float32),
        lax.all_to_all(
            split_rows(xproj_grad, data_count, seq_count).astype(jnp.bfloat16),
            "seq",
            split_axis=1,
            concat_axis=1,
            tiled=True,
        ).astype(jnp.float32),
        lax.all_to_all(
            split_rows(up_grad, data_count, seq_count).astype(jnp.bfloat16),
            "seq",
            split_axis=1,
            concat_axis=1,
            tiled=True,
        ).astype(jnp.float32),
        lax.all_to_all(
            split_rows(down_grad, data_count, seq_count).astype(jnp.bfloat16),
            "seq",
            split_axis=1,
            concat_axis=1,
            tiled=True,
        ).astype(jnp.float32),
    )
    folded = [fold_rows(member) for member in pieces]
    summed_mats = (
        lax.psum_scatter(folded[0], "dp", scatter_dimension=0, tiled=True),
        lax.psum_scatter(folded[1], "dp", scatter_dimension=0, tiled=True),
        lax.psum_scatter(folded[2], "dp", scatter_dimension=0, tiled=True),
        lax.psum_scatter(folded[3], "dp", scatter_dimension=0, tiled=True),
        lax.psum_scatter(folded[4], "dp", scatter_dimension=0, tiled=True),
        lax.psum_scatter(folded[5], "dp", scatter_dimension=0, tiled=True),
        lax.psum_scatter(folded[6], "dp", scatter_dimension=0, tiled=True),
        lax.psum_scatter(folded[7], "dp", scatter_dimension=0, tiled=True),
        lax.psum_scatter(folded[8], "dp", scatter_dimension=0, tiled=True),
        lax.psum_scatter(folded[9], "dp", scatter_dimension=0, tiled=True),
    )
    summed_vecs = (
        lax.psum_scatter(upbias_grad, ("dp", "seq"), scatter_dimension=0, tiled=True),
        lax.psum_scatter(downbias_grad, ("dp", "seq"), scatter_dimension=0, tiled=True),
        lax.psum_scatter(sgain_grad, ("dp", "seq"), scatter_dimension=0, tiled=True),
        lax.psum_scatter(sshift_grad, ("dp", "seq"), scatter_dimension=0, tiled=True),
        lax.psum_scatter(xgain_grad, ("dp", "seq"), scatter_dimension=0, tiled=True),
        lax.psum_scatter(xshift_grad, ("dp", "seq"), scatter_dimension=0, tiled=True),
        lax.psum_scatter(tgain_grad, ("dp", "seq"), scatter_dimension=0, tiled=True),
        lax.psum_scatter(tshift_grad, ("dp", "seq"), scatter_dimension=0, tiled=True),
        lax.psum_scatter(mgain_grad, ("dp", "seq"), scatter_dimension=0, tiled=True),
        lax.psum_scatter(mshift_grad, ("dp", "seq"), scatter_dimension=0, tiled=True),
    )
    return (text_out, text_grad, image_grad) + tuple(summed_mats) + tuple(summed_vecs)


def dot_plain(former, latter):
    return jnp.dot(former, latter, preferred_element_type=jnp.float32)


def dot_right(former, latter):
    return lax.dot_general(
        former, latter, (((1,), (1,)), ((), ())), preferred_element_type=jnp.float32
    )


def dot_left(former, latter):
    return lax.dot_general(
        former, latter, (((0,), (0,)), ((), ())), preferred_element_type=jnp.float32
    )


def low(values):
    return values.astype(jnp.bfloat16)


def wide(values):
    return values.astype(jnp.float32)


def block(index, size):
    if isinstance(index, int):
        return pl.ds(index * size, size)
    return pl.ds(pl.multiple_of(index * size, size), size)


def lanes(start, size):
    return pl.ds(start, size)


def norm_parts(values):
    average = jnp.mean(values, axis=-1, keepdims=True)
    centered = values - average
    spread = jnp.mean(centered * centered, axis=-1, keepdims=True)
    inverse = lax.rsqrt(spread + EPSILON)
    return centered * inverse, inverse


def norm_back(unit, inverse, gain_row, grad):
    scaled = grad * gain_row
    first = jnp.mean(scaled, axis=-1, keepdims=True)
    second = jnp.mean(scaled * unit, axis=-1, keepdims=True)
    return (scaled - first - unit * second) * inverse


def column_sum(values):
    return jnp.sum(values, axis=0, keepdims=True)


class Copies:
    def __init__(self, send_sems, recv_sems):
        self.send_sems, self.recv_sems = send_sems, recv_sems
        self.count = 0
        self.started = []

    def make(self, source, target, device):
        index = self.count
        self.count += 1
        return pltpu.make_async_remote_copy(
            src_ref=source,
            dst_ref=target,
            send_sem=self.send_sems.at[index],
            recv_sem=self.recv_sems.at[index],
            device_id=device,
            device_id_type=MESH,
        )

    def begin(self, source, target, device):
        copy = self.make(source, target, device)
        copy.start()
        self.started.append(copy)
        return copy


COPY_SLOTS = 256


def scratch_of(width, tokens, seq_count, data_count, hidden, main, shard):
    length = tokens * seq_count
    band = shard * seq_count
    inbox = data_count * main
    rests = seq_count * data_count
    keys = inbox * seq_count + rests
    bf16, f32 = jnp.bfloat16, jnp.float32
    return dict(
        vec_own=((16, LANES), f32),
        vec_all=((data_count, seq_count, 16, LANES), bf16),
        vec=((16, width), f32),
        up_bias=((1, hidden), f32),
        key_bias=((1, keys), f32),
        slab_out=((seq_count, shard, 1536 + hidden), bf16),
        slab_in=((seq_count, shard, 1536 + hidden), bf16),
        cols=((width, 768 + hidden), bf16),
        halves=((data_count, 2, band // 2, 768), bf16),
        cot_all=((length, width), bf16),
        h1=((length, width), bf16),
        h2=((length, width), bf16),
        h3=((length, width), bf16),
        e1=((length, width), bf16),
        e2=((length, width), bf16),
        out_all=((data_count, shard, 2 * width), bf16),
        out_in=((seq_count, data_count // seq_count, shard, 2 * width), bf16),
        out_rows=((256, 2 * width), bf16),
        down_all=((hidden, width), bf16),
        outbox=((inbox, width), bf16),
        units=((inbox, width), bf16),
        rest_rows=((data_count, width), f32),
        rest_wide=((rests * 16, LANES), f32),
        rest_out=((data_count, 16, LANES), bf16),
        rest_in=((seq_count, data_count, 16, LANES), bf16),
        tiles=((keys, width), bf16),
        kv2=((keys, 512), bf16),
        dkv2=((keys, 512), bf16),
        qm1=((3 * length, LANES), bf16),
        qm2=((3 * length, LANES), bf16),
        dom=((3 * length, LANES), bf16),
        qkv1=((length, 768), bf16),
        p1=((3 * length, length), f32),
        o1=((length, 256), bf16),
        o2=((length, 256), bf16),
        o_acc=((length, 256), f32),
        ds=((3 * length, keys), bf16),
        pr=((3 * length, keys), bf16),
        sums_out=((6, 3, tokens, width), bf16),
        sums_in=((6, 3, tokens, width), bf16),
        x2=((tokens, width), f32),
        x3=((tokens, width), f32),
        dx=((tokens, width), f32),
        act=((length, hidden), bf16),
        slope=((length, hidden), f32),
        du=((length, hidden), bf16),
        dqkv=((length, 768), bf16),
        dq2=((length, 256), bf16),
        dn=((keys, width), bf16),
        dn_pair=((2, inbox, width), bf16),
        dn_far=((inbox, width), bf16),
        dn_home=((inbox, width), bf16),
        dr_out=((seq_count, data_count, 16, LANES), bf16),
        dr_pair=((2, data_count, 16, LANES), bf16),
        dr_far=((data_count, 16, LANES), bf16),
        dr_home=((data_count, 16, LANES), bf16),
        g_cols=((width, 768 + hidden), bf16),
        g_half=((data_count, 2, band // 2, 768), bf16),
        half_in=((data_count, band // 2, 768), bf16),
        g_cross=((width, 256), bf16),
        g_down=((hidden, width), bf16),
        g_out=((data_count, shard, 2 * width), bf16),
        g_out_send=((2, seq_count, data_count // seq_count, shard, width), bf16),
        y_up=((4, band, hidden), bf16),
        z_up=((3, band, hidden), bf16),
        y_down=((4, band, width), bf16),
        z_down=((3, band, width), bf16),
        y_full=((4, band, 768), bf16),
        z_full=((3, band, 768), bf16),
        y_half=((4, band // 2, 768), bf16),
        z_half=((3, band // 2, 768), bf16),
        y_xout=((4, shard, width), bf16),
        z_xout=((3, shard, width), bf16),
        y_sout=((4, shard, width), bf16),
        z_sout=((3, shard, width), bf16),
        cols_out=((seq_count, shard, 768 + hidden), bf16),
        cols_in=((seq_count, shard, 768 + hidden), bf16),
        ends_out=((2, shard, 768), bf16),
        ends_in=((seq_count, shard, 768), bf16),
        vv=((16, width), f32),
        vv_out=((data_count, 16, LANES), f32),
        vv_in=((data_count, 16, LANES), f32),
        vq=((seq_count, 16, LANES), f32),
    )


def lane_pick(parts, lane):
    result = None
    for source, first, place, size in parts:
        start = first // LANES * LANES
        stop = start + LANES * (1 if first + size <= start + LANES else 2)
        window = source[:, start:stop]
        turn = (place - first + start) % (stop - start)
        if turn:
            window = pltpu.roll(window, turn, 1)
        window = window[:, 0:LANES]
        if result is None:
            result = window
        else:
            result = jnp.where((lane >= place) & (lane < place + size), window, result)
    return result


def spans(start, stop, size):
    while start < stop:
        end = min(stop, (start // size + 1) * size)
        yield start, end - start
        start = end


def fused_kernel(names, n_in, *refs):
    (
        slide, owner, text, img, cot, w_query, w_key, w_value, w_out, c_query, c_key, c_value,
        c_out, w_up, w_down, b_up, b_down, *gains,
    ) = refs[:n_in]
    r_text, r_tgrad, r_igrad, r_cols, r_half, r_outs, r_down, r_vec = refs[n_in : n_in + 8]
    m = SimpleNamespace(**dict(zip(names, refs[n_in + 8 :])))
    links = Copies(m.send, m.recv)
    begin = links.begin

    _, tokens, width = text.shape
    seq_count = m.slab_out.shape[0]
    length = tokens * seq_count
    shard = w_out.shape[0]
    data_count = m.vec_all.shape[0]
    hidden = m.down_all.shape[0]
    band = shard * seq_count
    tile_count, real_rows, _ = img.shape
    slides = owner.shape[0]
    main = real_rows // 16 * 16
    inbox = data_count * main
    keys_main = inbox * seq_count
    rests = seq_count * data_count
    keys = keys_main + rests
    columns = width // LANES
    factor = 1.0 / math.sqrt(HEAD)
    z_count = data_count // 2

    d = lax.axis_index("dp")
    s = lax.axis_index("seq")
    z, y = d // 2, d % 2
    core = s % 2
    sibling = s + 1 - 2 * core
    across = (s + 2) % 4
    corner = 3 - s
    seq_peers = [sibling, across, corner]
    z_pair = z + 1 - 2 * (z % 2)
    z_across = (z + 2) % 4
    z_corner = 3 - z
    near = (z * 2 + 1 - y, s)
    beside = (z_pair * 2 + y, s)
    beyond = (z_across * 2 + y, s)

    barrier = pltpu.get_barrier_semaphore()
    for peer in seq_peers:
        pl.semaphore_signal(barrier, inc=1, device_id=(d, peer), device_id_type=MESH)
    for k in range(1, data_count):
        pl.semaphore_signal(
            barrier, inc=1, device_id=((d + k) % data_count, s), device_id_type=MESH
        )

    lane = lax.broadcasted_iota(jnp.int32, (1, LANES), 1)
    head_masks = [
        jnp.where(lane < HEAD, 1.0, 0.0),
        jnp.where(lane >= HEAD, 1.0, 0.0),
        jnp.where(lane // HEAD == core, 1.0, 0.0),
    ]

    def arrive(copies):
        for copy in copies:
            copy.wait_recv()

    def seq_gather(views):
        own = [view(s) for view in views]
        pair = [begin(part, part, (d, sibling)) for part in own]
        far = [begin(part, part, (d, across)) for part in own]
        return views, pair, far

    def seq_pass(state):
        arrive(state[2])
        for part in [view(across) for view in state[0]]:
            state[1].append(begin(part, part, (d, sibling)))

    def seq_end(state):
        arrive(state[1])

    def rows_of(ref):
        return [lambda index: ref.at[block(index, tokens)]]

    def send_all(refs, device):
        return [begin(ref, ref, device) for ref in refs]

    def gather_open(view):
        return view, [], []

    def gather_far(state):
        own = state[0](d)
        state[1].extend([send_all(own, beyond), send_all(own, beside)])

    def gather_near(state):
        state[2].extend(send_all(state[0](d), near))

    def gather_step(state, k):
        view, far, close = state
        arrive(far[k])
        part = view((z_across, z_pair, z_corner)[k] * 2 + y)
        if k == 0:
            far.append(send_all(part, beside))
        close.extend(send_all(part, near))

    def gather_end(state):
        arrive(state[2])

    def seq_sum_begin(slot, produce):
        both = low(produce(sibling, corner))
        m.sums_out[slot, 0] = both[0:tokens]
        m.sums_out[slot, 1] = both[tokens : 2 * tokens]
        pair = pl.ds(0, 2)
        copy = begin(m.sums_out.at[slot, pair], m.sums_in.at[slot, pair], (d, sibling))
        both = produce(across, s)
        return slot, copy, both[0:tokens], both[tokens : 2 * tokens]

    def seq_sum_pass(state):
        slot, copy, far, own = state
        copy.wait_recv()
        m.sums_out[slot, 2] = low(far + wide(m.sums_in[slot, 1]))
        return slot, begin(m.sums_out.at[slot, 2], m.sums_in.at[slot, 2], (d, across)), own

    def seq_sum_end(state):
        slot, copy, own = state
        own = own + wide(m.sums_in[slot, 0])
        copy.wait_recv()
        return own + wide(m.sums_in[slot, 2])

    def pick(ref, first, second, place=slice(None)):
        return jnp.concatenate(
            [ref[block(first, tokens), place], ref[block(second, tokens), place]], axis=0
        )

    sum_targets = (z_corner, z_pair, z_across, z)

    def sum_begin(view, y_in, z_in):
        close = [
            [
                begin(part, ref.at[k], near)
                for part, ref in zip(view(target * 2 + 1 - y), y_in, strict=True)
            ]
            for k, target in enumerate(sum_targets)
        ]
        return SimpleNamespace(view=view, y_in=y_in, z_in=z_in, close=close, far=[], own=[])

    def sum_step(state, k):
        arrive(state.close[k])
        if k == 2:
            arrive(state.far[0])
        copies = []
        for index, part in enumerate(state.view(sum_targets[k] * 2 + y)):
            total = wide(part[...]) + wide(state.y_in[index][k])
            if k == 3:
                state.own.append(total)
                continue
            if k == 2:
                total = total + wide(state.z_in[index][0])
            part[...] = low(total)
            target = state.z_in[index].at[k]
            copies.append(begin(part, target, beyond if k == 2 else beside))
        state.far.append(copies)

    def sum_middle(state):
        for k in range(4):
            sum_step(state, k)

    def sum_end(state):
        arrive(state.far[1] + state.far[2])
        return [
            own + wide(ref[1]) + wide(ref[2])
            for own, ref in zip(state.own, state.z_in, strict=True)
        ]

    cross, own = (c_query, c_key, c_value), (w_query, w_key, w_value)
    up_wide = wide(w_up[...])
    slab_out, slab_in = m.slab_out, m.slab_in
    for j in range(seq_count):
        full, half = 3 * (j // 2) + 2 * (j % 2), 3 * (j // 2) + 1
        sources = [(matrix, full) for matrix in cross + own]
        sources += [(matrix, half) for matrix in cross + own]
        for k, (matrix, index) in enumerate(sources):
            place = slice(LANES * k, LANES * k + LANES)
            slab_out[j, :, place] = matrix[:, LANES * index : LANES * index + LANES]
        for tile in range(hidden // LANES):
            pieces = [
                (up_wide, band * (seq_count * (at // band) + j) + at % band, at % LANES, size)
                for at, size in spans(LANES * tile, LANES * tile + LANES, band)
            ]
            slab_out[j, :, 1536 + LANES * tile : 1536 + LANES * (tile + 1)] = low(
                lane_pick(pieces, lane)
            )
    vec_own = m.vec_own
    vec_own[...] = jnp.zeros(vec_own.shape, jnp.float32)
    for k, ref in enumerate((b_down, *gains)):
        vec_own[k : k + 1, 0:shard] = wide(ref[...])
    vec_own[9:10, 0:band] = wide(b_up[...])
    vec_all = m.vec_all
    vec_all[d, s] = low(vec_own[...])
    slab_in[s] = slab_out[s]
    out_all, down_all, cot_all = m.out_all, m.down_all, m.cot_all
    out_all[d, :, 0:width] = w_out[...]
    out_all[d, :, width : 2 * width] = c_out[...]
    down_all[block(d, band)] = w_down[...]
    cot_all[block(s, tokens)] = cot[0]
    m.rest_wide[...] = jnp.zeros(m.rest_wide.shape, jnp.float32)


    def destination(index):
        total = jnp.int32(0)
        for k in range(slides):
            total = total + jnp.where(slide[index] == k, owner[k], 0)
        return total

    own_places = [destination(d * tile_count + t) for t in range(tile_count)]
    route = [
        [jnp.where(place == p, 1.0, 0.0) for place in own_places] for p in range(data_count)
    ]
    spot = lax.broadcasted_iota(jnp.int32, (1, keys), 1)
    slot_of = jnp.where(spot < keys_main, spot % inbox // main, (spot - keys_main) % data_count)
    bias = jnp.zeros((1, keys), jnp.float32)
    for p in range(data_count):
        hits = jnp.int32(0)
        for t in range(tile_count):
            hits = hits + jnp.where(destination(p * tile_count + t) == d, 1, 0)
        bias = jnp.where(slot_of == p, jnp.where(hits > 0, 0.0, MASKED_SCORE), bias)
    m.key_bias[...] = bias
    text_unit, _ = norm_parts(wide(text[0]))

    outbox, tiles = m.outbox, m.tiles
    rest_rows, rest_wide, rest_out, rest_in = m.rest_rows, m.rest_wide, m.rest_out, m.rest_in
    units = [wide(low(norm_parts(wide(img[t]))[0])) for t in range(tile_count)]
    for p in range(data_count):
        total = units[0] * route[p][0]
        for t in range(1, tile_count):
            total = total + units[t] * route[p][t]
        outbox[block(p, main)] = low(total[0:main])
        rest_rows[p : p + 1] = total[main:real_rows]
    for k in range(columns):
        rest_wide[pl.ds(k, data_count, stride=16), :] = rest_rows[:, LANES * k : LANES * (k + 1)]
    rest_out[...] = low(rest_wide[0 : 16 * data_count]).reshape(rest_out.shape)
    own_slot = block(s * data_count + d, main)
    tiles[own_slot] = outbox[block(d, main)]
    rest_in[s, d] = rest_out[d]
    tile_dp = []

    def tile_out(k):
        peer = (d + k) % data_count
        tile_dp.append(begin(outbox.at[block(peer, main)], tiles.at[own_slot], (peer, s)))
        tile_dp.append(begin(rest_out.at[peer], rest_in.at[s, d], (peer, s)))

    pl.semaphore_wait(barrier, seq_count - 1 + data_count - 1)

    own_vec = vec_all.at[d, s]
    vec_dp = [begin(own_vec, own_vec, ((d + k) % data_count, s)) for k in range(1, data_count)]
    slab_seq = [begin(slab_out.at[peer], slab_in.at[s], (d, peer)) for peer in seq_peers]
    for k in (2, 1, 4, 3, 6, 5, 7):
        tile_out(k)
    out_view = lambda index: [out_all.at[index]]
    out_ag = gather_open(out_view)
    gather_far(out_ag)
    gather_near(out_ag)
    arrive(vec_dp)
    vec_column = vec_all.at[:, s]
    vec_seq = [begin(vec_column, vec_column, (d, peer)) for peer in seq_peers]
    arrive(slab_seq)
    cols, halves = m.cols, m.halves
    rows = jnp.concatenate([wide(slab_in[j]) for j in range(seq_count)], axis=0)
    cols[block(d, band), 0:768] = low(rows[:, 0:768])
    cols[block(d, band), 768 : 768 + hidden] = low(rows[:, 1536 : 1536 + hidden])
    rows = rows[:, 768:1536]
    rows = jnp.where(core == 0, rows[0 : band // 2], rows[band // 2 : band])
    halves[d, core] = low(rows)

    def group_view(full, half, first):
        place = lanes(first, 384)
        return lambda index: [
            full.at[block(index, band), place],
            half.at[index, core, :, place],
        ]

    def half_cols(first, size):
        return halves[:, :, :, first : first + size].reshape(width, size)

    def half_swap(first):
        part = halves.at[:, core, :, lanes(first, 384)]
        return begin(part, part, (d, sibling))

    self_view, cross_view = group_view(cols, halves, 384), group_view(cols, halves, 0)
    up_view = lambda index: [cols.at[block(index, band), lanes(768, hidden)]]
    down_view = lambda index: [down_all.at[block(index, band)]]
    self_ag, cross_ag = gather_open(self_view), gather_open(cross_view)
    up_ag, down_ag = gather_open(up_view), gather_open(down_view)
    gather_far(self_ag)
    for state in (self_ag, cross_ag, up_ag, down_ag):
        gather_near(state)
    arrive(vec_seq)
    stacked = vec_all[...].reshape(data_count * seq_count * 16, LANES)
    row_of = lax.broadcasted_iota(jnp.int32, (LANES, width), 0)
    col_of = lax.broadcasted_iota(jnp.int32, (LANES, width), 1)
    spread = dot_plain(stacked, jnp.where(row_of == col_of % shard, 1.0, 0.0).astype(jnp.bfloat16))
    spread = spread.reshape(data_count * seq_count, 16, width)
    which = lax.broadcasted_iota(jnp.int32, spread.shape, 0)
    column = lax.broadcasted_iota(jnp.int32, spread.shape, 2)
    vec = m.vec
    vec[...] = jnp.sum(jnp.where(which == column // shard, spread, 0.0), axis=0)

    def vector(index):
        return vec[index : index + 1, :]

    h1, h2, h3, e1, e2 = m.h1, m.h2, m.h3, m.e1, m.e2
    h1[block(s, tokens)] = low(text_unit * vector(1) + vector(2))
    h1_ag = seq_gather(rows_of(h1))

    arrive(tile_dp)
    whole_place = block(s, inbox)
    m.units[...] = tiles[whole_place]
    tiles[whole_place] = low(wide(m.units[...]) * vector(5) + vector(6))
    whole_own = tiles.at[block(s, inbox)]
    tile_pair = [
        begin(whole_own, whole_own, (d, sibling)),
        begin(rest_in.at[s], rest_in.at[s], (d, sibling)),
    ]
    rest_far = begin(rest_in.at[s], rest_in.at[s], (d, across))
    quarter = inbox // 4

    def quarter_of(index, k):
        return tiles.at[pl.ds(pl.multiple_of(index * inbox + k * quarter, quarter), quarter)]

    def tile_send(k):
        part = quarter_of(s, k)
        return begin(part, part, (d, across))

    def tile_pass(k):
        tile_far[k].wait_recv()
        part = quarter_of(across, k)
        tile_pair.append(begin(part, part, (d, sibling)))

    tile_far = [tile_send(k) for k in range(4)]
    gather_step(out_ag, 0)
    gather_step(out_ag, 1)
    gather_step(self_ag, 0)
    gather_step(self_ag, 1)
    gather_step(out_ag, 2)
    gather_far(cross_ag)
    gather_far(up_ag)
    seq_pass(h1_ag)
    gather_end(out_ag)
    per_seq = data_count // seq_count
    out_in = m.out_in
    out_seq = []
    for peer in (across, corner, sibling):
        out_seq.append(
            begin(out_all.at[pl.ds(peer * per_seq, per_seq)], out_in.at[s], (d, peer))
        )
    out_in[s] = out_all[pl.ds(s * per_seq, per_seq)]
    gather_step(self_ag, 2)
    gather_end(self_ag)
    half_copy = half_swap(384)
    seq_end(h1_ag)
    qkv1, qm1, p1, o1 = m.qkv1, m.qm1, m.p1, m.o1
    qkv1[:, 0:384] = low(dot_plain(h1[...], cols[:, 384:768]))
    arrive([half_copy])
    qkv1[:, 384:768] = low(dot_plain(h1[...], half_cols(384, 384)))
    gather_step(cross_ag, 0)
    gather_step(cross_ag, 1)
    gather_far(down_ag)

    spot_q = lax.broadcasted_iota(jnp.int32, (length, length), 0)
    spot_k = lax.broadcasted_iota(jnp.int32, (length, length), 1)
    causal = spot_q >= spot_k
    mixed = []
    for head in range(3):
        base = 384 * (head // 2)
        qm = low(wide(qkv1[:, base : base + 128]) * head_masks[head])
        qm1[block(head, length)] = qm
        scores = dot_right(qm, qkv1[:, base + 128 : base + 256]) * factor
        scores = jnp.where(causal, scores, MASKED_SCORE)
        exponent = jnp.exp(scores - jnp.max(scores, axis=1, keepdims=True))
        chances = exponent / jnp.sum(exponent, axis=1, keepdims=True)
        p1[block(head, length)] = chances
        mixed.append(
            dot_plain(low(chances), qkv1[:, base + 256 : base + 384]) * head_masks[head]
        )
    o1[:, 0:128] = low(mixed[0] + mixed[1])
    o1[:, 128:256] = low(mixed[2])

    arrive(out_seq)
    out_rows = m.out_rows
    natural = jnp.concatenate(
        [wide(out_in[j, i]) for i in range(per_seq) for j in range(seq_count)], axis=0
    )
    blank = jnp.zeros((64, 2 * width), jnp.float32)
    even = jnp.concatenate([natural, blank], axis=0)
    odd = jnp.concatenate([natural[64:192], blank, natural[0:64]], axis=0)
    out_rows[...] = low(jnp.where(core == 0, even, odd))

    state = seq_sum_begin(0, lambda i, j: dot_plain(pick(o1, i, j), out_rows[:, 0:width]))
    state = seq_sum_pass(state)
    gather_step(cross_ag, 2)
    x2, x3, dx = m.x2, m.x3, m.dx
    second = wide(text[0]) + seq_sum_end(state)
    x2[...] = second
    unit, _ = norm_parts(second)
    h2[block(s, tokens)] = low(unit * vector(3) + vector(4))
    h2_ag = seq_gather(rows_of(h2))
    cot_ag = seq_gather(rows_of(cot_all))
    gather_step(up_ag, 0)
    gather_step(up_ag, 1)
    row_up = lax.broadcasted_iota(jnp.int32, (LANES, hidden), 0)
    col_up = lax.broadcasted_iota(jnp.int32, (LANES, hidden), 1)
    spread = dot_plain(stacked, jnp.where(row_up == col_up % band, 1.0, 0.0).astype(jnp.bfloat16))
    spread = spread.reshape(data_count * seq_count, 16, hidden)
    which = lax.broadcasted_iota(jnp.int32, spread.shape, 0)
    column = lax.broadcasted_iota(jnp.int32, spread.shape, 2)
    picked = jnp.where(which == (column // band) * seq_count + s, spread, 0.0)
    m.up_bias[...] = jnp.sum(picked, axis=0)[9:10]


    kv2, qm2, pr, o2, o_acc = m.kv2, m.qm2, m.pr, m.o2, m.o_acc

    def keys_values(here):
        rows = tiles[here]
        kv2[here, 0:256] = low(dot_plain(rows, cols[:, 128:384]))
        kv2[here, 256:512] = low(dot_plain(rows, half_cols(128, 256)))

    gather_end(cross_ag)
    half_copy = half_swap(0)
    arrive([half_copy])
    keys_values(block(s, inbox))
    tile_pass(0)
    seq_pass(h2_ag)
    arrive(tile_pair[0:2])
    keys_values(block(sibling, inbox))
    tile_pass(1)
    rest_far.wait_recv()
    tile_pair.append(begin(rest_in.at[across], rest_in.at[across], (d, sibling)))
    seq_end(h2_ag)
    query_full = dot_plain(h2[...], cols[:, 0:128])
    query_half = dot_plain(h2[...], half_cols(0, 128))
    for head in range(3):
        source = query_full if head < 2 else query_half
        qm2[block(head, length)] = low(wide(low(source)) * (head_masks[head] * factor))
    tile_pass(2)
    tile_pass(3)
    gather_step(up_ag, 2)
    gather_step(down_ag, 0)
    keys_values(block(across, inbox))
    arrive(tile_pair[2:])
    keys_values(block(corner, inbox))
    rest_wide[...] = wide(rest_in[...]).reshape(rest_wide.shape)
    for k in range(columns):
        place = slice(LANES * k, LANES * (k + 1))
        tiles[keys_main:keys, place] = low(
            rest_wide[pl.ds(k, rests, stride=16), :] * vec[5:6, place] + vec[6:7, place]
        )
    keys_values(pl.ds(keys_main, rests))
    gather_step(down_ag, 1)
    for head in range(3):
        base = 256 * (head // 2)
        place = 128 * (head // 2)

        here = block(head, length)
        scores = dot_right(qm2[here], kv2[:, base : base + 128]) + m.key_bias[...]
        exponent = jnp.exp(scores - jnp.max(scores, axis=1, keepdims=True))
        chances = low(exponent * (1.0 / jnp.sum(exponent, axis=1, keepdims=True)))
        pr[here] = chances
        result = dot_plain(chances, kv2[:, base + 128 : base + 256]) * head_masks[head]
        if head == 1:
            result = result + o_acc[:, place : place + 128]
        o_acc[:, place : place + 128] = result
        if head == 0:
            gather_step(down_ag, 2)

    o2[...] = low(o_acc[...])
    state = seq_sum_begin(
        1, lambda i, j: dot_plain(pick(o2, i, j), out_rows[:, width : 2 * width])
    )
    state = seq_sum_pass(state)
    third = x2[...] + seq_sum_end(state)
    x3[...] = third
    unit, _ = norm_parts(third)
    h3[block(s, tokens)] = low(unit * vector(7) + vector(8))
    h3_ag = seq_gather(rows_of(h3))
    seq_pass(cot_ag)
    seq_end(cot_ag)
    seq_pass(h3_ag)
    gather_end(down_ag)
    act, slope, du = m.act, m.slope, m.du
    slope[...] = dot_right(cot_all[...], down_all[...])
    gather_end(up_ag)
    seq_end(h3_ag)

    @pl.loop(0, seq_count)
    def _(i):
        here = block(i, tokens)
        pre = dot_plain(h3[here], cols[:, 768 : 768 + hidden]) + m.up_bias[...]
        cdf = 0.5 * (1.0 + lax.erf(pre * (1.0 / math.sqrt(2.0))))
        density = jnp.exp(-0.5 * pre * pre) * (1.0 / math.sqrt(2.0 * math.pi))
        act[here] = low(pre * cdf)
        grad = wide(low(slope[here]))
        du[here] = low(grad * (cdf + pre * density))

    state = seq_sum_begin(
        2, lambda i, j: dot_right(pick(du, i, j), cols[:, 768 : 768 + hidden])
    )
    state = seq_sum_pass(state)
    g_cols, g_down = m.g_cols, m.g_down
    g_down[...] = low(dot_left(act[...], cot_all[...]))
    g_down_view = lambda index: [g_down.at[block(index, band)]]
    down_rs = sum_begin(g_down_view, [m.y_down], [m.z_down])
    grad_mid = seq_sum_end(state)
    unit, inverse = norm_parts(x3[...])
    vv = m.vv
    vv[...] = jnp.zeros(vv.shape, jnp.float32)
    grad_out = wide(cot[0])
    dx3 = grad_out + norm_back(unit, inverse, vector(7), grad_mid)
    dx[...] = dx3
    e2[block(s, tokens)] = low(dx3)
    e2_ag = seq_gather(rows_of(e2))
    vv[0:1] = column_sum(grad_out)
    vv[7:8] = column_sum(grad_mid * unit)
    vv[8:9] = column_sum(grad_mid)
    vv[9:10, 0:hidden] = column_sum(wide(du[...]))

    g_cols[:, 768 : 768 + hidden] = low(dot_left(h3[...], du[...]))
    g_up_view = lambda index: [g_cols.at[block(index, band), lanes(768, hidden)]]
    up_rs = sum_begin(g_up_view, [m.y_up], [m.z_up])
    sum_step(down_rs, 0)
    seq_pass(e2_ag)
    sum_step(down_rs, 1)
    seq_end(e2_ag)

    dom = m.dom
    grad_o = low(dot_right(e2[...], out_rows[:, width : 2 * width]))
    for head in range(3):
        place = 128 * (head // 2)
        dom[block(head, length)] = low(wide(grad_o[:, place : place + 128]) * head_masks[head])
    ds, dkv2, dq2 = m.ds, m.dkv2, m.dq2
    for head in range(3):
        base = 256 * (head // 2)
        place = 128 * (head // 2)

        here = block(head, length)
        chances = wide(pr[here])
        grad_p = dot_right(dom[here], kv2[:, base + 128 : base + 256])
        weighted = jnp.sum(chances * grad_p, axis=1, keepdims=True)
        grad_s = low(chances * (grad_p - weighted))
        ds[here] = grad_s
        result = dot_plain(grad_s, kv2[:, base : base + 128]) * (head_masks[head] * factor)
        if head == 1:
            result = result + o_acc[:, place : place + 128]
        o_acc[:, place : place + 128] = result
        if head < 2:
            sum_step(down_rs, 2 + head)

    dq2[...] = low(o_acc[...])
    sum_step(up_rs, 0)
    state = seq_sum_begin(
        4,
        lambda i, j: dot_right(pick(dq2, i, j, slice(0, 128)), cols[:, 0:128])
        + dot_right(pick(dq2, i, j, slice(128, 256)), half_cols(0, 128)),
    )

    g_out, g_out_send = m.g_out, m.g_out_send

    def out_grad(slot, value):
        odd = jnp.concatenate([value[192:256], value[0:128]], axis=0)
        natural = jnp.where(core == 0, value[0:192], odd)
        for i in range(per_seq):
            for j in range(seq_count):
                start = shard * (i * seq_count + j)
                g_out_send[slot, j, i] = low(natural[start : start + shard])
        target = g_out.at[pl.ds(s * per_seq, per_seq), :, lanes(slot * width, width)]
        copies = [begin(g_out_send.at[slot, peer], target, (d, peer)) for peer in seq_peers]
        g_out[pl.ds(s * per_seq, per_seq), :, slot * width : (slot + 1) * width] = g_out_send[
            slot, s
        ]
        return copies

    xout_seq = out_grad(1, dot_left(o2[...], e2[...]))
    state = seq_sum_pass(state)
    for tile in range(2):
        first, count = (0, 2 * length) if tile == 0 else (2 * length, length)
        base = 256 * tile
        for start, size in spans(0, keys, 512):
            cut = slice(start, start + size)
            dkv2[cut, base : base + 128] = low(
                dot_left(ds[first : first + count, cut], qm2[first : first + count])
            )
            dkv2[cut, base + 128 : base + 256] = low(
                dot_left(pr[first : first + count, cut], dom[first : first + count])
            )
    sum_step(up_rs, 1)
    second_grad = seq_sum_end(state)
    unit, inverse = norm_parts(x2[...])
    dx2 = dx[...] + norm_back(unit, inverse, vector(3), second_grad)
    dx[...] = dx2
    e1[block(s, tokens)] = low(dx2)
    e1_ag = seq_gather(rows_of(e1))
    vv[3:4] = column_sum(second_grad * unit)
    vv[4:5] = column_sum(second_grad)
    sum_step(up_rs, 2)
    arrive(xout_seq)
    xout_view = lambda index: [g_out.at[index, :, lanes(width, width)]]
    xout_rs = sum_begin(xout_view, [m.y_xout], [m.z_xout])

    dn = m.dn

    def tile_grads(here):
        dn[here] = low(
            dot_right(dkv2[here, 0:256], cols[:, 128:384])
            + dot_right(dkv2[here, 256:512], half_cols(128, 256))
        )

    dr_out, dr_pair, dr_far, dr_home = m.dr_out, m.dr_pair, m.dr_far, m.dr_home
    dn_pair, dn_far, dn_home = m.dn_pair, m.dn_far, m.dn_home
    tile_grads(block(corner, inbox))
    pair_far = begin(dn.at[block(corner, inbox)], dn_pair.at[1], (d, sibling))
    tile_grads(pl.ds(keys_main, rests))
    rest_wide[...] = jnp.zeros(rest_wide.shape, jnp.float32)
    for k in range(columns):
        rest_wide[pl.ds(k, rests, stride=16), :] = wide(
            dn[keys_main:keys, LANES * k : LANES * (k + 1)]
        )
    dr_out[...] = low(rest_wide[...]).reshape(dr_out.shape)
    rest_pair = [
        begin(dr_out.at[peer], dr_pair.at[k], (d, sibling))
        for k, peer in enumerate((sibling, corner))
    ]
    tile_grads(block(across, inbox))
    seq_pass(e1_ag)
    pair_far.wait_recv()
    fold = dn.at[block(across, inbox)]
    fold[...] = low(wide(fold[...]) + wide(dn_pair[1]))
    arrive(rest_pair)
    dr_out[across] = low(wide(dr_out[across]) + wide(dr_pair[1]))
    rest_far = begin(dr_out.at[across], dr_far, (d, across))

    def far_send(k):
        return begin(quarter_in(dn, across, k), dn_far.at[block(k, quarter)], (d, across))

    def quarter_in(ref, index, k):
        return ref.at[pl.ds(pl.multiple_of(index * inbox + k * quarter, quarter), quarter)]

    far_copies = [far_send(k) for k in range(4)]
    sum_step(up_rs, 3)
    g_half, half_in, g_cross = m.g_half, m.half_in, m.g_cross
    half_shape = (data_count, 2, band // 2)

    def half_send(first):
        place = lanes(first, 384)
        return begin(g_half.at[:, 1 - core, :, place], half_in.at[:, :, place], (d, sibling))

    def half_add(first, copy):
        copy.wait_recv()
        place = lanes(first, 384)
        g_half[:, core, :, place] = low(
            wide(g_half[:, core, :, place]) + wide(half_in[:, :, place])
        )

    seq_end(e1_ag)
    grad_o = low(dot_right(e1[...], out_rows[:, 0:width]))
    grads = []
    dqkv = m.dqkv
    for head in range(3):
        base = 384 * (head // 2)
        place = 128 * (head // 2)
        here = block(head, length)
        dm = low(wide(grad_o[:, place : place + 128]) * head_masks[head])
        chances = p1[here]
        grad_p = dot_right(dm, qkv1[:, base + 256 : base + 384])
        weighted = jnp.sum(chances * grad_p, axis=1, keepdims=True)
        grad_s = low(chances * (grad_p - weighted))
        grads.append(
            (
                dot_plain(grad_s, qkv1[:, base + 128 : base + 256]) * (head_masks[head] * factor),
                dot_left(grad_s, qm1[here]) * factor,
                dot_left(low(chances), dm),
            )
        )
    for k in range(3):
        dqkv[:, 128 * k : 128 * k + 128] = low(grads[0][k] + grads[1][k])
        dqkv[:, 384 + 128 * k : 512 + 128 * k] = low(grads[2][k])
    state = seq_sum_begin(
        5,
        lambda i, j: dot_right(pick(dqkv, i, j, slice(0, 384)), cols[:, 384:768])
        + dot_right(pick(dqkv, i, j, slice(384, 768)), half_cols(384, 384)),
    )

    grad = dot_left(h1[...], dqkv[...])
    g_cols[:, 384:768] = low(grad[:, 0:384])
    g_half[:, :, :, 384:768] = low(grad[:, 384:768]).reshape(*half_shape, 384)
    half_copy = half_send(384)
    state = seq_sum_pass(state)
    sout_seq = out_grad(0, dot_left(o1[...], e1[...]))
    half_add(384, half_copy)
    self_rs = sum_begin(
        group_view(g_cols, g_half, 384),
        [m.y_full.at[:, :, lanes(384, 384)], m.y_half.at[:, :, lanes(384, 384)]],
        [m.z_full.at[:, :, lanes(384, 384)], m.z_half.at[:, :, lanes(384, 384)]],
    )
    tile_grads(block(sibling, inbox))
    pair_own = begin(dn.at[block(sibling, inbox)], dn_pair.at[0], (d, sibling))
    tile_grads(block(s, inbox))

    sum_middle(xout_rs)
    grad = dot_left(h2[...], dq2[...])
    g_cols[:, 0:128] = low(grad[:, 0:128])
    g_half[:, :, :, 0:128] = low(grad[:, 128:256]).reshape(*half_shape, 128)
    for cut in range(3):
        span = slice(256 * cut, 256 * cut + 256)
        grad = dot_left(tiles[:, span], dkv2[...])
        g_cols[span, 128:384] = low(grad[:, 0:256])
        g_cross[span] = low(grad[:, 256:512])
    g_half[:, :, :, 128:384] = g_cross[...].reshape(*half_shape, 256)
    half_copy = half_send(0)
    sum_step(self_rs, 0)
    half_add(0, half_copy)
    cross_rs = sum_begin(
        group_view(g_cols, g_half, 0),
        [m.y_full.at[:, :, lanes(0, 384)], m.y_half.at[:, :, lanes(0, 384)]],
        [m.z_full.at[:, :, lanes(0, 384)], m.z_half.at[:, :, lanes(0, 384)]],
    )
    sum_step(self_rs, 1)
    arrive([pair_own, rest_far])
    dr_out[s] = low(wide(dr_out[s]) + wide(dr_pair[0]) + wide(dr_far[...]))

    home_dp = []
    own_home = block(d, main)
    for k in range(4):
        far_copies[k].wait_recv()
        mine = quarter_in(dn, s, k)
        there = block(k, quarter)
        mine[...] = low(wide(mine[...]) + wide(dn_pair[0, there]) + wide(dn_far[there]))

    def home_send(k):
        peer = (d + k) % data_count
        source = dn.at[block(s * data_count + peer, main)]
        home_dp.append(begin(source, dn_home.at[own_home], (peer, s)))
        home_dp.append(begin(dr_out.at[s, peer], dr_home.at[d], (peer, s)))

    sum_step(self_rs, 2)
    for k in (2, 4, 6):
        home_send(k)
    sum_step(self_rs, 3)
    sum_step(cross_rs, 0)
    sum_step(cross_rs, 1)
    for k in (1, 3, 5, 7):
        home_send(k)
    dn_home[own_home] = dn[block(s * data_count + d, main)]
    dr_home[d] = dr_out[s, d]
    out_state = seq_sum_begin(3, lambda i, j: dot_plain(pick(act, i, j), down_all[...]))
    grad = wide(dn[block(s, inbox)])
    vv[5:6] = column_sum(grad * wide(m.units[...]))
    vv[6:7] = column_sum(grad)
    rest = wide(dr_out[s])
    for row, total in ((5, rest * wide(rest_in[s])), (6, rest)):
        total = jnp.sum(total, axis=0)
        total = jnp.concatenate([total[k : k + 1] for k in range(columns)], axis=1)
        vv[row : row + 1] = vv[row : row + 1] + total
    first_grad = seq_sum_end(state)
    unit, inverse = norm_parts(wide(text[0]))
    vv[1:2] = column_sum(first_grad * unit)
    vv[2:3] = column_sum(first_grad)
    r_tgrad[...] = low(dx[...] + norm_back(unit, inverse, vector(1), first_grad))
    vv_out, vv_in, vq = m.vv_out, m.vv_in, m.vq
    everything = vv[...]
    for p in range(data_count):
        turned = everything if p == 0 else pltpu.roll(everything, width - band * p, 1)
        vv_out[p] = turned[:, 0:LANES]
    vv_dp = []
    for k in range(1, data_count):
        peer = (d + k) % data_count
        vv_dp.append(begin(vv_out.at[peer], vv_in.at[d], (peer, s)))
    vv_in[d] = vv_out[d]
    arrive(sout_seq)
    sout_view = lambda index: [g_out.at[index, :, lanes(0, width)]]
    sout_rs = sum_begin(sout_view, [m.y_sout], [m.z_sout])
    out_state = seq_sum_pass(out_state)
    cols_out, cols_in, ends_out, ends_in = m.cols_out, m.cols_in, m.ends_out, m.ends_in

    def finish_cols(first, size, total):
        place = lanes(first, size)
        for j in range(seq_count):
            cols_out[j, :, place] = low(total[shard * j : shard * (j + 1)])
        cols_in[s, :, place] = cols_out[s, :, place]
        return [
            begin(cols_out.at[peer, :, place], cols_in.at[s, :, place], (d, peer))
            for peer in seq_peers
        ]

    def finish_half(first, total):
        place = lanes(first, 384)
        for j in range(2):
            ends_out[j, :, place] = low(total[shard * j : shard * (j + 1)])
        ends_in[s, :, place] = ends_out[core, :, place]
        return [
            begin(ends_out.at[peer % 2, :, place], ends_in.at[s, :, place], (d, peer))
            for peer in seq_peers
        ]

    (r_down[...],) = sum_end(down_rs)
    ends = finish_cols(768, hidden, sum_end(up_rs)[0])
    (r_outs[1],) = sum_end(xout_rs)
    sum_step(cross_rs, 2)
    sum_step(cross_rs, 3)
    sum_middle(sout_rs)
    arrive(vv_dp)
    total = vv_in[0]
    for p in range(1, data_count):
        total = total + vv_in[p]
    vq[s] = total
    vq_seq = [begin(vq.at[s], vq.at[s], (d, peer)) for peer in seq_peers]
    bias_grad = total[9:10]
    r_text[...] = low(x3[...] + seq_sum_end(out_state) + vector(0))

    full, half = sum_end(self_rs)
    ends += finish_cols(384, 384, full) + finish_half(384, half)

    arrive(home_dp)
    for t in range(tile_count):
        grad = wide(dn_home[block(0, main)]) * route[0][t]
        rest = wide(dr_home[0]) * route[0][t]
        for p in range(1, data_count):
            grad = grad + wide(dn_home[block(p, main)]) * route[p][t]
            rest = rest + wide(dr_home[p]) * route[p][t]
        rest = jnp.concatenate([rest[k : k + 1] for k in range(columns)], axis=1)
        unit, inverse = norm_parts(wide(img[t, 0:main]))
        r_igrad[t, 0:main] = low(norm_back(unit, inverse, vector(5), grad))
        unit, inverse = norm_parts(wide(img[t, main:real_rows]))
        r_igrad[t, main:real_rows] = low(norm_back(unit, inverse, vector(5), rest))


    full, half = sum_end(cross_rs)
    ends += finish_cols(0, 384, full) + finish_half(0, half)
    (r_outs[0],) = sum_end(sout_rs)

    arrive(ends)
    r_cols[...] = cols_in[...]
    r_half[...] = ends_in[...]
    arrive(vq_seq)
    total = vq[0] + vq[1] + vq[2] + vq[3]
    r_vec[...] = pltpu.roll(total, (LANES - shard * s) % LANES, 1)
    r_vec[9:10] = bias_grad

    for copy in links.started:
        copy.wait_send()


def unpack_kernel(t_out, t_grad, i_grad, cols, ends, outs, down, vec, *results):
    o_text, o_tgrad, o_igrad, o_q, o_k, o_v, o_o, o_xq, o_xk, o_xv, o_xo, o_up, o_down, *vectors = (
        results
    )
    seq_count, shard, total = cols.shape
    hidden = total - 768
    core = lax.axis_index("seq") // 2
    band = down.shape[0]
    o_text[0] = t_out[...]
    o_tgrad[0] = t_grad[...]
    o_igrad[...] = i_grad[...]
    for k, result in enumerate((o_xq, o_xk, o_xv, o_q, o_k, o_v)):
        here = slice(LANES * k, LANES * (k + 1))
        for j, tile in ((0, 0), (1, 2), (2, 3), (3, 5)):
            result[:, LANES * tile : LANES * (tile + 1)] = wide(cols[j, :, here])
        for j, tile in ((0, 1), (2, 4)):
            result[:, LANES * tile : LANES * (tile + 1)] = wide(ends[j + core, :, here])
    o_o[...] = outs[0]
    o_xo[...] = outs[1]
    o_down[...] = down[...]
    lane = lax.broadcasted_iota(jnp.int32, (1, LANES), 1)
    parts = [wide(cols[j, :, 768:total]) for j in range(seq_count)]
    for tile in range(hidden * seq_count // LANES):
        pieces = []
        for at, size in spans(LANES * tile, LANES * tile + LANES, band):
            group = at // band
            first = band * (group // seq_count) + at % band
            pieces.append((parts[group % seq_count], first, at % LANES, size))
        o_up[:, LANES * tile : LANES * (tile + 1)] = lane_pick(pieces, lane)
    vectors[0][...] = vec[9, 0:band]
    for k, result in enumerate(vectors[1:]):
        result[...] = vec[k, 0:shard]


def fused_device(
    text_in, image_in, tile_slide, owner_map, text_cot,
    w_query, w_key, w_value, w_out, c_query, c_key, c_value, c_out, w_up, w_down, b_up, b_down,
    self_gain, self_shift, cross_gain, cross_shift, tile_gain, tile_shift, mlp_gain, mlp_shift,
):
    data_count, seq_count = lax.axis_size("dp"), lax.axis_size("seq")
    tile_count, real_rows, width = image_in.shape
    tokens = text_in.shape[1]
    shard = w_query.shape[0]
    band = shard * seq_count
    hidden = w_up.shape[1] // seq_count
    main = real_rows // 16 * 16

    gains = (
        self_gain, self_shift, cross_gain, cross_shift, tile_gain, tile_shift, mlp_gain, mlp_shift,
    )
    inputs = (
        tile_slide, owner_map, text_in, image_in, text_cot, w_query, w_key, w_value, w_out,
        c_query, c_key, c_value, c_out, w_up, w_down,
        *[member.reshape(1, -1) for member in (b_up, b_down, *gains)],
    )
    in_specs = [pl.BlockSpec(memory_space=pltpu.SMEM)] * 2
    in_specs += [pl.BlockSpec(memory_space=pltpu.VMEM)] * (len(inputs) - 2)
    row_out = jax.ShapeDtypeStruct((tokens, width), jnp.bfloat16)
    packed_shape = [
        row_out,
        row_out,
        jax.ShapeDtypeStruct(image_in.shape, jnp.bfloat16),
        jax.ShapeDtypeStruct((seq_count, shard, 768 + hidden), jnp.bfloat16),
        jax.ShapeDtypeStruct((seq_count, shard, 768), jnp.bfloat16),
        jax.ShapeDtypeStruct((2, shard, width), jnp.float32),
        jax.ShapeDtypeStruct((band, width), jnp.float32),
        jax.ShapeDtypeStruct((16, LANES), jnp.float32),
    ]
    shapes = scratch_of(width, tokens, seq_count, data_count, hidden, main, shard)
    scratch = [pltpu.VMEM(shape, kind) for shape, kind in shapes.values()]
    scratch += [pltpu.SemaphoreType.DMA((COPY_SLOTS,))] * 2
    names = [*shapes, "send", "recv"]
    packed = pl.pallas_call(
        partial(fused_kernel, names, len(inputs)),
        out_shape=packed_shape,
        in_specs=in_specs,
        out_specs=[pl.BlockSpec(memory_space=pltpu.VMEM)] * len(packed_shape),
        scratch_shapes=scratch,
        compiler_params=pltpu.CompilerParams(
            collective_id=0, has_side_effects=True, vmem_limit_bytes=60 * 1024 * 1024
        ),
        name="decoder_layer",
    )(*inputs)
    square = jax.ShapeDtypeStruct((shard, width), jnp.float32)
    out_shape = [
        jax.ShapeDtypeStruct(text_in.shape, jnp.bfloat16),
        jax.ShapeDtypeStruct(text_in.shape, jnp.bfloat16),
        jax.ShapeDtypeStruct(image_in.shape, jnp.bfloat16),
        *[square] * 8,
        jax.ShapeDtypeStruct((shard, hidden * seq_count), jnp.float32),
        jax.ShapeDtypeStruct((band, width), jnp.float32),
        jax.ShapeDtypeStruct((band,), jnp.float32),
        *[jax.ShapeDtypeStruct((shard,), jnp.float32)] * 9,
    ]
    return tuple(
        pl.pallas_call(
            unpack_kernel,
            out_shape=out_shape,
            in_specs=[pl.BlockSpec(memory_space=pltpu.VMEM)] * len(packed),
            out_specs=[pl.BlockSpec(memory_space=pltpu.VMEM)] * len(out_shape),
            name="unpack",
        )(*packed)
    )


def fused_fits(mesh):
    return mesh.shape["seq"] == 4 and 768 % (8 * mesh.shape["dp"] * mesh.shape["seq"]) == 0


def solution(mesh):
    placed = (
        P("dp", "seq", None),
        P("dp", "seq", None),
        P(),
        P(),
        P("dp", "seq", None),
        P(("dp", "seq"), None),
        P(("dp", "seq"), None),
        P(("dp", "seq"), None),
        P(("dp", "seq"), None),
        P(("dp", "seq"), None),
        P(("dp", "seq"), None),
        P(("dp", "seq"), None),
        P(("dp", "seq"), None),
        P(("dp", "seq"), None),
        P(("dp", "seq"), None),
        P(("dp", "seq")),
        P(("dp", "seq")),
        P(("dp", "seq")),
        P(("dp", "seq")),
        P(("dp", "seq")),
        P(("dp", "seq")),
        P(("dp", "seq")),
        P(("dp", "seq")),
        P(("dp", "seq")),
        P(("dp", "seq")),
    )
    return jax.shard_map(
        fused_device if fused_fits(mesh) else per_device,
        mesh=mesh,
        in_specs=placed,
        out_specs=(
            P("dp", "seq", None),
            P("dp", "seq", None),
            P("dp", "seq", None),
            P(("dp", "seq"), None),
            P(("dp", "seq"), None),
            P(("dp", "seq"), None),
            P(("dp", "seq"), None),
            P(("dp", "seq"), None),
            P(("dp", "seq"), None),
            P(("dp", "seq"), None),
            P(("dp", "seq"), None),
            P(("dp", "seq"), None),
            P(("dp", "seq"), None),
            P(("dp", "seq")),
            P(("dp", "seq")),
            P(("dp", "seq")),
            P(("dp", "seq")),
            P(("dp", "seq")),
            P(("dp", "seq")),
            P(("dp", "seq")),
            P(("dp", "seq")),
            P(("dp", "seq")),
            P(("dp", "seq")),
        ),
        check_vma=False,
    )
```
